32 devices in a mesh: section: 2 (over y), dp: 8 (over z, core), tensor: 2 (over x).
Axes of the slice: x: 2, y: 2, z: 4, core: 2. Of those that a mesh axis runs over, the one named last changes fastest.
Arguments:
- inputs: bfloat16 [32, 1280, 768], P('dp', 'tensor'), may hold values from -6 to 6
- cotangent: bfloat16 [32, 1280, 768], P('dp', 'tensor'), may hold values from -6 to 6
- segment_ids: int32 [32, 1280], P('dp'), may hold values from 0 to 4, never falling along the last dimension, each value on 1 to 512 neighbouring positions
- norm_gains: float32 [2, 2, 768], P('section'), may hold values from 0.25 to 1.75
- norm_biases: float32 [2, 2, 768], P('section'), may hold values from -1.25 to 1.25
- qkv_weight: bfloat16 [2, 3, 768, 768], P('section', None, None, 'tensor'), may hold values from -0.21875 to 0.21875
- qv_bias: float32 [2, 2, 768], P('section'), may hold values from -1.25 to 1.25
- out_weight: bfloat16 [2, 768, 768], P('section', 'tensor'), may hold values from -1.25 to 1.25
- up_weight: bfloat16 [2, 768, 3072], P('section', None, 'tensor'), may hold values from -0.21875 to 0.21875
- up_bias: float32 [2, 3072], P('section'), may hold values from -1.25 to 1.25
- down_weight: bfloat16 [2, 3072, 768], P('section', 'tensor'), may hold values from -0.109375 to 0.109375
- out_biases: float32 [2, 2, 768], P('section'), may hold values from -1.25 to 1.25
Outputs:
- hidden_states: bfloat16 [2, 32, 1280, 768], P('section', 'dp', 'tensor')
- hidden_grads: float32 [2, 32, 1280, 768], P('section', 'dp', 'tensor')
- grad_norm_gains: float32 [2, 2, 768], P('section')
- grad_norm_biases: float32 [2, 2, 768], P('section')
- grad_qkv_weight: float32 [2, 3, 768, 768], P('section', None, None, 'tensor')
- grad_qv_bias: float32 [2, 2, 768], P('section')
- grad_out_weight: float32 [2, 768, 768], P('section', 'tensor')
- grad_up_weight: float32 [2, 768, 3072], P('section', None, 'tensor')
- grad_up_bias: float32 [2, 3072], P('section')
- grad_down_weight: float32 [2, 3072, 768], P('section', 'tensor')
- grad_out_biases: float32 [2, 2, 768], P('section')
The draws below stay inside these ranges and needn't reach their ends.
Inputs may be any that keep to these rules, and one draw needn't show every extreme that they name: `segment_ids`: in each sequence the image numbers never fall, each image holds 1 to 512 tokens, and one image holds exactly 512.
All inputs are finite; a program needn't handle non-finite values.
Results may differ from the reference program's by a relative error of at most 0.03.
Values may be sent and summed in bfloat16 or wider, within the bound.
A program may use at most 448 MiB of HBM per device.

```python
import functools
import math
import jax
import jax.numpy as jnp
import numpy as np
from jax import lax

HEADS = 16
HEAD_DIM = 48
D = 768
FF = 3072
SEQ_LEN = 1280
IMAGES = 5
IMAGE_MOST = 512
LAYERS = 2
SEQS = 32


def shard_levels(own_key, shape, shards, low, high):
    gain = 1.0
    for axis_at, parts in shards:
        draws = jax.random.uniform(jax.random.fold_in(jax.random.fold_in(own_key, 6), axis_at), (parts,), jnp.float32, low / len(shards), high / len(shards))
        gain = gain * jnp.repeat(jnp.exp(draws), shape[axis_at] // parts).reshape((-1,) + (1,) * (len(shape) - 1 - axis_at))
    return gain


def length_profile(amount, total, bound, slope):
    portions = [(1 << 20) // math.isqrt(standing ** slope) + 1 for standing in range(2, amount + 1)]
    rest, counts = total - bound - (amount - 1), [1] * (amount - 1)
    while rest > 0:
        free = [i for i in range(amount - 1) if counts[i] < bound]
        pool, remaining = sum([portions[i] for i in free]), rest
        for i in free:
            more = min(bound - counts[i], max(1, remaining * portions[i] // pool), rest)
            counts[i] = counts[i] + more
            rest = rest - more
    return np.array([bound] + counts)


def ragged_sizes(rng, amount, total, most, lean):
    if amount == 2:
        one = jax.random.randint(rng, (), max(1, total - most), min(most, total - 1) + 1)
        return jnp.stack([one, total - one])
    sizes = jnp.asarray(length_profile(amount, total, most, lean), jnp.int32)
    pairs = (amount - 1) // 2
    source_of, receiver = sizes[1:1 + 2 * pairs:2], sizes[2:2 + 2 * pairs:2]
    slack = jnp.minimum(source_of - 1, most - receiver)
    shifted = jax.random.randint(jax.random.fold_in(rng, 1), (pairs,), 0, 1 << 20) % (slack + 1)
    sizes = sizes.at[1:1 + 2 * pairs:2].set(source_of - shifted).at[2:2 + 2 * pairs:2].set(receiver + shifted)
    return sizes[jax.random.permutation(jax.random.fold_in(rng, 2), amount)]


def scatter_about(key, extent, width, bound, split=(), held_as=jnp.bfloat16):
    drawn = jax.random.normal(key, extent, jnp.float32) * width
    if len(split) > 0:
        drawn = shard_levels(key, extent, split, -0.22, 0.18) * drawn
    return jnp.clip(drawn, min=-bound, max=bound).astype(held_as)


def setup_inputs(seed: int = 0) -> dict:
    seeds = jax.random.split(jax.random.key(seed), 13)
    return {
        "inputs": scatter_about(seeds[0], (SEQS, SEQ_LEN, D), 1.0, 6.0, ((0, 8), (1, 2))),
        "cotangent": scatter_about(seeds[1], (SEQS, SEQ_LEN, D), 1.0, 6.0, ((0, 8), (1, 2))),
        "segment_ids": jax.vmap(lambda own: jnp.searchsorted(jnp.cumsum(ragged_sizes(own, IMAGES, SEQ_LEN, IMAGE_MOST, 0)), jnp.arange(SEQ_LEN), side="right"))(jax.random.split(seeds[2], SEQS)).reshape((SEQS, SEQ_LEN)).astype(jnp.int32),
        "norm_gains": jnp.clip(1.0 + 0.15 * jax.random.normal(seeds[3], (LAYERS, 2, D), jnp.float32), 0.25, 1.75),
        "norm_biases": scatter_about(seeds[4], (LAYERS, 2, D), 0.2, 1.25, ((0, 2),), jnp.float32),
        "qkv_weight": scatter_about(seeds[5], (LAYERS, 3, D, D), D ** -0.5, 0.21875, ((0, 2), (3, 2))),
        "qv_bias": scatter_about(seeds[6], (LAYERS, 2, D), 0.2, 1.25, ((0, 2),), jnp.float32),
        "out_weight": scatter_about(seeds[7], (LAYERS, D, D), (max(D // 32, 1)) ** -0.5, 1.25, ((0, 2), (1, 2))),
        "up_weight": scatter_about(seeds[8], (LAYERS, D, FF), D ** -0.5, 0.21875, ((0, 2), (2, 2))),
        "up_bias": scatter_about(seeds[9], (LAYERS, FF), 0.2, 1.25, ((0, 2),), jnp.float32),
        "down_weight": scatter_about(seeds[10], (LAYERS, FF, D), FF ** -0.5, 0.109375, ((0, 2), (1, 2))),
        "out_biases": scatter_about(seeds[11], (LAYERS, 2, D), 0.2, 1.25, ((0, 2),), jnp.float32),
    }


@jax.custom_vjp
def low(v):
    return lax.optimization_barrier(v.astype(jnp.bfloat16)).astype(jnp.float32)

@jax.custom_vjp
def low_back(v):
    return v

def low_keep(v):
    return (low(v), None)

def low_pass(kept, grad):
    return (grad,)

def back_keep(v):
    return (v, None)

def back_low(kept, grad):
    return (low(grad),)
low.defvjp(low_keep, low_pass)
low_back.defvjp(back_keep, back_low)
EPSILON = 1e-05
NEGATIVE = -1e+30
HIGHEST = lax.Precision.HIGHEST

def normed(token_rows, gain_row, shift_row):
    centre = token_rows - lax.optimization_barrier(jnp.mean(token_rows, axis=-1, keepdims=True))
    spread = lax.optimization_barrier(jnp.mean(centre * centre, axis=-1, keepdims=True))
    return centre * lax.rsqrt(spread + EPSILON) * gain_row + shift_row

def project(token_rows, weight):
    return jnp.einsum('...d,de->...e', token_rows, weight, precision=HIGHEST)

def attend_sequence(queries, key_rows, value_rows, segment):
    half_rows = SEQ_LEN // 2
    scaling = HEAD_DIM ** (-0.5)

    def one_block(block_index):
        row_start = block_index * half_rows
        block_queries = lax.dynamic_slice_in_dim(queries, row_start, half_rows, 0)
        block_segment = lax.dynamic_slice_in_dim(segment, row_start, half_rows, 0)
        scores = low_back(jnp.einsum('qhd,khd->hqk', block_queries, key_rows, precision=HIGHEST) * scaling)
        allowed = block_segment[:, None] == segment[None, :]
        scores = jnp.where(allowed[None], scores, NEGATIVE)
        weights = jax.nn.softmax(scores, axis=-1)
        return jnp.einsum('hqk,khd->qhd', low(weights), value_rows, precision=HIGHEST)
    blocks = lax.map(jax.checkpoint(one_block), jnp.arange(2, dtype=jnp.int32))
    return blocks.reshape(SEQ_LEN, HEADS, HEAD_DIM)

def to_heads(tensor):
    return tensor.reshape(tensor.shape[0], SEQ_LEN, HEADS, HEAD_DIM)

def residual_block(token_rows, segment, params):
    gain_rows, shift_rows, qkv_matrix, qv_shift, out_matrix, up_matrix, up_shift, down_matrix, out_shift = params
    normed_one = low(normed(token_rows, gain_rows[0], shift_rows[0]))
    queries = low(low_back(project(normed_one, qkv_matrix[0])) + qv_shift[0])
    key_rows = low(low_back(project(normed_one, qkv_matrix[1])))
    value_rows = low(low_back(project(normed_one, qkv_matrix[2])) + qv_shift[1])
    mixed_rows = jax.vmap(attend_sequence)(to_heads(queries), to_heads(key_rows), to_heads(value_rows), segment)
    mixed_rows = low_back(low(mixed_rows.reshape(token_rows.shape)))
    middle = token_rows + low_back(project(mixed_rows, out_matrix)) + out_shift[0]
    normed_two = low(normed(middle, gain_rows[1], shift_rows[1]))
    hidden = low_back(project(normed_two, up_matrix)) + up_shift
    active = low(jax.nn.gelu(hidden, approximate=False))
    return middle + low_back(project(active, down_matrix)) + out_shift[1]

def two_layers(first_in, probe, stacked, segment):
    layer_one = tuple((weight[0] for weight in stacked))
    layer_two = tuple((weight[1] for weight in stacked))
    handed = low(residual_block(first_in, segment, layer_one))
    second_in = low_back(handed) + probe
    return (residual_block(second_in, segment, layer_two), handed)

def reference(inputs, cotangent, segment_ids, norm_gains, norm_biases, qkv_weight, qv_bias, out_weight, up_weight, up_bias, down_weight, out_biases):
    stacked = tuple((weight.astype(jnp.float32) for weight in (norm_gains, norm_biases, qkv_weight, qv_bias, out_weight, up_weight, up_bias, down_weight, out_biases)))
    group_size = 2
    groups = SEQS // group_size

    def regroup(array):
        return array.reshape((groups, group_size) + array.shape[1:])

    def one_group(totals, pieces):
        group_in, group_cot, group_segment = pieces
        first_in = group_in.astype(jnp.float32)
        probe = jnp.zeros_like(first_in)
        block_out, pullback, handed = jax.vjp(functools.partial(two_layers, segment=group_segment), first_in, probe, stacked, has_aux=True)
        in_grad, probe_grad, weight_grads = pullback(group_cot.astype(jnp.float32))
        totals = tuple((total + piece for total, piece in zip(totals, weight_grads)))
        return (totals, (handed.astype(jnp.bfloat16), block_out.astype(jnp.bfloat16), in_grad, probe_grad))
    zero_grads = tuple((jnp.zeros_like(weight) for weight in stacked))
    totals, (handed, final_rows, in_grad, probe_grad) = lax.scan(one_group, zero_grads, (regroup(inputs), regroup(cotangent), regroup(segment_ids)))
    full_shape = (SEQS, SEQ_LEN, D)
    hidden_states = jnp.stack([handed.reshape(full_shape), final_rows.reshape(full_shape)])
    hidden_grads = jnp.stack([in_grad.reshape(full_shape), probe_grad.reshape(full_shape)])
    return (hidden_states, hidden_grads, totals[0], totals[1], totals[2], totals[3], totals[4], totals[5], totals[6], totals[7], totals[8])
```

```python
import functools
import math

import jax
import jax.numpy as jnp
from jax import lax
from jax.experimental import pallas as pl
from jax.experimental.pallas import tpu as pltpu
from jax.sharding import PartitionSpec as P

HEAD_DIM = 48
IMAGE_IDS = 5
IMAGE_MOST = 512
EPSILON = 1e-05
NEGATIVE = -1e30
TILE = 128
EXTRA = 16
LOG2E = math.log2(math.e)
SCALING = HEAD_DIM ** (-0.5)
AXES = ("section", "dp", "tensor")
VMEM_LIMIT = 56 * 1024 * 1024
HALF_ERF = (0.127414796, -0.142248368, 0.7107068705, -0.7265760135, 0.5307027145)
ERF_RATE = 0.3275911 * math.sqrt(0.5)
F32 = jnp.float32
BF16 = jnp.bfloat16


def nn(left, right):
    return lax.dot_general(left, right, (((1,), (0,)), ((), ())), preferred_element_type=F32)


def nt(left, right):
    return lax.dot_general(left, right, (((1,), (1,)), ((), ())), preferred_element_type=F32)


def tn(left, right):
    return lax.dot_general(left, right, (((0,), (0,)), ((), ())), preferred_element_type=F32)


def normalise(rows):
    centre = rows - jnp.mean(rows, axis=-1, keepdims=True)
    inverse = lax.rsqrt(jnp.mean(centre * centre, axis=-1, keepdims=True) + EPSILON)
    return centre * inverse, inverse


def normalise_back(gradient, scaled, inverse, gain):
    upstream = gradient * gain
    return inverse * (
        upstream
        - jnp.mean(upstream, axis=-1, keepdims=True)
        - scaled * jnp.mean(upstream * scaled, axis=-1, keepdims=True)
    )


def gelu_pair(values):
    bell = jnp.exp2(values * values * (-0.5 * LOG2E))
    step = 1.0 / (1.0 + ERF_RATE * jnp.abs(values))
    poly = HALF_ERF[4]
    for term in HALF_ERF[3::-1]:
        poly = poly * step + term
    tail = poly * step * bell
    share = jnp.where(values >= 0, 1.0 - tail, tail)
    return values * share, share + values * bell * (1.0 / math.sqrt(2 * math.pi))


def extra_rows(rows, width):
    at = lax.broadcasted_iota(jnp.int32, (EXTRA, width), 0)
    out = jnp.zeros((EXTRA, width), F32)
    for index, row in enumerate(rows):
        out = jnp.where(at == index, row, out)
    return out.astype(BF16)


def three_parts(row):
    first = row.astype(BF16).astype(F32)
    second = (row - first).astype(BF16).astype(F32)
    return [first, second, row - first - second]


def each_image(start_ref, tiles_ref, body):
    most = IMAGE_MOST // TILE + 1

    def image(index, carry):
        first = start_ref[index]
        tiles = tiles_ref[index]
        for count in range(1, most + 1):

            @pl.when(tiles == count)
            def _():
                body(index, pl.multiple_of(first * TILE, TILE), count * TILE)

        return carry

    lax.fori_loop(0, IMAGE_IDS, image, 0)


def piece_copies(refs, sems, targets):
    low_ref, high_ref = refs
    half = low_ref.shape[0]
    copies = []
    for slot, (first, count, target) in enumerate(targets):
        source = low_ref.at[first : first + count] if first < half else high_ref.at[first - half : first - half + count]
        copies.append(pltpu.make_async_copy(source, target, sems.at[slot]))
    return copies


def start_pieces(sel, own, other, copies_of):
    for index in range(len(own)):

        @pl.when(sel == 0)
        def _():
            for copy in copies_of(index, own[index]):
                copy.start()

        @pl.when(sel != 0)
        def _():
            for copy in copies_of(index, other[index]):
                copy.start()


def attend_forward_image(index, at, width, heads, seg_ref, qkv_ref, store):
    win = pl.ds(at, width)
    mine = seg_ref[:, win] == index
    mask = jnp.where(mine, 0.0, NEGATIVE)
    one = jnp.ones((1, width), F32)
    query_extra = extra_rows([mask, one], width)
    key_extra = extra_rows([one, mask], width)
    value_extra = extra_rows([one], width)
    cols = heads * HEAD_DIM

    def head(which, carry):
        low = pl.multiple_of(which * HEAD_DIM, EXTRA)
        queries = jnp.concatenate([qkv_ref[0, pl.ds(low, HEAD_DIM), win], query_extra], axis=0)
        keys = jnp.concatenate([qkv_ref[0, pl.ds(cols + low, HEAD_DIM), win], key_extra], axis=0)
        values = jnp.concatenate([qkv_ref[0, pl.ds(2 * cols + low, HEAD_DIM), win], value_extra], axis=0)
        scores = tn(keys, queries)
        peak = jnp.max(scores, axis=0, keepdims=True)
        weights = jnp.exp2(scores - peak).astype(BF16)
        mixed = nn(values, weights)
        total = mixed[HEAD_DIM : HEAD_DIM + 1]
        store(which, low, win, mine, mixed[:HEAD_DIM] * (1.0 / total), peak + jnp.log2(total))
        return carry

    lax.fori_loop(0, heads, head, 0, unroll=True)


def mixer_forward_kernel(
    sel_ref, start_ref, tiles_ref, seg_ref, hidden_ref, norm_ref, qkv_shift_ref, out_shift_ref, *rest, pieces, heads
):
    own = [rest[2 * i : 2 * i + 2] for i in range(pieces)]
    other = [rest[2 * pieces + 2 * i : 2 * pieces + 2 * i + 2] for i in range(pieces)]
    qkv_ref, mixed_ref, total_ref, middle_ref, weight, out_weight, normed, mixed_all, sems = rest[4 * pieces :]
    step = pl.program_id(0)
    sel = sel_ref[0]
    cols = heads * HEAD_DIM
    rows_all = hidden_ref.shape[0]
    block = 256
    half = own[0][0].shape[0]

    def copies_of(index, refs):
        return piece_copies(
            refs,
            sems.at[index],
            [
                (0, half, weight.at[index, 0:half]),
                (half, 3 * cols - half, weight.at[index, half : 3 * cols]),
                (3 * cols, cols, out_weight.at[index * cols : (index + 1) * cols]),
            ],
        )

    @pl.when(step == 0)
    def _():
        start_pieces(sel, own, other, copies_of)

        def norm_block(i, carry):
            rows = pl.ds(pl.multiple_of(i * block, block), block)
            scaled, _ = normalise(hidden_ref[rows, :].astype(F32))
            normed[rows, :] = (scaled * norm_ref[0:1, :] + norm_ref[1:2, :]).astype(BF16)
            return carry

        lax.fori_loop(0, rows_all // block, norm_block, 0)

    for index in range(pieces):

        @pl.when(step == index)
        def _():
            for copy in copies_of(index, own[index]):
                copy.wait()

    def project(i, carry):
        win = pl.ds(pl.multiple_of(i * block, block), block)
        projected = nt(weight[step], normed[win, :]) + qkv_shift_ref[0]
        qkv_ref[0, 0:cols, win] = (projected[0:cols] * (SCALING * LOG2E)).astype(BF16)
        qkv_ref[0, cols : 3 * cols, win] = projected[cols : 3 * cols].astype(BF16)
        return carry

    lax.fori_loop(0, rows_all // block, project, 0)

    def store(which, low, win, mine, mixed, total):
        rows = pl.ds(low, HEAD_DIM)
        old = mixed_ref[0, rows, win].astype(F32)
        mixed_ref[0, rows, win] = jnp.where(mine, mixed, old).astype(BF16)
        total_ref[which, :, win] = jnp.where(mine, total, total_ref[which, :, win])

    each_image(
        start_ref,
        tiles_ref,
        lambda index, at, width: attend_forward_image(index, at, width, heads, seg_ref, qkv_ref, store),
    )
    mixed_all[pl.ds(pl.multiple_of(step * cols, cols), cols), :] = mixed_ref[0]

    @pl.when(step == pieces - 1)
    def _():
        def finish(i, carry):
            rows = pl.ds(pl.multiple_of(i * block, block), block)
            branch = tn(mixed_all[:, rows], out_weight[...])
            middle_ref[rows, :] = hidden_ref[rows, :].astype(F32) + branch + out_shift_ref[...]
            return carry

        lax.fori_loop(0, rows_all // block, finish, 0)


def once(shape):
    zeros = (0,) * len(shape)
    return pl.BlockSpec(shape, lambda *_: zeros, pipeline_mode=pl.Buffered(1))


def anywhere(count):
    return [pl.BlockSpec(memory_space=pl.ANY)] * count


def flat(pieces):
    return [half for piece in pieces for half in piece]


def mixer_forward(sel, images, hidden, norm, qkv_shift, out_shift, own, other):
    rows, width = hidden.shape
    pieces = len(own)
    heads = width // HEAD_DIM // pieces
    cols = heads * HEAD_DIM
    start, tiles, segment = images
    return pl.pallas_call(
        functools.partial(mixer_forward_kernel, pieces=pieces, heads=heads),
        grid_spec=pltpu.PrefetchScalarGridSpec(
            num_scalar_prefetch=3,
            grid=(pieces,),
            in_specs=[
                once((1, rows)),
                once((rows, width)),
                once((2, width)),
                pl.BlockSpec((1, 3 * cols, 1), lambda i, *_: (i, 0, 0)),
                once((1, width)),
            ]
            + anywhere(4 * pieces),
            out_specs=[
                pl.BlockSpec((1, 3 * cols, rows), lambda i, *_: (i, 0, 0)),
                pl.BlockSpec((1, cols, rows), lambda i, *_: (i, 0, 0)),
                pl.BlockSpec((heads, 1, rows), lambda i, *_: (i, 0, 0)),
                once((rows, width)),
            ],
            scratch_shapes=[
                pltpu.VMEM((pieces, 3 * cols, width), BF16),
                pltpu.VMEM((width, width), BF16),
                pltpu.VMEM((rows, width), BF16),
                pltpu.VMEM((width, rows), BF16),
                pltpu.SemaphoreType.DMA((pieces, 3)),
            ],
        ),
        out_shape=[
            jax.ShapeDtypeStruct((pieces, 3 * cols, rows), BF16),
            jax.ShapeDtypeStruct((pieces, cols, rows), BF16),
            jax.ShapeDtypeStruct((pieces * heads, 1, rows), F32),
            jax.ShapeDtypeStruct((rows, width), F32),
        ],
        compiler_params=pltpu.CompilerParams(vmem_limit_bytes=VMEM_LIMIT),
        cost_estimate=pl.CostEstimate(flops=16_000_000_000, bytes_accessed=20_000_000, transcendentals=0),
        name="mixer_forward",
    )(sel, start, tiles, segment, hidden, norm, qkv_shift, out_shift, *flat(own), *flat(other))


def feed_forward_kernel(sel_ref, middle_ref, norm_ref, up_shift_ref, out_shift_ref, *rest, pieces):
    up_own, down_own, up_other, down_other = [
        [rest[2 * (pieces * k + i) : 2 * (pieces * k + i) + 2] for i in range(pieces)] for k in range(4)
    ]
    out_ref, active_ref, slope_ref, up_weight, down_weight, sems = rest[8 * pieces :]
    step = pl.program_id(0)
    sel = sel_ref[0]
    size = up_weight.shape[2]
    half = up_own[0][0].shape[0]

    def copies_of(index, refs, kind):
        target = (up_weight, down_weight)[kind]
        return piece_copies(
            refs,
            sems.at[kind, index],
            [(0, half, target.at[index, 0:half]), (half, half, target.at[index, half : 2 * half])],
        )

    @pl.when(step == 0)
    def _():
        start_pieces(sel, up_own, up_other, functools.partial(copies_of, kind=0))
        start_pieces(sel, down_own, down_other, functools.partial(copies_of, kind=1))

    scaled, _ = normalise(middle_ref[...])
    normed = (scaled * norm_ref[0:1, :] + norm_ref[1:2, :]).astype(BF16)
    total = middle_ref[...] + out_shift_ref[...]
    for index in range(pieces):

        @pl.when(step == 0)
        def _():
            for copy in copies_of(index, up_own[index], 0) + copies_of(index, down_own[index], 1):
                copy.wait()

        part = pl.ds(index * size, size)
        raised = nn(normed, up_weight[index]) + up_shift_ref[:, part]
        active, slope = gelu_pair(raised)
        active = active.astype(BF16)
        active_ref[:, part] = active
        slope_ref[:, part] = slope.astype(BF16)
        total = total + nn(active, down_weight[index])
    out_ref[...] = total.astype(BF16)


def feed_forward(sel, middle, norm, up_shift, out_shift, up_own, down_own, up_other, down_other):
    rows, width = middle.shape
    pieces = len(up_own)
    hidden = up_shift.shape[1]
    size = hidden // pieces
    block = 256
    return pl.pallas_call(
        functools.partial(feed_forward_kernel, pieces=pieces),
        grid_spec=pltpu.PrefetchScalarGridSpec(
            num_scalar_prefetch=1,
            grid=(rows // block,),
            in_specs=[
                pl.BlockSpec((block, width), lambda i, *_: (i, 0)),
                once((2, width)),
                once((1, hidden)),
                once((1, width)),
            ]
            + anywhere(8 * pieces),
            out_specs=[
                pl.BlockSpec((block, width), lambda i, *_: (i, 0)),
                pl.BlockSpec((block, hidden), lambda i, *_: (i, 0)),
                pl.BlockSpec((block, hidden), lambda i, *_: (i, 0)),
            ],
            scratch_shapes=[
                pltpu.VMEM((pieces, width, size), BF16),
                pltpu.VMEM((pieces, size, width), BF16),
                pltpu.SemaphoreType.DMA((2, pieces, 2)),
            ],
        ),
        out_shape=[
            jax.ShapeDtypeStruct((rows, width), BF16),
            jax.ShapeDtypeStruct((rows, hidden), BF16),
            jax.ShapeDtypeStruct((rows, hidden), BF16),
        ],
        compiler_params=pltpu.CompilerParams(vmem_limit_bytes=VMEM_LIMIT),
        cost_estimate=pl.CostEstimate(flops=16_000_000_000, bytes_accessed=20_000_000, transcendentals=0),
        name="feed_forward",
    )(sel, middle, norm, up_shift, out_shift, *flat(up_own), *flat(down_own), *flat(up_other), *flat(down_other))


def feed_backward_kernel(sel_ref, grad_ref, middle_ref, norm_ref, active_ref, slope_ref, *rest, pieces, parts):
    up_own, down_own, up_other, down_other = [
        [rest[2 * (pieces * k + i) : 2 * (pieces * k + i) + 2] for i in range(pieces)] for k in range(4)
    ]
    (
        weight_grad_ref,
        up_shift_grad_ref,
        middle_grad_ref,
        small_ref,
        up_weight,
        down_weight,
        normed_t,
        grad_t,
        low_grad,
        normed_grad,
        sems,
    ) = rest[8 * pieces :]
    step = pl.program_id(0)
    sel = sel_ref[0]
    rows_all, width = grad_ref.shape
    chunk = active_ref.shape[1]
    block = 256
    blocks = rows_all // block
    half = up_own[0][0].shape[0]

    def copies_of(index, refs, kind):
        target = (up_weight, down_weight)[kind]
        return piece_copies(
            refs,
            sems.at[kind, index],
            [(0, half, target.at[index, 0:half]), (half, half, target.at[index, half : 2 * half])],
        )

    @pl.when(step == 0)
    def _():
        start_pieces(sel, down_own, down_other, functools.partial(copies_of, kind=1))
        start_pieces(sel, up_own, up_other, functools.partial(copies_of, kind=0))

        def prepare(i, carry):
            rows = pl.ds(pl.multiple_of(i * block, block), block)
            scaled, _ = normalise(middle_ref[rows, :])
            normed = (scaled * norm_ref[0:1, :] + norm_ref[1:2, :]).astype(BF16)
            normed_t[:, rows] = normed.T
            grad_t[:, rows] = grad_ref[rows, :].T
            return carry

        lax.fori_loop(0, blocks, prepare, 0)

    for index in range(pieces):

        @pl.when(step == index * parts)
        def _():
            for copy in copies_of(index, up_own[index], 0) + copies_of(index, down_own[index], 1):
                copy.wait()

    piece = step // parts
    for part in range(parts):

        @pl.when(step % parts == part)
        def _():
            cols = pl.ds(part * chunk, chunk)

            def back(i, shift_grad):
                rows = pl.ds(pl.multiple_of(i * block, block), block)
                active_grad = nt(grad_ref[rows, :], down_weight[piece, cols, :])
                hidden_grad = active_grad * slope_ref[rows, :].astype(F32)
                low = hidden_grad.astype(BF16)
                low_grad[rows, :] = low
                term = nt(low, up_weight[piece, :, cols])

                @pl.when(step == 0)
                def _():
                    normed_grad[rows, :] = term

                @pl.when(step != 0)
                def _():
                    normed_grad[rows, :] += term

                return shift_grad + jnp.sum(hidden_grad, axis=0, keepdims=True)

            up_shift_grad_ref[0] = lax.fori_loop(0, blocks, back, jnp.zeros((1, chunk), F32))

    def weigh(i, carry):
        rows = pl.ds(pl.multiple_of(i * block, block), block)
        weight_grad_ref[0, rows, :] = nn(normed_t[rows, :], low_grad[...]).astype(BF16)
        lower = pl.ds(pl.multiple_of(width + i * block, block), block)
        weight_grad_ref[0, lower, :] = nn(grad_t[rows, :], active_ref[...]).astype(BF16)
        return carry

    lax.fori_loop(0, width // block, weigh, 0)

    @pl.when(step == pieces * parts - 1)
    def _():
        def finish(i, sums):
            rows = pl.ds(pl.multiple_of(i * block, block), block)
            scaled, inverse = normalise(middle_ref[rows, :])
            gradient = normed_grad[rows, :]
            upper = grad_ref[rows, :].astype(F32)
            middle_grad = upper + normalise_back(gradient, scaled, inverse, norm_ref[0:1, :])
            middle_grad_ref[rows, :] = middle_grad
            terms = (gradient * scaled, gradient, middle_grad, upper)
            return tuple(old + jnp.sum(term, axis=0, keepdims=True) for old, term in zip(sums, terms))

        zero = jnp.zeros((1, width), F32)
        sums = lax.fori_loop(0, blocks, finish, (zero, zero, zero, zero))
        for index, row in enumerate(sums):
            small_ref[index : index + 1, :] = row


def feed_backward(sel, grad, middle, norm, active, slope, up_own, down_own, up_other, down_other):
    rows, width = middle.shape
    pieces = len(up_own)
    hidden = active.shape[1]
    size = hidden // pieces
    parts = 2
    chunk = size // parts
    return pl.pallas_call(
        functools.partial(feed_backward_kernel, pieces=pieces, parts=parts),
        grid_spec=pltpu.PrefetchScalarGridSpec(
            num_scalar_prefetch=1,
            grid=(pieces * parts,),
            in_specs=[
                once((rows, width)),
                once((rows, width)),
                once((2, width)),
                pl.BlockSpec((rows, chunk), lambda i, *_: (0, i)),
                pl.BlockSpec((rows, chunk), lambda i, *_: (0, i)),
            ]
            + anywhere(8 * pieces),
            out_specs=[
                pl.BlockSpec((1, 2 * width, chunk), lambda i, *_: (i // parts, 0, i % parts)),
                pl.BlockSpec((1, 1, chunk), lambda i, *_: (i, 0, 0)),
                once((rows, width)),
                once((4, width)),
            ],
            scratch_shapes=[
                pltpu.VMEM((pieces, width, size), BF16),
                pltpu.VMEM((pieces, size, width), BF16),
                pltpu.VMEM((width, rows), BF16),
                pltpu.VMEM((width, rows), BF16),
                pltpu.VMEM((rows, chunk), BF16),
                pltpu.VMEM((rows, width), F32),
                pltpu.SemaphoreType.DMA((2, pieces, 2)),
            ],
        ),
        out_shape=[
            jax.ShapeDtypeStruct((pieces, 2 * width, size), BF16),
            jax.ShapeDtypeStruct((pieces * parts, 1, chunk), F32),
            jax.ShapeDtypeStruct((rows, width), F32),
            jax.ShapeDtypeStruct((4, width), F32),
        ],
        compiler_params=pltpu.CompilerParams(vmem_limit_bytes=VMEM_LIMIT),
        cost_estimate=pl.CostEstimate(flops=30_000_000_000, bytes_accessed=50_000_000, transcendentals=0),
        name="feed_backward",
    )(sel, grad, middle, norm, active, slope, *flat(up_own), *flat(down_own), *flat(up_other), *flat(down_other))


def attend_backward_image(index, at, width, heads, seg_ref, qkv_ref, mixed_ref, total_ref, mixed_grad, sums):
    win = pl.ds(at, width)
    mine = seg_ref[:, win] == index
    mask = jnp.where(mine, 0.0, NEGATIVE)
    one = jnp.ones((1, width), F32)
    key_extra = extra_rows([one, mask, one, one, one], width)
    value_extra = extra_rows([one, one, one], width)
    cols = heads * HEAD_DIM

    def head(which, carry):
        low = pl.multiple_of(which * HEAD_DIM, EXTRA)
        query_rows = pl.ds(low, HEAD_DIM)
        key_rows = pl.ds(cols + low, HEAD_DIM)
        value_rows = pl.ds(2 * cols + low, HEAD_DIM)
        queries = qkv_ref[0, query_rows, win]
        keys = qkv_ref[0, key_rows, win]
        values = qkv_ref[0, value_rows, win]
        grads = mixed_grad[query_rows, win]
        inner = jnp.sum(
            grads.astype(F32) * mixed_ref[0, query_rows, win].astype(F32), axis=0, keepdims=True
        )
        query_extra = extra_rows([mask, one] + three_parts(-total_ref[which, :, win]), width)
        grad_extra = extra_rows(three_parts(-inner), width)
        scores = tn(jnp.concatenate([keys, key_extra], axis=0), jnp.concatenate([queries, query_extra], axis=0))
        weights = jnp.exp2(scores)
        terms = tn(jnp.concatenate([values, value_extra], axis=0), jnp.concatenate([grads, grad_extra], axis=0))
        score_grads = (weights * terms).astype(BF16)
        sums[query_rows, win] += nn(keys, score_grads) * SCALING
        sums[key_rows, win] += nt(queries, score_grads) * (1.0 / LOG2E)
        sums[value_rows, win] += nt(grads, weights.astype(BF16))
        return carry

    lax.fori_loop(0, heads, head, 0, unroll=2)


def mixer_backward_kernel(
    sel_ref, start_ref, tiles_ref, seg_ref, hidden_ref, middle_grad_ref, norm_ref, qkv_ref, mixed_ref, total_ref, *rest,
    pieces, heads,
):
    own = [rest[2 * i : 2 * i + 2] for i in range(pieces)]
    other = [rest[2 * pieces + 2 * i : 2 * pieces + 2 * i + 2] for i in range(pieces)]
    (
        weight_grad_ref,
        qkv_shift_grad_ref,
        in_grad_ref,
        small_ref,
        weight,
        out_weight,
        normed,
        low_middle,
        mixed_grad,
        sums,
        projected_grad,
        sems,
    ) = rest[4 * pieces :]
    step = pl.program_id(0)
    sel = sel_ref[0]
    cols = heads * HEAD_DIM
    rows_all, width = hidden_ref.shape
    block = 256
    blocks = rows_all // block
    half = own[0][0].shape[0]

    def copies_of(index, refs):
        first = index * 3 * cols
        return piece_copies(
            refs,
            sems.at[index],
            [
                (3 * cols, cols, out_weight.at[index * cols : (index + 1) * cols]),
                (0, half, weight.at[first : first + half]),
                (half, 3 * cols - half, weight.at[first + half : first + 3 * cols]),
            ],
        )

    @pl.when(step == 0)
    def _():
        start_pieces(sel, own, other, copies_of)

        def prepare(i, carry):
            rows = pl.ds(pl.multiple_of(i * block, block), block)
            scaled, _ = normalise(hidden_ref[rows, :].astype(F32))
            normed[rows, :] = (scaled * norm_ref[0:1, :] + norm_ref[1:2, :]).astype(BF16)
            low_middle[rows, :] = middle_grad_ref[rows, :].astype(BF16)
            return carry

        lax.fori_loop(0, blocks, prepare, 0)

    for index in range(pieces):

        @pl.when(step == index)
        def _():
            for copy in copies_of(index, own[index]):
                copy.wait()

    def spread(i, carry):
        win = pl.ds(pl.multiple_of(i * block, block), block)
        mine = out_weight[pl.ds(pl.multiple_of(step * cols, cols), cols), :]
        mixed_grad[:, win] = nt(mine, low_middle[win, :]).astype(BF16)
        return carry

    lax.fori_loop(0, blocks, spread, 0)
    weight_grad_ref[0, 3 * cols : 4 * cols, :] = nn(mixed_ref[0], low_middle[...]).astype(BF16)
    sums[...] = jnp.zeros_like(sums)
    each_image(
        start_ref,
        tiles_ref,
        lambda index, at, width: attend_backward_image(
            index, at, width, heads, seg_ref, qkv_ref, mixed_ref, total_ref, mixed_grad, sums
        ),
    )
    for third in range(3):
        rows = pl.ds(third * cols, cols)
        gradient = sums[rows, :]
        low = gradient.astype(BF16)
        projected_grad[pl.ds(pl.multiple_of(step * (3 * cols) + third * cols, cols), cols), :] = low
        qkv_shift_grad_ref[0, rows, :] = jnp.sum(gradient, axis=1, keepdims=True)
        weight_grad_ref[0, rows, :] = nn(low, normed[...]).astype(BF16)

    @pl.when(step == pieces - 1)
    def _():
        def finish(i, carry):
            rows = pl.ds(pl.multiple_of(i * block, block), block)
            scaled, inverse = normalise(hidden_ref[rows, :].astype(F32))
            gradient = tn(projected_grad[:, rows], weight[...])
            in_grad = middle_grad_ref[rows, :] + normalise_back(gradient, scaled, inverse, norm_ref[0:1, :])
            in_grad_ref[rows, :] = in_grad.astype(BF16)
            terms = (gradient * scaled, gradient)
            return tuple(old + jnp.sum(term, axis=0, keepdims=True) for old, term in zip(carry, terms))

        zero = jnp.zeros((1, width), F32)
        totals = lax.fori_loop(0, blocks, finish, (zero, zero))
        for index, row in enumerate(totals):
            small_ref[index : index + 1, :] = row


def mixer_backward(sel, images, hidden, middle_grad, norm, qkv, mixed, totals, own, other):
    rows, width = hidden.shape
    pieces = len(own)
    heads = width // HEAD_DIM // pieces
    cols = heads * HEAD_DIM
    start, tiles, segment = images
    return pl.pallas_call(
        functools.partial(mixer_backward_kernel, pieces=pieces, heads=heads),
        grid_spec=pltpu.PrefetchScalarGridSpec(
            num_scalar_prefetch=3,
            grid=(pieces,),
            in_specs=[
                once((1, rows)),
                once((rows, width)),
                once((rows, width)),
                once((2, width)),
                pl.BlockSpec((1, 3 * cols, rows), lambda i, *_: (i, 0, 0)),
                pl.BlockSpec((1, cols, rows), lambda i, *_: (i, 0, 0)),
                pl.BlockSpec((heads, 1, rows), lambda i, *_: (i, 0, 0)),
            ]
            + anywhere(4 * pieces),
            out_specs=[
                pl.BlockSpec((1, 4 * cols, width), lambda i, *_: (i, 0, 0)),
                pl.BlockSpec((1, 3 * cols, 1), lambda i, *_: (i, 0, 0)),
                once((rows, width)),
                once((2, width)),
            ],
            scratch_shapes=[
                pltpu.VMEM((3 * width, width), BF16),
                pltpu.VMEM((width, width), BF16),
                pltpu.VMEM((rows, width), BF16),
                pltpu.VMEM((rows, width), BF16),
                pltpu.VMEM((cols, rows), BF16),
                pltpu.VMEM((3 * cols, rows), F32),
                pltpu.VMEM((3 * width, rows), BF16),
                pltpu.SemaphoreType.DMA((pieces, 3)),
            ],
        ),
        out_shape=[
            jax.ShapeDtypeStruct((pieces, 4 * cols, width), BF16),
            jax.ShapeDtypeStruct((pieces, 3 * cols, 1), F32),
            jax.ShapeDtypeStruct((rows, width), BF16),
            jax.ShapeDtypeStruct((2, width), F32),
        ],
        compiler_params=pltpu.CompilerParams(vmem_limit_bytes=VMEM_LIMIT),
        cost_estimate=pl.CostEstimate(flops=40_000_000_000, bytes_accessed=20_000_000, transcendentals=0),
        name="mixer_backward",
    )(sel, start, tiles, segment, hidden, middle_grad, norm, qkv, mixed, totals, *flat(own), *flat(other))


def route(change):
    shape = [lax.axis_size(axis) for axis in AXES]
    pairs = []
    for s in range(shape[0]):
        for d in range(shape[1]):
            for t in range(shape[2]):
                to = change(s, d, t)
                if to is not None:
                    pairs.append(((s * shape[1] + d) * shape[2] + t, (to[0] * shape[1] + to[1]) * shape[2] + to[2]))
    return pairs


def swap(block, change):
    return lax.ppermute(block, AXES, route(change))


def over_tensor(s, d, t):
    return (s, d, 1 - t)


def over_section(s, d, t):
    return (1 - s, d, t)


def over_core(s, d, t):
    return (s, d ^ 1, t)


def gather_family(own_halves, core):
    mine = lax.dynamic_index_in_dim(own_halves, core, 0, keepdims=False)
    twin = lax.dynamic_index_in_dim(own_halves, 1 - core, 0, keepdims=False)
    half = mine.shape[0] // 2
    beside = swap(mine, over_tensor)
    across = swap(mine, over_section)
    far_low = swap(beside[:half], over_section)
    far_high = swap(across[half:], over_tensor)

    def halves(piece):
        return (piece[:half], piece[half:])

    own = [halves(mine), halves(twin), halves(beside), halves(swap(beside, over_core))]
    other = [
        halves(across),
        halves(swap(across, over_core)),
        (far_low, far_high),
        (swap(far_low, over_core), swap(far_high, over_core)),
    ]
    return own, other


def take_half(block, which, axis):
    half = block.shape[axis] // 2
    return lax.dynamic_slice_in_dim(block, which * half, half, axis)


def added(left, right):
    return (left.astype(F32) + right.astype(F32)).astype(BF16)


def reduce_family(grads, layer, section, core, z_index, z_count):
    pieces, rows, columns = grads.shape
    pairs = grads.reshape(2, 2, rows, columns)
    chip = added(pairs[:, 0], swap(pairs[:, 1], over_core))
    lane = added(chip[0], swap(chip[1], over_tensor))
    part = added(take_half(lane, section, 0), swap(take_half(lane, 1 - section, 0), over_section))
    bits = []
    distance = 1
    while distance < z_count:
        bits.append(distance)
        distance *= 2
    for distance in bits:
        along = lambda s, d, t, distance=distance: (s, ((d // 2) ^ distance) * 2 + d % 2, t)
        bit = (z_index // distance) % 2
        part = added(take_half(part, bit, 0), swap(take_half(part, 1 - bit, 0), along))
    for distance in reversed(bits):
        along = lambda s, d, t, distance=distance: (s, ((d // 2) ^ distance) * 2 + d % 2, t)
        bit = (z_index // distance) % 2
        came = swap(part, along)
        part = jnp.where(bit == 0, jnp.concatenate([part, came], 0), jnp.concatenate([came, part], 0))
    back = swap(part, lambda s, d, t: (layer, d, t) if s != layer else None)
    whole = jnp.concatenate([part, back] if layer == 0 else [back, part], 0)
    twin = swap(whole, over_core)
    return jnp.where(core == 0, jnp.stack([whole, twin]), jnp.stack([twin, whole]))


def spread_output(block, layer, lane):
    mine = take_half(block, lane, 0)
    rest = take_half(block, 1 - lane, 0)
    return [
        mine,
        swap(rest, lambda s, d, t: (s, d, 1 - t) if s == layer else None),
        swap(mine, lambda s, d, t: (layer, d, t) if s != layer else None),
        swap(rest, lambda s, d, t: (layer, d, 1 - t) if s != layer else None),
    ]


def reordered(pieces, lane, core):
    pieces = jnp.where(lane == 0, pieces, pieces[jnp.array([2, 3, 0, 1])])
    return jnp.where(core == 0, pieces, pieces[jnp.array([1, 0, 3, 2])])


def one_sequence_each(
    inputs,
    cotangent,
    segment_ids,
    norm_gains,
    norm_biases,
    qkv_weight,
    qv_bias,
    out_weight,
    up_weight,
    up_bias,
    down_weight,
    out_biases,
):
    section = lax.axis_index("section")
    group = lax.axis_index("dp")
    lane = lax.axis_index("tensor")
    core = group % 2
    z_index = group // 2
    z_count = lax.axis_size("dp") // 2
    own_rows, width = inputs.shape[1:]
    hidden = up_bias.shape[1]
    cols = qkv_weight.shape[3]
    part = cols // 2
    mine = 2 * section + lane

    projections = qkv_weight[0].transpose(0, 2, 1).reshape(3, 2, part, width).transpose(1, 0, 2, 3)
    mixer_halves = jnp.concatenate(
        [projections.reshape(2, 3 * part, width), out_weight[0].reshape(2, part, width)], axis=1
    )
    up_halves = up_weight[0].reshape(width, 2, -1).transpose(1, 0, 2)
    down_halves = down_weight[0].reshape(2, -1, width)

    def whole_sequence(array):
        kept = lax.dynamic_index_in_dim(array, mine, 0, keepdims=False)
        sent = lax.dynamic_index_in_dim(array, 2 * section + 1 - lane, 0, keepdims=False)
        came = swap(sent, over_tensor)
        return jnp.where(lane == 0, jnp.concatenate([kept, came], 0), jnp.concatenate([came, kept], 0))

    small = jnp.concatenate(
        [
            norm_gains.reshape(-1),
            norm_biases.reshape(-1),
            qv_bias.reshape(-1),
            up_bias.reshape(-1),
            out_biases.reshape(-1),
        ]
    )
    small_other = swap(small, over_section)
    smalls = [jnp.where(section == layer, small, small_other) for layer in range(2)]

    first_in = whole_sequence(inputs)
    mixer_own, mixer_other = gather_family(mixer_halves, core)
    up_own, up_other = gather_family(up_halves, core)
    down_own, down_other = gather_family(down_halves, core)
    last_grad = whole_sequence(cotangent)

    segment = lax.dynamic_index_in_dim(segment_ids, mine, 0, keepdims=True)
    ids = jnp.arange(IMAGE_IDS, dtype=jnp.int32)[:, None]
    begin = jnp.sum((segment < ids).astype(jnp.int32), axis=1)
    end = jnp.sum((segment <= ids).astype(jnp.int32), axis=1)
    start = begin // TILE
    images = (start, (end - 1) // TILE - start + 1, segment)

    def params(layer):
        vector = smalls[layer]
        gains = vector[: 2 * width].reshape(2, width)
        shifts = vector[2 * width : 4 * width].reshape(2, width)
        qv = vector[4 * width : 6 * width].reshape(2, 4, part)
        ups = vector[6 * width : 6 * width + hidden].reshape(4, hidden // 4)
        outs = vector[6 * width + hidden :].reshape(2, 1, width)
        zero = jnp.zeros((4, part), F32)
        qkv_shift = jnp.concatenate([reordered(qv[0], lane, core), zero, reordered(qv[1], lane, core)], axis=1)
        up_shift = reordered(ups, lane, core).reshape(1, hidden)
        norms = [jnp.stack([gains[i], shifts[i]]) for i in range(2)]
        return norms, qkv_shift[:, :, None], up_shift, outs

    state = first_in
    kept = []
    outputs = []
    for layer in range(2):
        sel = (section ^ layer).astype(jnp.int32).reshape(1)
        norms, qkv_shift, up_shift, outs = params(layer)
        qkv, mixed, totals, middle = mixer_forward(
            sel, images, state, norms[0], qkv_shift, outs[0], mixer_own, mixer_other
        )
        result, active, slope = feed_forward(
            sel, middle, norms[1], up_shift, outs[1], up_own, down_own, up_other, down_other
        )
        kept.append((sel, norms, state, qkv, mixed, totals, middle, active, slope))
        state = result
        outputs.append(spread_output(result, layer, lane))

    grad = last_grad
    weight_grads = [None, None]
    small_grads = [None, None]
    in_grads = [None, None]
    for layer in (1, 0):
        sel, norms, state, qkv, mixed, totals, middle, active, slope = kept[layer]
        feed_grads, up_shift_grad, middle_grad, feed_small = feed_backward(
            sel, grad, middle, norms[1], active, slope, up_own, down_own, up_other, down_other
        )
        feed_sum = reduce_family(feed_grads, layer, section, core, z_index, z_count)
        mixer_grads, qkv_shift_grad, grad, mixer_small = mixer_backward(
            sel, images, state, middle_grad, norms[0], qkv, mixed, totals, mixer_own, mixer_other
        )
        in_grads[layer] = spread_output(grad, layer, lane)
        mixer_sum = reduce_family(mixer_grads, layer, section, core, z_index, z_count)
        weight_grads[layer] = (feed_sum, mixer_sum)
        qkv_shift_grad = qkv_shift_grad.reshape(4, 3, part)
        query_grad = reordered(qkv_shift_grad[:, 0], lane, core).reshape(-1)
        value_grad = reordered(qkv_shift_grad[:, 2], lane, core).reshape(-1)
        up_grad = reordered(up_shift_grad.reshape(4, hidden // 4), lane, core).reshape(-1)
        vector = jnp.concatenate(
            [
                mixer_small[0],
                feed_small[0],
                mixer_small[1],
                feed_small[1],
                query_grad,
                value_grad,
                up_grad,
                feed_small[2],
                feed_small[3],
            ]
        )
        small_grads[layer] = lax.psum(vector, AXES)

    def pick(pair):
        return jnp.where(section == 0, pair[0], pair[1])

    def gathered(pair):
        relative = jnp.stack([pick(both) for both in zip(*pair)])
        relative = jnp.where(lane == 0, relative, relative[jnp.array([1, 0, 3, 2])])
        return jnp.where(section == 0, relative, relative[jnp.array([2, 3, 0, 1])])

    states = gathered(outputs)
    grads = gathered(in_grads).astype(F32)
    feed_sum = pick([pair[0] for pair in weight_grads]).astype(F32)
    mixer_sum = pick([pair[1] for pair in weight_grads]).astype(F32)
    vector = pick(small_grads)
    qkv_grad = mixer_sum[:, : 3 * part].reshape(2, 3, part, width).transpose(1, 3, 0, 2).reshape(3, width, cols)
    out_grad = mixer_sum[:, 3 * part :].reshape(cols, width)
    up_grad = feed_sum[:, :width].transpose(1, 0, 2).reshape(width, -1)
    down_grad = feed_sum[:, width:].transpose(0, 2, 1).reshape(-1, width)
    return (
        states[None],
        grads[None],
        vector[: 2 * width].reshape(1, 2, width),
        vector[2 * width : 4 * width].reshape(1, 2, width),
        qkv_grad[None],
        vector[4 * width : 6 * width].reshape(1, 2, width),
        out_grad[None],
        up_grad[None],
        vector[6 * width : 6 * width + hidden].reshape(1, hidden),
        down_grad[None],
        vector[6 * width + hidden :].reshape(1, 2, width),
    )


def passed_along(block, axis, distance):
    devices = range(lax.axis_size(axis))
    route = [(i - distance, i) for i in devices if i - distance in devices]
    return lax.ppermute(block, axis, route)


def norm_parts(token_rows, gain_row, shift_row):
    centre = token_rows - jnp.mean(token_rows, axis=-1, keepdims=True)
    inverse = lax.rsqrt(jnp.mean(centre * centre, axis=-1, keepdims=True) + EPSILON)
    scaled = centre * inverse
    return (scaled * gain_row + shift_row, scaled, inverse)


def norm_back(gradient, scaled, inverse, gain_row):
    upstream = gradient * gain_row
    return inverse * (
        upstream
        - jnp.mean(upstream, axis=-1, keepdims=True)
        - scaled * jnp.mean(upstream * scaled, axis=-1, keepdims=True)
    )


def gelu_exact(values):
    return jax.nn.gelu(values, approximate=False)


def head_view(matrix, heads_local):
    return matrix.reshape(matrix.shape[0], heads_local, HEAD_DIM)


def join_heads(stacked):
    return stacked.transpose(1, 0, 2).reshape(stacked.shape[1], stacked.shape[0] * stacked.shape[2])


def attend_forward(queries, key_rows, value_rows, segment):
    seq_len = queries.shape[0]
    half_rows = seq_len // 2
    heads_local = queries.shape[1] // HEAD_DIM
    scaling = HEAD_DIM ** (-0.5)
    query_heads = head_view(queries, heads_local)
    key_heads = head_view(key_rows, heads_local)
    value_heads = head_view(value_rows, heads_local)

    def one_item(item):
        head_index = item // 2
        row_start = item % 2 * half_rows
        head_keys = lax.dynamic_index_in_dim(key_heads, head_index, 1, keepdims=False)
        head_values = lax.dynamic_index_in_dim(value_heads, head_index, 1, keepdims=False)
        head_queries = lax.dynamic_index_in_dim(query_heads, head_index, 1, keepdims=False)
        block_queries = lax.dynamic_slice_in_dim(head_queries, row_start, half_rows, 0)
        block_segment = lax.dynamic_slice_in_dim(segment, row_start, half_rows, 0)
        scores = (
            jnp.einsum("qd,kd->qk", block_queries, head_keys, preferred_element_type=jnp.float32)
            * scaling
        )
        scores = jnp.where(block_segment[:, None] == segment[None, :], scores, NEGATIVE)
        row_peak = jnp.max(scores, axis=-1, keepdims=True)
        expanded = jnp.exp(scores - row_peak)
        denominator = jnp.sum(expanded, axis=-1, keepdims=True)
        weights = (expanded / denominator).astype(jnp.bfloat16)
        block_out = jnp.dot(weights, head_values, preferred_element_type=jnp.float32).astype(
            jnp.bfloat16
        )
        return (block_out, row_peak[:, 0] + jnp.log(denominator[:, 0]))

    outputs, log_totals = lax.map(one_item, jnp.arange(2 * heads_local, dtype=jnp.int32))
    mixed_rows = join_heads(outputs.reshape(heads_local, seq_len, HEAD_DIM))
    return (mixed_rows, log_totals.reshape(heads_local, seq_len))


def attend_backward(queries, key_rows, value_rows, mixed_grad, log_totals, segment):
    seq_len = queries.shape[0]
    half_rows = seq_len // 2
    heads_local = queries.shape[1] // HEAD_DIM
    scaling = HEAD_DIM ** (-0.5)
    query_heads = head_view(queries, heads_local)
    key_heads = head_view(key_rows, heads_local)
    value_heads = head_view(value_rows, heads_local)
    grad_heads = head_view(mixed_grad, heads_local)

    def one_head(head_index):
        head_queries = lax.dynamic_index_in_dim(query_heads, head_index, 1, keepdims=False)
        head_keys = lax.dynamic_index_in_dim(key_heads, head_index, 1, keepdims=False)
        head_values = lax.dynamic_index_in_dim(value_heads, head_index, 1, keepdims=False)
        head_grads = lax.dynamic_index_in_dim(grad_heads, head_index, 1, keepdims=False)
        head_totals = lax.dynamic_index_in_dim(log_totals, head_index, 0, keepdims=False)

        def one_block(carry, block_index):
            key_grad, value_grad = carry
            row_start = block_index * half_rows
            block_queries = lax.dynamic_slice_in_dim(head_queries, row_start, half_rows, 0)
            block_grads = lax.dynamic_slice_in_dim(head_grads, row_start, half_rows, 0)
            block_totals = lax.dynamic_slice_in_dim(head_totals, row_start, half_rows, 0)
            block_segment = lax.dynamic_slice_in_dim(segment, row_start, half_rows, 0)
            scores = (
                jnp.einsum(
                    "qd,kd->qk", block_queries, head_keys, preferred_element_type=jnp.float32
                )
                * scaling
            )
            scores = jnp.where(block_segment[:, None] == segment[None, :], scores, NEGATIVE)
            weights = jnp.exp(scores - block_totals[:, None])
            low_weights = weights.astype(jnp.bfloat16)
            block_out = jnp.dot(
                low_weights, head_values, preferred_element_type=jnp.float32
            ).astype(jnp.bfloat16)
            weight_grads = jnp.einsum(
                "qd,kd->qk", block_grads, head_values, preferred_element_type=jnp.float32
            )
            row_terms = jnp.sum(weights * weight_grads, axis=-1, keepdims=True)
            score_grads = (weights * (weight_grads - row_terms)).astype(jnp.bfloat16)
            query_grad = (
                jnp.dot(score_grads, head_keys, preferred_element_type=jnp.float32) * scaling
            )
            key_grad = (
                key_grad
                + jnp.einsum(
                    "qk,qd->kd", score_grads, block_queries, preferred_element_type=jnp.float32
                )
                * scaling
            )
            value_grad = value_grad + jnp.einsum(
                "qk,qd->kd", low_weights, block_grads, preferred_element_type=jnp.float32
            )
            return ((key_grad, value_grad), (block_out, query_grad))

        empty = jnp.zeros((seq_len, HEAD_DIM), jnp.float32)
        (key_grad, value_grad), (block_outs, query_grads) = lax.scan(
            one_block, (empty, empty), jnp.arange(2, dtype=jnp.int32)
        )
        return (
            block_outs.reshape(seq_len, HEAD_DIM),
            query_grads.reshape(seq_len, HEAD_DIM),
            key_grad,
            value_grad,
        )

    results = lax.map(one_head, jnp.arange(heads_local, dtype=jnp.int32))
    return tuple((join_heads(item) for item in results))


def store_at(array, value, which, running):
    return array.at[which].set(jnp.where(running, value, array[which]))


def pipelined(
    inputs,
    cotangent,
    segment_ids,
    norm_gains,
    norm_biases,
    qkv_weight,
    qv_bias,
    out_weight,
    up_weight,
    up_bias,
    down_weight,
    out_biases,
):
    section_index = lax.axis_index("section")
    section_count = lax.axis_size("section")
    lane_index = lax.axis_index("tensor")
    micro_count, own_rows, model_width = inputs.shape
    seq_len = segment_ids.shape[1]
    cols_local = qkv_weight.shape[3]
    hidden_local = up_weight.shape[2]
    heads_local = cols_local // HEAD_DIM
    gain_rows = norm_gains[0]
    shift_rows = norm_biases[0]
    joined = jnp.concatenate([qkv_weight[0, 0], qkv_weight[0, 1], qkv_weight[0, 2]], axis=1)
    query_shift = lax.dynamic_slice_in_dim(qv_bias[0, 0], lane_index * cols_local, cols_local)
    value_shift = lax.dynamic_slice_in_dim(qv_bias[0, 1], lane_index * cols_local, cols_local)
    up_shift = lax.dynamic_slice_in_dim(up_bias[0], lane_index * hidden_local, hidden_local)
    out_matrix = out_weight[0]
    up_matrix = up_weight[0]
    down_matrix = down_weight[0]
    mixer_shift = out_biases[0, 0]
    feed_shift = out_biases[0, 1]

    def spread_rows(normed_rows, weight):
        return (
            None,
            jnp.dot(
                lax.all_gather(normed_rows, "tensor", axis=0, tiled=True),
                weight,
                preferred_element_type=jnp.float32,
            ),
        )

    def regather(normed_rows):
        return lax.all_gather(normed_rows, "tensor", axis=0, tiled=True)

    def gather_grads(grad_rows):
        return lax.all_gather(grad_rows.astype(jnp.bfloat16), "tensor", axis=0, tiled=True)

    def branch_sum(left_rows, weight):
        return lax.psum_scatter(
            jnp.dot(left_rows, weight, preferred_element_type=jnp.float32).astype(jnp.bfloat16),
            "tensor",
            scatter_dimension=0,
            tiled=True,
        ).astype(jnp.float32)

    def input_sum(grad_rows, weight):
        return lax.psum_scatter(
            jnp.einsum("sc,dc->sd", grad_rows, weight, preferred_element_type=jnp.float32).astype(
                jnp.bfloat16
            ),
            "tensor",
            scatter_dimension=0,
            tiled=True,
        ).astype(jnp.float32)

    def split_projected(projected):
        queries = (projected[:, :cols_local] + query_shift).astype(jnp.bfloat16)
        key_rows = projected[:, cols_local : 2 * cols_local].astype(jnp.bfloat16)
        value_rows = (projected[:, 2 * cols_local :] + value_shift).astype(jnp.bfloat16)
        return (queries, key_rows, value_rows)

    def layer_backward(block_in, middle, log_totals, segment, out_grad):
        residual = block_in.astype(jnp.float32)
        full_grad = gather_grads(out_grad)
        normed_two, scaled_two, inverse_two = norm_parts(middle, gain_rows[1], shift_rows[1])
        normed_two = normed_two.astype(jnp.bfloat16)
        full_two = regather(normed_two)
        hidden = jnp.dot(full_two, up_matrix, preferred_element_type=jnp.float32) + up_shift
        active, gelu_pullback = jax.vjp(gelu_exact, hidden)
        active = active.astype(jnp.bfloat16)
        down_grad = jnp.einsum("sf,sd->fd", active, full_grad, preferred_element_type=jnp.float32)
        active_grad = jnp.einsum(
            "sd,fd->sf", full_grad, down_matrix, preferred_element_type=jnp.float32
        )
        hidden_grad = gelu_pullback(active_grad)[0]
        up_shift_grad = jnp.sum(hidden_grad, axis=0)
        hidden_low = hidden_grad.astype(jnp.bfloat16)
        up_grad = jnp.einsum("sd,sf->df", full_two, hidden_low, preferred_element_type=jnp.float32)
        normed_grad_two = input_sum(hidden_low, up_matrix)
        feed_shift_grad = jnp.sum(out_grad, axis=0)
        middle_grad = out_grad + norm_back(normed_grad_two, scaled_two, inverse_two, gain_rows[1])
        gain_two = jnp.sum(normed_grad_two * scaled_two, axis=0)
        shift_two = jnp.sum(normed_grad_two, axis=0)
        full_mid_grad = gather_grads(middle_grad)
        normed_one, scaled_one, inverse_one = norm_parts(residual, gain_rows[0], shift_rows[0])
        normed_one = normed_one.astype(jnp.bfloat16)
        full_one = regather(normed_one)
        projected = jnp.dot(full_one, joined, preferred_element_type=jnp.float32)
        queries, key_rows, value_rows = split_projected(projected)
        mixed_grad = jnp.einsum(
            "sd,cd->sc", full_mid_grad, out_matrix, preferred_element_type=jnp.float32
        ).astype(jnp.bfloat16)
        mixed_rows, query_grad, key_grad, value_grad = attend_backward(
            queries, key_rows, value_rows, mixed_grad, log_totals, segment
        )
        out_grad_matrix = jnp.einsum(
            "sc,sd->cd", mixed_rows, full_mid_grad, preferred_element_type=jnp.float32
        )
        mixer_shift_grad = jnp.sum(middle_grad, axis=0)
        qkv_low = jnp.concatenate([query_grad, key_grad, value_grad], axis=1).astype(jnp.bfloat16)
        joined_grad = jnp.einsum("sd,sc->dc", full_one, qkv_low, preferred_element_type=jnp.float32)
        normed_grad_one = input_sum(qkv_low, joined)
        in_grad = middle_grad + norm_back(normed_grad_one, scaled_one, inverse_one, gain_rows[0])
        gain_one = jnp.sum(normed_grad_one * scaled_one, axis=0)
        shift_one = jnp.sum(normed_grad_one, axis=0)
        qv_local = jnp.stack([jnp.sum(query_grad, axis=0), jnp.sum(value_grad, axis=0)])
        qv_full = lax.dynamic_update_slice_in_dim(
            jnp.zeros((2, model_width), jnp.float32), qv_local, lane_index * cols_local, 1
        )
        up_full = lax.dynamic_update_slice_in_dim(
            jnp.zeros((up_bias.shape[1],), jnp.float32), up_shift_grad, lane_index * hidden_local, 0
        )
        weight_terms = (joined_grad, out_grad_matrix, up_grad, down_grad)
        small_terms = (
            jnp.stack([gain_one, gain_two]),
            jnp.stack([shift_one, shift_two]),
            qv_full,
            up_full,
            jnp.stack([mixer_shift_grad, feed_shift_grad]),
        )
        return (in_grad, weight_terms, small_terms)

    ticks = micro_count + section_count - 1
    received = jnp.zeros((own_rows, model_width), jnp.bfloat16)
    saved_in = jnp.zeros_like(inputs)
    saved_mid = jnp.zeros((micro_count, own_rows, model_width), jnp.float32)
    saved_totals = jnp.zeros((micro_count, heads_local, seq_len), jnp.float32)
    states = jnp.zeros_like(inputs)
    for tick in range(ticks):
        micro = tick - section_index
        running = (micro >= 0) & (micro < micro_count)
        which = jnp.clip(micro, 0, micro_count - 1)
        own_in = lax.dynamic_index_in_dim(inputs, which, 0, keepdims=False)
        block_in = jnp.where(section_index == 0, own_in, received)
        segment = lax.dynamic_index_in_dim(segment_ids, which, 0, keepdims=False)
        layer_residual = block_in.astype(jnp.float32)
        layer_normed_one = norm_parts(layer_residual, gain_rows[0], shift_rows[0])[0].astype(
            jnp.bfloat16
        )
        layer_full_one, layer_projected = spread_rows(layer_normed_one, joined)
        layer_queries, layer_key_rows, layer_value_rows = split_projected(layer_projected)
        layer_mixed_rows, layer_log_totals = attend_forward(
            layer_queries, layer_key_rows, layer_value_rows, segment
        )
        layer_middle = layer_residual + branch_sum(layer_mixed_rows, out_matrix) + mixer_shift
        layer_normed_two = norm_parts(layer_middle, gain_rows[1], shift_rows[1])[0].astype(
            jnp.bfloat16
        )
        layer_full_two, layer_hidden = spread_rows(layer_normed_two, up_matrix)
        layer_active = gelu_exact(layer_hidden + up_shift).astype(jnp.bfloat16)
        block_out = layer_middle + branch_sum(layer_active, down_matrix) + feed_shift
        block_out, middle, log_totals, full_one, full_two = (
            block_out,
            layer_middle,
            layer_log_totals,
            layer_full_one,
            layer_full_two,
        )
        handed = block_out.astype(jnp.bfloat16)
        saved_in = store_at(saved_in, block_in, which, running)
        saved_mid = store_at(saved_mid, middle, which, running)
        saved_totals = store_at(saved_totals, log_totals, which, running)
        states = store_at(states, handed, which, running)
        if tick + 1 < ticks:
            received = passed_along(handed, "section", 1)
    back_received = jnp.zeros((own_rows, model_width), jnp.bfloat16)
    weight_totals = (
        jnp.zeros(joined.shape, jnp.float32),
        jnp.zeros(out_matrix.shape, jnp.float32),
        jnp.zeros(up_matrix.shape, jnp.float32),
        jnp.zeros(down_matrix.shape, jnp.float32),
    )
    small_totals = (
        jnp.zeros((2, model_width), jnp.float32),
        jnp.zeros((2, model_width), jnp.float32),
        jnp.zeros((2, model_width), jnp.float32),
        jnp.zeros((up_bias.shape[1],), jnp.float32),
        jnp.zeros((2, model_width), jnp.float32),
    )
    grads_store = jnp.zeros((micro_count, own_rows, model_width), jnp.float32)
    for tick in range(ticks):
        micro = tick - (section_count - 1) + section_index
        running = (micro >= 0) & (micro < micro_count)
        which = jnp.clip(micro, 0, micro_count - 1)
        own_grad = lax.dynamic_index_in_dim(cotangent, which, 0, keepdims=False)
        out_grad = jnp.where(section_index == section_count - 1, own_grad, back_received).astype(
            jnp.float32
        )
        in_grad, weight_terms, small_terms = layer_backward(
            lax.dynamic_index_in_dim(saved_in, which, 0, keepdims=False),
            lax.dynamic_index_in_dim(saved_mid, which, 0, keepdims=False),
            lax.dynamic_index_in_dim(saved_totals, which, 0, keepdims=False),
            lax.dynamic_index_in_dim(segment_ids, which, 0, keepdims=False),
            out_grad,
        )
        joined_term, out_term, up_term, down_term = tuple(
            (jnp.where(running, term, 0.0) for term in weight_terms)
        )
        weight_terms = (joined_term, out_term, up_term, down_term)
        weight_totals = tuple((total + term for total, term in zip(weight_totals, weight_terms)))
        small_totals = tuple(
            (
                total + jnp.where(running, term, 0.0)
                for total, term in zip(small_totals, small_terms)
            )
        )
        grads_store = store_at(grads_store, in_grad, which, running)
        if tick + 1 < ticks:
            back_received = passed_along(in_grad.astype(jnp.bfloat16), "section", -1)
    joined_total, out_total, up_total, down_total = weight_totals
    summed = (
        lax.psum(joined_total.astype(jnp.bfloat16), "dp").astype(jnp.float32),
        lax.psum(out_total.astype(jnp.bfloat16), "dp").astype(jnp.float32),
        lax.psum(up_total.astype(jnp.bfloat16), "dp").astype(jnp.float32),
        lax.psum(down_total.astype(jnp.bfloat16), "dp").astype(jnp.float32),
    )
    gain_total, shift_total, qv_total, up_shift_total, out_shift_total = small_totals
    small_summed = lax.psum(
        (gain_total, shift_total, qv_total, up_shift_total, out_shift_total), ("dp", "tensor")
    )
    qkv_grad = summed[0].reshape(model_width, 3, cols_local).transpose(1, 0, 2)
    return (
        states[None],
        grads_store[None],
        small_summed[0][None],
        small_summed[1][None],
        qkv_grad[None],
        small_summed[2][None],
        summed[1][None],
        summed[2][None],
        small_summed[3][None],
        summed[3][None],
        small_summed[4][None],
    )


def solution(mesh):
    placed = (
        P("dp", "tensor", None),
        P("dp", "tensor", None),
        P("dp", None),
        P("section", None, None),
        P("section", None, None),
        P("section", None, None, "tensor"),
        P("section", None, None),
        P("section", "tensor", None),
        P("section", None, "tensor"),
        P("section", None),
        P("section", "tensor", None),
        P("section", None, None),
    )
    sizes = dict(mesh.shape)

    def on_device(inputs, *rest):
        each = inputs.shape[0] == sizes["section"] * sizes["tensor"]
        paired = sizes["section"] == 2 and sizes["tensor"] == 2 and sizes["dp"] % 2 == 0
        doubling = (sizes["dp"] // 2) & (sizes["dp"] // 2 - 1) == 0
        if each and paired and doubling:
            return one_sequence_each(inputs, *rest)
        return pipelined(inputs, *rest)

    return jax.shard_map(
        on_device,
        mesh=mesh,
        in_specs=placed,
        out_specs=(
            P("section", "dp", "tensor", None),
            P("section", "dp", "tensor", None),
            P("section", None, None),
            P("section", None, None),
            P("section", None, None, "tensor"),
            P("section", None, None),
            P("section", "tensor", None),
            P("section", None, "tensor"),
            P("section", None),
            P("section", "tensor", None),
            P("section", None, None),
        ),
        check_vma=False,
    )
```

```python
import functools
import math

import jax
import jax.numpy as jnp
from jax import lax
from jax.experimental import pallas as pl
from jax.experimental.pallas import tpu as pltpu
from jax.sharding import PartitionSpec as P

HEAD_DIM = 48
IMAGE_IDS = 5
IMAGE_MOST = 512
EPSILON = 1e-05
NEGATIVE = -1e30
TILE = 128
BLOCK = 256
EXTRA = 16
LOG2E = math.log2(math.e)
SCALING = HEAD_DIM ** (-0.5)
AXES = ("section", "dp", "tensor")
VMEM_LIMIT = 60 * 1024 * 1024
MESH = pl.DeviceIdType.MESH
F32 = jnp.float32
BF16 = jnp.bfloat16


def nn(left, right):
    return lax.dot_general(left, right, (((1,), (0,)), ((), ())), preferred_element_type=F32)


def nt(left, right):
    return lax.dot_general(left, right, (((1,), (1,)), ((), ())), preferred_element_type=F32)


def tn(left, right):
    return lax.dot_general(left, right, (((0,), (0,)), ((), ())), preferred_element_type=F32)


def normalise(rows):
    centre = rows - jnp.mean(rows, axis=-1, keepdims=True)
    inverse = lax.rsqrt(jnp.mean(centre * centre, axis=-1, keepdims=True) + EPSILON)
    return centre * inverse, inverse


def normalise_back(gradient, scaled, inverse, gain):
    upstream = gradient * gain
    return inverse * (
        upstream
        - jnp.mean(upstream, axis=-1, keepdims=True)
        - scaled * jnp.mean(upstream * scaled, axis=-1, keepdims=True)
    )


def gelu_pair(values):
    share = 0.5 + 0.5 * lax.erf(values * math.sqrt(0.5))
    bell = jnp.exp2(values * values * (-0.5 * LOG2E))
    return values * share, share + values * bell * (1.0 / math.sqrt(2 * math.pi))


def extra_rows(rows, width):
    at = lax.broadcasted_iota(jnp.int32, (EXTRA, width), 0)
    out = jnp.zeros((EXTRA, width), F32)
    for index, row in enumerate(rows):
        out = jnp.where(at == index, row, out)
    return out.astype(BF16)


def three_parts(row):
    first = row.astype(BF16).astype(F32)
    second = (row - first).astype(BF16).astype(F32)
    return [first, second, row - first - second]


def each_image(start_ref, tiles_ref, body):
    most = IMAGE_MOST // TILE + 1

    def image(index, carry):
        first = start_ref[index]
        tiles = tiles_ref[index]
        for count in range(1, most + 1):

            @pl.when(tiles == count)
            def _():
                body(index, pl.multiple_of(first * TILE, TILE), count * TILE)

        return carry

    lax.fori_loop(0, IMAGE_IDS, image, 0)


def run_copies(copies):
    for copy in copies:
        copy.start()


def wait_copies(copies):
    for copy in copies:
        copy.wait()


def slot_of(place_ref, index):
    return 2 * (place_ref[0] ^ (index // 2)) + (place_ref[1] ^ (index % 2))


def once(shape):
    zeros = (0,) * len(shape)
    return pl.BlockSpec(shape, lambda *_: zeros, pipeline_mode=pl.Buffered(1))


def anywhere(count):
    return [pl.BlockSpec(memory_space=pl.ANY)] * count


def settings(flops, collective=None):
    remote = {} if collective is None else dict(collective_id=collective, has_side_effects=True)
    return dict(
        compiler_params=pltpu.CompilerParams(vmem_limit_bytes=VMEM_LIMIT, **remote),
        cost_estimate=pl.CostEstimate(flops=flops, bytes_accessed=1_000_000, transcendentals=0),
    )


def blocks_of(ref, axis=0):
    return ref.shape[axis] // BLOCK


def block_at(index):
    return pl.ds(pl.multiple_of(index * BLOCK, BLOCK), BLOCK)


def big_blocks(rows):
    size = rows // 2
    return [slice(i * size, (i + 1) * size) for i in range(2)]


def attend_forward_image(index, at, width, heads, seg_ref, qkv_ref, store):
    win = pl.ds(at, width)
    mine = seg_ref[:, win] == index
    mask = jnp.where(mine, 0.0, NEGATIVE)
    one = jnp.ones((1, width), F32)
    query_extra = extra_rows([mask, one], width)
    key_extra = extra_rows([one, mask], width)
    value_extra = extra_rows([one], width)
    cols = heads * HEAD_DIM

    def rows_of(third, head):
        low = third * cols + head * HEAD_DIM
        return qkv_ref[low : low + HEAD_DIM, win]

    def scores(head):
        queries = jnp.concatenate([rows_of(0, head), query_extra], axis=0)
        keys = jnp.concatenate([rows_of(1, head), key_extra], axis=0)
        return tn(keys, queries)

    following = scores(0)
    for head in range(heads):
        current = following
        if head + 1 < heads:
            following = scores(head + 1)
        peak = jnp.max(current, axis=0, keepdims=True)
        weights = jnp.exp2(current - peak).astype(BF16)
        mixed = nn(jnp.concatenate([rows_of(2, head), value_extra], axis=0), weights)
        total = mixed[HEAD_DIM : HEAD_DIM + 1]
        store(head, win, mine, mixed[:HEAD_DIM] * (1.0 / total), peak + jnp.log2(total))


def attend_backward_image(index, at, width, heads, seg_ref, qkv_ref, mixed_ref, total_ref, mixed_grad, sums):
    win = pl.ds(at, width)
    mine = seg_ref[:, win] == index
    mask = jnp.where(mine, 0.0, NEGATIVE)
    one = jnp.ones((1, width), F32)
    key_extra = extra_rows([one, mask, one, one, one], width)
    value_extra = extra_rows([one, one, one], width)
    cols = heads * HEAD_DIM

    def span(third, head):
        low = third * cols + head * HEAD_DIM
        return slice(low, low + HEAD_DIM)

    def products(head):
        own = span(0, head)
        grads = mixed_grad[own, win]
        inner = jnp.sum(grads.astype(F32) * mixed_ref[own, win].astype(F32), axis=0, keepdims=True)
        query_extra = extra_rows([mask, one] + three_parts(-total_ref[head, :, win]), width)
        grad_extra = extra_rows(three_parts(-inner), width)
        keys = jnp.concatenate([qkv_ref[span(1, head), win], key_extra], axis=0)
        queries = jnp.concatenate([qkv_ref[own, win], query_extra], axis=0)
        values = jnp.concatenate([qkv_ref[span(2, head), win], value_extra], axis=0)
        return tn(keys, queries), tn(values, jnp.concatenate([grads, grad_extra], axis=0))

    following = products(0)
    for head in range(heads):
        scores, terms = following
        if head + 1 < heads:
            following = products(head + 1)
        weights = jnp.exp2(scores)
        score_grads = (weights * terms).astype(BF16)
        sums[span(0, head), win] += nn(qkv_ref[span(1, head), win], score_grads) * SCALING
        sums[span(1, head), win] += nt(qkv_ref[span(0, head), win], score_grads) * (1.0 / LOG2E)
        sums[span(2, head), win] += nt(mixed_grad[span(0, head), win], weights.astype(BF16))


def mixer_forward_kernel(
    place_ref, start_ref, tiles_ref, seg_ref, hidden_ref, norm_ref, qkv_shift_ref, *rest, pieces, out_pieces, heads
):
    first = out_pieces in (0, pieces)
    last = out_pieces > 0
    rest = list(rest)
    weights = [rest.pop(0) for _ in range(pieces)]
    if not first:
        normed_in = rest.pop(0)
        mixed_before = rest.pop(0)
    if last:
        out_weights = [rest.pop(0) for _ in range(out_pieces)]
        out_shift_ref = rest.pop(0)
    qkv_ref, mixed_ref, total_ref = rest.pop(0), rest.pop(0), rest.pop(0)
    if first:
        normed_out = rest.pop(0)
    if last:
        middle_ref = rest.pop(0)
    weight, normed, sems = rest.pop(0), rest.pop(0), rest.pop(0)
    if last:
        out_weight, mixed_all, out_sems = rest
    step = pl.program_id(0)
    cols = heads * HEAD_DIM
    before = out_pieces - pieces if last else 0
    copies = [
        pltpu.make_async_copy(
            weights[i].at[0 : 3 * cols], weight.at[i], sems.at[i]
        )
        for i in range(pieces)
    ]
    if not first:
        norm_copy = pltpu.make_async_copy(normed_in, normed, sems.at[pieces])
    out_copies = []
    if last:
        for i in range(out_pieces):
            out_copies.append(
                pltpu.make_async_copy(
                    out_weights[i].at[3 * cols : 4 * cols],
                    out_weight.at[i * cols : (i + 1) * cols],
                    out_sems.at[i],
                )
            )
        for i in range(before):
            out_copies.append(
                pltpu.make_async_copy(
                    mixed_before.at[i], mixed_all.at[i * cols : (i + 1) * cols], out_sems.at[out_pieces + i]
                )
            )

    @pl.when(step == 0)
    def _():
        if not first:
            norm_copy.start()
        run_copies(copies + out_copies)
        if first:

            def norm_block(i, carry):
                rows = block_at(i)
                scaled, _ = normalise(hidden_ref[rows, :].astype(F32))
                result = (scaled * norm_ref[0:1, :] + norm_ref[1:2, :]).astype(BF16)
                normed[rows, :] = result
                normed_out[rows, :] = result
                return carry

            lax.fori_loop(0, blocks_of(hidden_ref), norm_block, 0)
        else:
            norm_copy.wait()

    for index in range(pieces):

        @pl.when(step == index)
        def _():
            copies[index].wait()

    projected = nt(weight[step], normed[...]) + qkv_shift_ref[0]
    qkv_ref[0, 0:cols, :] = (projected[0:cols] * (SCALING * LOG2E)).astype(BF16)
    qkv_ref[0, cols : 3 * cols, :] = projected[cols : 3 * cols].astype(BF16)

    def store(head, win, mine, mixed, total):
        rows = slice(head * HEAD_DIM, (head + 1) * HEAD_DIM)
        old = mixed_ref[0, rows, win].astype(F32)
        mixed_ref[0, rows, win] = jnp.where(mine, mixed, old).astype(BF16)
        total_ref[head, :, win] = jnp.where(mine, total, total_ref[head, :, win])

    each_image(
        start_ref,
        tiles_ref,
        lambda index, at, width: attend_forward_image(
            index, at, width, heads, seg_ref, qkv_ref.at[0], store
        ),
    )
    if last:
        mixed_all[pl.ds(pl.multiple_of((before + step) * cols, cols), cols), :] = mixed_ref[0]

        @pl.when(step == pieces - 1)
        def _():
            wait_copies(out_copies)

            for rows in big_blocks(hidden_ref.shape[0]):
                branch = tn(mixed_all[:, rows], out_weight[...])
                middle_ref[rows, :] = hidden_ref[rows, :].astype(F32) + branch + out_shift_ref[...]


def mixer_forward(images, hidden, norm, qkv_shift, pieces, offset=0, before=None, out_pieces=(), out_shift=None):
    rows, width = hidden.shape
    count = len(pieces)
    cols = width // 4
    heads = cols // HEAD_DIM
    place, start, tiles, segment = images
    operands = list(pieces)
    outs = [
        jax.ShapeDtypeStruct((count, 3 * cols, rows), BF16),
        jax.ShapeDtypeStruct((count, cols, rows), BF16),
        jax.ShapeDtypeStruct((count * heads, 1, rows), F32),
    ]
    scratch = [
        pltpu.VMEM((count, 3 * cols, width), BF16),
        pltpu.VMEM((rows, width), BF16),
        pltpu.SemaphoreType.DMA((count + 1,)),
    ]
    if before is None:
        outs.append(jax.ShapeDtypeStruct((rows, width), BF16))
    else:
        operands += list(before)
    specs = anywhere(len(operands) + len(out_pieces))
    operands += list(out_pieces)
    if out_pieces:
        operands.append(out_shift)
        specs.append(once((1, width)))
        outs.append(jax.ShapeDtypeStruct((rows, width), F32))
        scratch += [
            pltpu.VMEM((width, width), BF16),
            pltpu.VMEM((width, rows), BF16),
            pltpu.SemaphoreType.DMA((2 * len(out_pieces),)),
        ]
    return pl.pallas_call(
        functools.partial(
            mixer_forward_kernel,
            pieces=count,
            out_pieces=len(out_pieces),
            heads=heads,
        ),
        grid_spec=pltpu.PrefetchScalarGridSpec(
            num_scalar_prefetch=3,
            grid=(count,),
            in_specs=[
                once((1, rows)),
                once((rows, width)),
                once((2, width)),
                pl.BlockSpec((1, 3 * cols, 1), lambda i, place, *_: (slot_of(place, i + offset), 0, 0)),
            ]
            + specs,
            out_specs=[
                pl.BlockSpec((1, 3 * cols, rows), lambda i, *_: (i, 0, 0)),
                pl.BlockSpec((1, cols, rows), lambda i, *_: (i, 0, 0)),
                pl.BlockSpec((heads, 1, rows), lambda i, *_: (i, 0, 0)),
            ]
            + [once((rows, width))] * (len(outs) - 3),
            scratch_shapes=scratch,
        ),
        out_shape=outs,
        name="mixer_forward",
        **settings(4_000_000_000),
    )(place, start, tiles, segment, hidden, norm, qkv_shift, *operands)


def feed_forward_kernel(place_ref, middle_ref, norm_ref, up_shift_ref, start_ref, *rest, pieces, offset, last):
    ups, downs = rest[:pieces], rest[pieces : 2 * pieces]
    out_ref, active_ref, slope_ref, up_weight, down_weight, sems = rest[2 * pieces :]
    step = pl.program_id(0)
    size = up_weight.shape[2]
    copies = []
    for i in range(pieces):
        copies.append(
            pltpu.make_async_copy(ups[i], up_weight.at[i], sems.at[0, i])
        )
        copies.append(
            pltpu.make_async_copy(downs[i], down_weight.at[i], sems.at[1, i])
        )

    @pl.when(step == 0)
    def _():
        run_copies(copies)

    scaled, _ = normalise(middle_ref[...])
    normed = (scaled * norm_ref[0:1, :] + norm_ref[1:2, :]).astype(BF16)
    total = start_ref[...] if offset else middle_ref[...] + start_ref[...]

    @pl.when(step == 0)
    def _():
        wait_copies(copies)

    def raise_by(index):
        return nn(normed, up_weight[index]) + up_shift_ref[slot_of(place_ref, offset + index)]

    following = raise_by(0)
    for index in range(pieces):
        raised = following
        if index + 1 < pieces:
            following = raise_by(index + 1)
        part = pl.ds(index * size, size)
        active, slope = gelu_pair(raised)
        active = active.astype(BF16)
        active_ref[:, part] = active
        slope_ref[:, part] = slope.astype(BF16)
        total = total + nn(active, down_weight[index])
    out_ref[...] = total.astype(out_ref.dtype)


def feed_forward(place, middle, norm, up_shift, begin, ups, downs, offset, last):
    rows, width = middle.shape
    pieces = len(ups)
    size = up_shift.shape[2]
    hidden = size * pieces
    return pl.pallas_call(
        functools.partial(
            feed_forward_kernel,
            pieces=pieces,
            offset=offset,
            last=last,
        ),
        grid_spec=pltpu.PrefetchScalarGridSpec(
            num_scalar_prefetch=1,
            grid=(rows // BLOCK,),
            in_specs=[
                pl.BlockSpec((BLOCK, width), lambda i, *_: (i, 0)),
                once((2, width)),
                once(up_shift.shape),
                pl.BlockSpec((BLOCK, width), lambda i, *_: (i, 0)) if offset else once((1, width)),
            ]
            + anywhere(2 * pieces),
            out_specs=[
                pl.BlockSpec((BLOCK, width), lambda i, *_: (i, 0)),
                pl.BlockSpec((BLOCK, hidden), lambda i, *_: (i, 0)),
                pl.BlockSpec((BLOCK, hidden), lambda i, *_: (i, 0)),
            ],
            scratch_shapes=[
                pltpu.VMEM((pieces, width, size), BF16),
                pltpu.VMEM((pieces, size, width), BF16),
                pltpu.SemaphoreType.DMA((2, pieces)),
            ],
        ),
        out_shape=[
            jax.ShapeDtypeStruct((rows, width), BF16 if last else F32),
            jax.ShapeDtypeStruct((rows, hidden), BF16),
            jax.ShapeDtypeStruct((rows, hidden), BF16),
        ],
        name="feed_forward",
        **settings(4_000_000_000),
    )(place, middle, norm, up_shift, begin, *ups, *downs)


ORDER = (1, 3, 0, 2)


def greet_core(step):
    group = lax.axis_index("dp")
    other = group + 1 - 2 * lax.rem(group, 2)

    @pl.when(step == 0)
    def _():
        barrier = pltpu.get_barrier_semaphore()
        pl.semaphore_signal(barrier, inc=1, device_id={"dp": other}, device_id_type=MESH)
        pl.semaphore_wait(barrier, 1)

    return other


def sum_with_core(step, other, index, grad_of, sent, came, out_ref, send_sems, recv_sems):
    def copy_of(slot):
        return pltpu.make_async_remote_copy(
            src_ref=sent.at[slot],
            dst_ref=came.at[slot],
            send_sem=send_sems.at[slot],
            recv_sem=recv_sems.at[slot],
            device_id={"dp": other},
            device_id_type=MESH,
        )

    slot = index % 2
    if index < 2:
        grad_of(lambda where, value: sent.__setitem__((slot,) + where, value.astype(BF16)))
        copy_of(slot).start()
    else:
        copy_of(slot).wait_recv()
        grad_of(
            lambda where, value: out_ref.__setitem__(
                (0,) + where, (value + came[(slot,) + where].astype(F32)).astype(BF16)
            )
        )
        copy_of(slot).wait_send()


def feed_backward_kernel(grad_ref, middle_ref, norm_ref, *rest, columns):
    pieces = 4
    rest = list(rest)
    actives = [rest.pop(0) for _ in range(pieces)]
    slopes = [rest.pop(0) for _ in range(pieces)]
    ups = [rest.pop(0) for _ in range(pieces)]
    downs = [rest.pop(0) for _ in range(pieces)]
    weight_grad_ref, up_shift_grad_ref, middle_grad_ref, small_ref = rest[:4]
    (
        normed_t,
        grad_t,
        normed_grad,
        up_weight,
        down_weight,
        active,
        slope,
        low_grad,
        sent,
        came,
        sems,
        send_sems,
        recv_sems,
    ) = rest[4:]
    step = pl.program_id(0)
    rows_all, width = grad_ref.shape
    size = up_weight.shape[2]
    blocks = blocks_of(grad_ref)
    other = greet_core(step)
    copies = []
    for slot, i in enumerate(ORDER):
        own = pl.ds(columns[i] * size, size)
        at = slot % 2
        copies.append(
            [
                pltpu.make_async_copy(downs[i], down_weight.at[at], sems.at[0, at]),
                pltpu.make_async_copy(slopes[i].at[:, own], slope.at[at], sems.at[1, at]),
                pltpu.make_async_copy(ups[i], up_weight.at[at], sems.at[2, at]),
                pltpu.make_async_copy(actives[i].at[:, own], active.at[at], sems.at[3, at]),
            ]
        )

    @pl.when(step == 0)
    def _():
        run_copies(copies[0])

        def prepare(i, carry):
            rows = block_at(i)
            scaled, _ = normalise(middle_ref[rows, :])
            normed = (scaled * norm_ref[0:1, :] + norm_ref[1:2, :]).astype(BF16)
            normed_t[:, rows] = normed.T
            grad_t[:, rows] = grad_ref[rows, :].T
            return carry

        lax.fori_loop(0, blocks, prepare, 0)

    for index in range(pieces):

        @pl.when(step == index)
        def _():
            at = index % 2
            wait_copies(copies[index])
            if index + 1 < pieces:
                run_copies(copies[index + 1])
            shift_grad = jnp.zeros((1, size), F32)
            for rows in big_blocks(rows_all):
                hidden_grad = nt(grad_ref[rows, :], down_weight[at]) * slope[at, rows, :].astype(F32)
                low = hidden_grad.astype(BF16)
                low_grad[rows, :] = low
                shift_grad = shift_grad + jnp.sum(hidden_grad, axis=0, keepdims=True)
                term = nt(low, up_weight[at])
                normed_grad[rows, :] = term if index == 0 else normed_grad[rows, :] + term
            up_shift_grad_ref[0] = shift_grad

            def grad_of(put):
                for rows in big_blocks(width):
                    put((0, rows, slice(None)), nn(normed_t[rows, :], low_grad[...]))
                    put((1, rows, slice(None)), nn(grad_t[rows, :], active[at]))

            sum_with_core(step, other, index, grad_of, sent, came, weight_grad_ref, send_sems, recv_sems)

    @pl.when(step == pieces - 1)
    def _():
        def finish(i, sums):
            rows = block_at(i)
            scaled, inverse = normalise(middle_ref[rows, :])
            gradient = normed_grad[rows, :]
            upper = grad_ref[rows, :].astype(F32)
            middle_grad = upper + normalise_back(gradient, scaled, inverse, norm_ref[0:1, :])
            middle_grad_ref[rows, :] = middle_grad
            terms = (gradient * scaled, gradient, middle_grad, upper)
            return tuple(old + jnp.sum(term, axis=0, keepdims=True) for old, term in zip(sums, terms))

        zero = jnp.zeros((1, width), F32)
        sums = lax.fori_loop(0, blocks, finish, (zero, zero, zero, zero))
        for index, row in enumerate(sums):
            small_ref[index : index + 1, :] = row


def tensor_slot(step):
    return lax.max(step - 2, 0)


def feed_backward(grad, middle, norm, actives, slopes, columns, ups, downs, collective):
    rows, width = middle.shape
    pieces = len(ups)
    size = ups[0].shape[1]
    operands = [*actives, *slopes, *ups, *downs]
    return pl.pallas_call(
        functools.partial(feed_backward_kernel, columns=columns),
        grid=(pieces,),
        in_specs=[once((rows, width)), once((rows, width)), once((2, width))] + anywhere(len(operands)),
        out_specs=[
            pl.BlockSpec((1, 2, width, size), lambda i: (tensor_slot(i), 0, 0, 0)),
            pl.BlockSpec((1, 1, size), lambda i: (i, 0, 0)),
            once((rows, width)),
            once((4, width)),
        ],
        scratch_shapes=[
            pltpu.VMEM((width, rows), BF16),
            pltpu.VMEM((width, rows), BF16),
            pltpu.VMEM((rows, width), F32),
            pltpu.VMEM((2, width, size), BF16),
            pltpu.VMEM((2, size, width), BF16),
            pltpu.VMEM((2, rows, size), BF16),
            pltpu.VMEM((2, rows, size), BF16),
            pltpu.VMEM((rows, size), BF16),
            pltpu.VMEM((2, 2, width, size), BF16),
            pltpu.VMEM((2, 2, width, size), BF16),
            pltpu.SemaphoreType.DMA((4, 2)),
            pltpu.SemaphoreType.DMA((2,)),
            pltpu.SemaphoreType.DMA((2,)),
        ],
        out_shape=[
            jax.ShapeDtypeStruct((2, 2, width, size), BF16),
            jax.ShapeDtypeStruct((pieces, 1, size), F32),
            jax.ShapeDtypeStruct((rows, width), F32),
            jax.ShapeDtypeStruct((4, width), F32),
        ],
        name="feed_backward",
        **settings(16_000_000_000, collective),
    )(grad, middle, norm, *operands)


def mixer_backward_kernel(
    start_ref, tiles_ref, seg_ref, middle_grad_ref, qkv_ref_all, *rest, saved, heads
):
    pieces = len(saved)
    rest = [qkv_ref_all] + list(rest)
    qkvs = [rest.pop(0) for _ in range(pieces)]
    mixeds = [rest.pop(0) for _ in range(pieces)]
    log_totals = [rest.pop(0) for _ in range(pieces)]
    weights = [rest.pop(0) for _ in range(pieces)]
    projected_ref, qkv_shift_grad_ref = rest[:2]
    qkv, mixed, totals, out_weight, low_middle, mixed_grad, sums, sems = rest[2:]
    step = pl.program_id(0)
    cols = heads * HEAD_DIM
    copies = []
    for i in range(pieces):
        at = saved[i]
        copies.append(
            [
                pltpu.make_async_copy(weights[i].at[3 * cols : 4 * cols], out_weight.at[i], sems.at[0, i]),
                pltpu.make_async_copy(qkvs[i].at[at], qkv.at[i], sems.at[1, i]),
                pltpu.make_async_copy(mixeds[i].at[at], mixed.at[i], sems.at[2, i]),
                pltpu.make_async_copy(
                    log_totals[i].at[at * heads : (at + 1) * heads], totals.at[i], sems.at[3, i]
                ),
            ]
        )

    @pl.when(step == 0)
    def _():
        for group in copies:
            run_copies(group)
        low_middle[...] = middle_grad_ref[...].astype(BF16)

    for index in range(pieces):

        @pl.when(step == index)
        def _():
            wait_copies(copies[index])

    mixed_grad[...] = nt(out_weight[step], low_middle[...]).astype(BF16)
    sums[...] = jnp.zeros_like(sums)
    each_image(
        start_ref,
        tiles_ref,
        lambda index, at, span: attend_backward_image(
            index, at, span, heads, seg_ref, qkv.at[step], mixed.at[step], totals.at[step], mixed_grad, sums
        ),
    )
    gradient = sums[...]
    projected_ref[0] = gradient.astype(BF16)
    qkv_shift_grad_ref[0] = jnp.sum(gradient, axis=1, keepdims=True)


def mixer_backward(images, middle_grad, qkvs, mixeds, log_totals, saved, weights):
    rows, width = middle_grad.shape
    count = len(weights)
    cols = width // 4
    heads = cols // HEAD_DIM
    place, start, tiles, segment = images
    operands = [*qkvs, *mixeds, *log_totals, *weights]
    return pl.pallas_call(
        functools.partial(mixer_backward_kernel, saved=saved, heads=heads),
        grid_spec=pltpu.PrefetchScalarGridSpec(
            num_scalar_prefetch=2,
            grid=(count,),
            in_specs=[once((1, rows)), once((rows, width))] + anywhere(len(operands)),
            out_specs=[
                pl.BlockSpec((1, 3 * cols, rows), lambda i, *_: (i, 0, 0)),
                pl.BlockSpec((1, 3 * cols, 1), lambda i, *_: (i, 0, 0)),
            ],
            scratch_shapes=[
                pltpu.VMEM((count, 3 * cols, rows), BF16),
                pltpu.VMEM((count, cols, rows), BF16),
                pltpu.VMEM((count, heads, 1, rows), F32),
                pltpu.VMEM((count, cols, width), BF16),
                pltpu.VMEM((rows, width), BF16),
                pltpu.VMEM((cols, rows), BF16),
                pltpu.VMEM((3 * cols, rows), F32),
                pltpu.SemaphoreType.DMA((4, count)),
            ],
        ),
        out_shape=[
            jax.ShapeDtypeStruct((count, 3 * cols, rows), BF16),
            jax.ShapeDtypeStruct((count, 3 * cols, 1), F32),
        ],
        name="mixer_backward",
        **settings(16_000_000_000),
    )(start, tiles, segment, middle_grad, *operands)


def input_backward_kernel(hidden_ref, middle_grad_ref, norm_ref, projected, normed_in, *rest, saved):
    pieces = len(saved)
    rest = list(rest)
    mixeds = [rest.pop(0) for _ in range(pieces)]
    weights = [rest.pop(0) for _ in range(pieces)]
    weight_grad_ref, in_grad_ref, small_ref = rest[:3]
    projected_grad, mixed, normed, low_middle, weight, sent, came, sems, send_sems, recv_sems = rest[3:]
    step = pl.program_id(0)
    rows_all, width = hidden_ref.shape
    count = projected.shape[1]
    other = greet_core(step)
    copies = []
    for i in range(pieces):
        copies.append(
            [
                pltpu.make_async_copy(
                    projected.at[i], projected_grad.at[i * count : (i + 1) * count], sems.at[0, i]
                ),
                pltpu.make_async_copy(mixeds[i].at[saved[i]], mixed.at[i], sems.at[1, i]),
                pltpu.make_async_copy(
                    weights[i].at[0:count], weight.at[i * count : (i + 1) * count], sems.at[2, i]
                ),
            ]
        )
    norm_copy = pltpu.make_async_copy(normed_in, normed, sems.at[3, 0])

    @pl.when(step == 0)
    def _():
        norm_copy.start()
        for i in ORDER:
            run_copies(copies[i])
        low_middle[...] = middle_grad_ref[...].astype(BF16)
        norm_copy.wait()

    for index, piece in enumerate(ORDER):

        @pl.when(step == index)
        def _():
            wait_copies(copies[piece])

            def grad_of(put):
                own = slice(piece * count, (piece + 1) * count)
                put((slice(0, count), slice(None)), nn(projected_grad[own, :], normed[...]))
                put((slice(count, width), slice(None)), nn(mixed[piece], low_middle[...]))

            sum_with_core(step, other, index, grad_of, sent, came, weight_grad_ref, send_sems, recv_sems)

    @pl.when(step == pieces - 1)
    def _():
        total = jnp.zeros((1, width), F32)
        shift = jnp.zeros((1, width), F32)
        for rows in big_blocks(rows_all):
            scaled, inverse = normalise(hidden_ref[rows, :].astype(F32))
            gradient = tn(projected_grad[:, rows], weight[...])
            in_grad = middle_grad_ref[rows, :] + normalise_back(gradient, scaled, inverse, norm_ref[0:1, :])
            in_grad_ref[rows, :] = in_grad.astype(BF16)
            total = total + jnp.sum(gradient * scaled, axis=0, keepdims=True)
            shift = shift + jnp.sum(gradient, axis=0, keepdims=True)
        small_ref[0:1, :] = total
        small_ref[1:2, :] = shift


def input_backward(hidden, middle_grad, norm, projected, normed, mixeds, saved, weights, collective):
    rows, width = hidden.shape
    number, count, _ = projected.shape
    operands = [projected, normed, *mixeds, *weights]
    return pl.pallas_call(
        functools.partial(input_backward_kernel, saved=saved),
        grid=(number,),
        in_specs=[once((rows, width)), once((rows, width)), once((2, width))] + anywhere(len(operands)),
        out_specs=[
            pl.BlockSpec((1, width, width), lambda i: (tensor_slot(i), 0, 0)),
            once((rows, width)),
            once((2, width)),
        ],
        scratch_shapes=[
            pltpu.VMEM((number * count, rows), BF16),
            pltpu.VMEM((number, width - count, rows), BF16),
            pltpu.VMEM((rows, width), BF16),
            pltpu.VMEM((rows, width), BF16),
            pltpu.VMEM((number * count, width), BF16),
            pltpu.VMEM((2, width, width), BF16),
            pltpu.VMEM((2, width, width), BF16),
            pltpu.SemaphoreType.DMA((4, number)),
            pltpu.SemaphoreType.DMA((2,)),
            pltpu.SemaphoreType.DMA((2,)),
        ],
        out_shape=[
            jax.ShapeDtypeStruct((2, width, width), BF16),
            jax.ShapeDtypeStruct((rows, width), BF16),
            jax.ShapeDtypeStruct((2, width), F32),
        ],
        name="input_backward",
        **settings(8_000_000_000, collective),
    )(hidden, middle_grad, norm, *operands)


def unpack_kernel(feed_ref, mixer_ref, qkv_ref, out_ref, up_ref, down_ref):
    width = feed_ref.shape[2]
    part = width // 4
    for core in range(2):
        up_ref[:, core * width : (core + 1) * width] = feed_ref[core, 0].astype(F32)
        down_ref[core * width : (core + 1) * width, :] = feed_ref[core, 1].astype(F32).T
        out_ref[core * part : (core + 1) * part, :] = mixer_ref[core, 3 * part :, :].astype(F32)
    for third in range(3):
        rows = slice(third * part, (third + 1) * part)
        both = jnp.concatenate([mixer_ref[0, rows, :], mixer_ref[1, rows, :]], axis=0)
        qkv_ref[third] = both.astype(F32).T


def unpack(feed, mixer):
    width = feed.shape[2]
    half = width // 2
    return pl.pallas_call(
        unpack_kernel,
        out_shape=[
            jax.ShapeDtypeStruct((3, width, half), F32),
            jax.ShapeDtypeStruct((half, width), F32),
            jax.ShapeDtypeStruct((width, 2 * width), F32),
            jax.ShapeDtypeStruct((2 * width, width), F32),
        ],
        name="unpack",
        compiler_params=pltpu.CompilerParams(vmem_limit_bytes=VMEM_LIMIT),
    )(feed, mixer)


def route(change):
    shape = [lax.axis_size(axis) for axis in AXES]
    pairs = []
    for s in range(shape[0]):
        for d in range(shape[1]):
            for t in range(shape[2]):
                to = change(s, d, t)
                if to is not None:
                    pairs.append(((s * shape[1] + d) * shape[2] + t, (to[0] * shape[1] + to[1]) * shape[2] + to[2]))
    return pairs


def moved(block, change):
    return lax.ppermute(block, AXES, route(change))


def over_tensor(s, d, t):
    return (s, d, 1 - t)


def over_section(s, d, t):
    return (1 - s, d, t)


def over_both(s, d, t):
    return (1 - s, d, 1 - t)


def over_core(s, d, t):
    return (s, d ^ 1, t)


def along_z(distance):
    count = lax.axis_size("dp") // 2
    return lambda s, d, t: (s, (d // 2 + distance) % count * 2 + d % 2, t)


def tie(*values):
    return lax.optimization_barrier(values)


def take_part(block, which, count, axis=0):
    size = block.shape[axis] // count
    return lax.dynamic_slice_in_dim(block, which * size, size, axis)


def added(*terms):
    total = terms[0].astype(F32)
    for term in terms[1:]:
        total = total + term.astype(F32)
    return total.astype(terms[0].dtype)


def send_plane(sums, section):
    return [
        moved(take_part(sums[1], section, 2), over_tensor),
        moved(take_part(sums[0], 1 - section, 2), over_section),
        moved(take_part(sums[1], 1 - section, 2), over_both),
    ]


def send_line(part, z_index):
    count = lax.axis_size("dp") // 2
    return [moved(take_part(part, (z_index + step) % count, count), along_z(step)) for step in range(1, count)]


def reordered(pieces, lane, core):
    pieces = jnp.where(lane == 0, pieces, pieces[jnp.array([2, 3, 0, 1])])
    return jnp.where(core == 0, pieces, pieces[jnp.array([1, 0, 3, 2])])


def one_sequence_each(
    inputs,
    cotangent,
    segment_ids,
    norm_gains,
    norm_biases,
    qkv_weight,
    qv_bias,
    out_weight,
    up_weight,
    up_bias,
    down_weight,
    out_biases,
):
    section = lax.axis_index("section")
    group = lax.axis_index("dp")
    lane = lax.axis_index("tensor")
    core = group % 2
    z_index = group // 2
    z_count = lax.axis_size("dp") // 2
    width = inputs.shape[2]
    hidden = up_bias.shape[1]
    cols = qkv_weight.shape[3]
    part = cols // 2
    mine = 2 * section + lane

    def own_half(array, axis):
        return take_part(array, core, 2, axis)

    mixer_own = jnp.concatenate(
        [
            own_half(qkv_weight[0], 2).transpose(0, 2, 1).reshape(3 * part, width),
            own_half(out_weight[0], 0),
        ],
        axis=0,
    )
    up_own = own_half(up_weight[0], 1)
    down_own = own_half(down_weight[0], 0)
    small = jnp.concatenate(
        [item.reshape(-1) for item in (norm_gains, norm_biases, qv_bias, up_bias, out_biases)]
    )

    def sequence_halves(array):
        kept = lax.dynamic_index_in_dim(array, mine, 0, keepdims=False)
        sent = lax.dynamic_index_in_dim(array, 2 * section + 1 - lane, 0, keepdims=False)
        return kept, sent

    def joined(kept, came):
        return jnp.where(lane == 0, jnp.concatenate([kept, came], 0), jnp.concatenate([came, kept], 0))

    segment = lax.dynamic_index_in_dim(segment_ids, mine, 0, keepdims=True)
    ids = jnp.arange(IMAGE_IDS, dtype=jnp.int32)[:, None]
    begin = jnp.sum((segment < ids).astype(jnp.int32), axis=1)
    end = jnp.sum((segment <= ids).astype(jnp.int32), axis=1)
    start = begin // TILE
    place = jnp.stack([lane, core]).astype(jnp.int32)
    images = (place, start, (end - 1) // TILE - start + 1, segment)

    def params(vector):
        gains = vector[: 2 * width].reshape(2, width)
        shifts = vector[2 * width : 4 * width].reshape(2, width)
        qv = vector[4 * width : 6 * width].reshape(2, 4, part)
        up_shift = vector[6 * width : 6 * width + hidden].reshape(4, 1, hidden // 4)
        outs = vector[6 * width + hidden :].reshape(2, 1, width)
        zero = jnp.zeros((4, part), F32)
        qkv_shift = jnp.concatenate([qv[0], zero, qv[1]], axis=1)
        norms = [jnp.stack([gains[i], shifts[i]]) for i in range(2)]
        return norms, qkv_shift[:, :, None], up_shift, outs

    def by_layer(own, came):
        return jnp.where(section == 0, own, came), jnp.where(section == 1, own, came)

    kept, sent = sequence_halves(inputs)
    came, mixer_came, small_came = tie(
        moved(sent, over_tensor), moved(mixer_own, over_section), moved(small, over_section)
    )
    state = joined(kept, came)
    mixers = by_layer(mixer_own, mixer_came)
    layer_params = [params(vector) for vector in by_layer(small, small_came)]
    mixer_pieces = [[mixers[0], moved(mixers[0], over_core)], None]
    norms, qkv_shift, up_shift, outs = layer_params[0]
    mixer_a, beside, up_came = tie(
        mixer_forward(images, state, norms[0], qkv_shift, mixer_pieces[0]),
        moved(mixers[0], over_tensor),
        moved(up_own, over_section),
    )
    ups = by_layer(up_own, up_came)
    mixer_pieces[0] = mixer_pieces[0] + [beside, moved(beside, over_core)]
    mixer_b, up_beside, up_twin, down_came = tie(
        mixer_forward(
            images,
            state,
            norms[0],
            qkv_shift,
            mixer_pieces[0][2:],
            2,
            (mixer_a[3], mixer_a[1]),
            mixer_pieces[0],
            outs[0],
        ),
        moved(ups[0], over_tensor),
        moved(ups[0], over_core),
        moved(down_own, over_section),
    )
    downs = by_layer(down_own, down_came)
    down_twin = moved(downs[0], over_core)
    feed_a, down_beside, up_corner = tie(
        feed_forward(
            place, mixer_b[3], norms[1], up_shift, outs[1], [ups[0], up_twin], [downs[0], down_twin], 0, False
        ),
        moved(downs[0], over_tensor),
        moved(up_beside, over_core),
    )
    up_pieces = [[ups[0], up_twin, up_beside, up_corner], None]
    down_pieces = [[downs[0], down_twin, down_beside, moved(down_beside, over_core)], None]
    feed_b, beside, twin = tie(
        feed_forward(
            place, mixer_b[3], norms[1], up_shift, feed_a[0], up_pieces[0][2:], down_pieces[0][2:], 2, True
        ),
        moved(mixers[1], over_tensor),
        moved(mixers[1], over_core),
    )
    first_out = feed_b[0]
    saved = [
        dict(
            state=state,
            normed=mixer_a[3],
            qkv=[mixer_a[0], mixer_a[0], mixer_b[0], mixer_b[0]],
            mixed=[mixer_a[1], mixer_a[1], mixer_b[1], mixer_b[1]],
            totals=[mixer_a[2], mixer_a[2], mixer_b[2], mixer_b[2]],
            at=[0, 1, 0, 1],
            middle=mixer_b[3],
            active=[feed_a[1], feed_a[1], feed_b[1], feed_b[1]],
            slope=[feed_a[2], feed_a[2], feed_b[2], feed_b[2]],
        )
    ]
    norms, qkv_shift, up_shift, outs = layer_params[1]
    mixer_pieces[1] = [mixers[1], twin, beside, moved(beside, over_core)]
    mixer_a, up_beside, up_twin, down_beside, down_twin = tie(
        mixer_forward(images, first_out, norms[0], qkv_shift, mixer_pieces[1], 0, None, mixer_pieces[1], outs[0]),
        moved(ups[1], over_tensor),
        moved(ups[1], over_core),
        moved(downs[1], over_tensor),
        moved(downs[1], over_core),
    )
    up_pieces[1] = [ups[1], up_twin, up_beside, moved(up_beside, over_core)]
    down_pieces[1] = [downs[1], down_twin, down_beside, moved(down_beside, over_core)]
    grad_kept, grad_sent = sequence_halves(cotangent)
    feed_a, grad_came = tie(
        feed_forward(place, mixer_a[4], norms[1], up_shift, outs[1], up_pieces[1], down_pieces[1], 0, True),
        moved(grad_sent, over_tensor),
    )
    second_out = feed_a[0]
    saved.append(
        dict(
            state=first_out,
            normed=mixer_a[3],
            qkv=[mixer_a[0]] * 4,
            mixed=[mixer_a[1]] * 4,
            totals=[mixer_a[2]] * 4,
            at=[0, 1, 2, 3],
            middle=mixer_a[4],
            active=[feed_a[1]] * 4,
            slope=[feed_a[2]] * 4,
        )
    )
    grad = joined(grad_kept, grad_came)

    def exchange(own, other):
        return [
            take_part(own, lane, 2),
            moved(take_part(own, 1 - lane, 2), over_tensor),
            moved(take_part(other, lane, 2), over_section),
            moved(take_part(other, 1 - lane, 2), over_both),
        ]

    def ordered(relative):
        relative = jnp.stack(relative)
        relative = jnp.where(lane == 0, relative, relative[jnp.array([1, 0, 3, 2])])
        return jnp.where(section == 0, relative, relative[jnp.array([2, 3, 0, 1])])

    out_parts = exchange(
        jnp.where(section == 0, first_out, second_out), jnp.where(section == 0, second_out, first_out)
    )

    def feed_back(layer, grad):
        kept = saved[layer]
        return feed_backward(
            grad,
            kept["middle"],
            layer_params[layer][0][1],
            kept["active"],
            kept["slope"],
            kept["at"],
            up_pieces[layer],
            down_pieces[layer],
            layer,
        )

    def mixer_back(layer, middle_grad):
        kept = saved[layer]
        return mixer_backward(
            images, middle_grad, kept["qkv"], kept["mixed"], kept["totals"], kept["at"], mixer_pieces[layer]
        )

    def input_back(layer, middle_grad, projected):
        kept = saved[layer]
        return input_backward(
            kept["state"],
            middle_grad,
            layer_params[layer][0][0],
            projected,
            kept["normed"],
            kept["mixed"],
            kept["at"],
            mixer_pieces[layer],
            2 + layer,
        )

    def small_vector(feed, mixer, in_small):
        shifts = reordered(mixer[1].reshape(4, 3, part), lane, core)
        ups = reordered(feed[1].reshape(4, -1)[jnp.array([2, 0, 3, 1])], lane, core)
        return jnp.concatenate(
            [
                in_small[0],
                feed[3][0],
                in_small[1],
                feed[3][1],
                shifts[:, 0].reshape(-1),
                shifts[:, 2].reshape(-1),
                ups.reshape(-1),
                feed[3][2],
                feed[3][3],
            ]
        ).reshape(-1, TILE)

    def plane_sum(sums, came):
        return added(take_part(sums[0], section, 2), *came)

    def line_sum(block, came):
        return added(take_part(block, z_index, z_count), *came)

    feed1, out_parts = tie(feed_back(1, grad), out_parts)
    feed_sums1 = feed1[0].reshape(2, -1, width)
    mixer1, came = tie(mixer_back(1, feed1[2]), send_plane(feed_sums1, section))
    feed_part1 = plane_sum(feed_sums1, came)
    input1 = input_back(1, feed1[2], mixer1[0])
    in_grad1 = input1[1]
    feed0, came, came_line = tie(
        feed_back(0, in_grad1), send_plane(input1[0], section), send_line(feed_part1, z_index)
    )
    mixer_part1 = plane_sum(input1[0], came)
    feed_total1 = line_sum(feed_part1, came_line)
    feed_sums0 = feed0[0].reshape(2, -1, width)
    mixer0, came, came_line = tie(
        mixer_back(0, feed0[2]), send_plane(feed_sums0, section), send_line(mixer_part1, z_index)
    )
    feed_part0 = plane_sum(feed_sums0, came)
    mixer_total1 = line_sum(mixer_part1, came_line)
    input0, came_line = tie(input_back(0, feed0[2], mixer0[0]), send_line(feed_part0, z_index))
    feed_total0 = line_sum(feed_part0, came_line)
    mixer_part0 = plane_sum(input0[0], send_plane(input0[0], section))
    mixer_total0 = line_sum(mixer_part0, send_line(mixer_part0, z_index))
    in_parts = exchange(
        jnp.where(section == 0, input0[1], in_grad1), jnp.where(section == 0, in_grad1, input0[1])
    )
    vector = jnp.stack([small_vector(feed0, mixer0, input0[2]), small_vector(feed1, mixer1, input1[2])])
    vector = vector + moved(vector, over_core)
    vector = added(vector, *[moved(vector, along_z(step)) for step in range(1, z_count)])
    vector = added(vector, *[moved(vector, change) for change in (over_tensor, over_section, over_both)])
    vector = jnp.where(section == 0, vector[0], vector[1]).reshape(-1)

    def whole(total0, total1):
        own = jnp.where(section == 0, total0, total1)
        came = moved(jnp.where(section == 0, total1, total0), over_section)
        both = jnp.where(section == 0, jnp.stack([own, came]), jnp.stack([came, own]))
        parts = [both] + [moved(both, along_z(step)) for step in range(1, z_count)]
        order = (z_index - jnp.arange(z_count)) % z_count
        line = jnp.stack(parts)[order].transpose(1, 0, 2, 3).reshape(2, -1, width)
        twin = moved(line, over_core)
        return jnp.where(core == 0, jnp.stack([line, twin]), jnp.stack([twin, line]))

    feed_sum = whole(feed_total0, feed_total1)
    mixer_sum = whole(mixer_total0, mixer_total1).reshape(2, 4 * part, width)
    qkv_grad, out_grad, up_grad, down_grad = unpack(feed_sum, mixer_sum)
    states = ordered(out_parts)
    grads = ordered(in_parts).astype(F32)
    return (
        states[None],
        grads[None],
        vector[: 2 * width].reshape(1, 2, width),
        vector[2 * width : 4 * width].reshape(1, 2, width),
        qkv_grad[None],
        vector[4 * width : 6 * width].reshape(1, 2, width),
        out_grad[None],
        up_grad[None],
        vector[6 * width : 6 * width + hidden].reshape(1, hidden),
        down_grad[None],
        vector[6 * width + hidden :].reshape(1, 2, width),
    )


def passed_along(block, axis, distance):
    devices = range(lax.axis_size(axis))
    route = [(i - distance, i) for i in devices if i - distance in devices]
    return lax.ppermute(block, axis, route)


def norm_parts(token_rows, gain_row, shift_row):
    centre = token_rows - jnp.mean(token_rows, axis=-1, keepdims=True)
    inverse = lax.rsqrt(jnp.mean(centre * centre, axis=-1, keepdims=True) + EPSILON)
    scaled = centre * inverse
    return (scaled * gain_row + shift_row, scaled, inverse)


def norm_back(gradient, scaled, inverse, gain_row):
    upstream = gradient * gain_row
    return inverse * (
        upstream
        - jnp.mean(upstream, axis=-1, keepdims=True)
        - scaled * jnp.mean(upstream * scaled, axis=-1, keepdims=True)
    )


def gelu_exact(values):
    return jax.nn.gelu(values, approximate=False)


def head_view(matrix, heads_local):
    return matrix.reshape(matrix.shape[0], heads_local, HEAD_DIM)


def join_heads(stacked):
    return stacked.transpose(1, 0, 2).reshape(stacked.shape[1], stacked.shape[0] * stacked.shape[2])


def attend_forward(queries, key_rows, value_rows, segment):
    seq_len = queries.shape[0]
    half_rows = seq_len // 2
    heads_local = queries.shape[1] // HEAD_DIM
    scaling = HEAD_DIM ** (-0.5)
    query_heads = head_view(queries, heads_local)
    key_heads = head_view(key_rows, heads_local)
    value_heads = head_view(value_rows, heads_local)

    def one_item(item):
        head_index = item // 2
        row_start = item % 2 * half_rows
        head_keys = lax.dynamic_index_in_dim(key_heads, head_index, 1, keepdims=False)
        head_values = lax.dynamic_index_in_dim(value_heads, head_index, 1, keepdims=False)
        head_queries = lax.dynamic_index_in_dim(query_heads, head_index, 1, keepdims=False)
        block_queries = lax.dynamic_slice_in_dim(head_queries, row_start, half_rows, 0)
        block_segment = lax.dynamic_slice_in_dim(segment, row_start, half_rows, 0)
        scores = (
            jnp.einsum("qd,kd->qk", block_queries, head_keys, preferred_element_type=jnp.float32)
            * scaling
        )
        scores = jnp.where(block_segment[:, None] == segment[None, :], scores, NEGATIVE)
        row_peak = jnp.max(scores, axis=-1, keepdims=True)
        expanded = jnp.exp(scores - row_peak)
        denominator = jnp.sum(expanded, axis=-1, keepdims=True)
        weights = (expanded / denominator).astype(jnp.bfloat16)
        block_out = jnp.dot(weights, head_values, preferred_element_type=jnp.float32).astype(
            jnp.bfloat16
        )
        return (block_out, row_peak[:, 0] + jnp.log(denominator[:, 0]))

    outputs, log_totals = lax.map(one_item, jnp.arange(2 * heads_local, dtype=jnp.int32))
    mixed_rows = join_heads(outputs.reshape(heads_local, seq_len, HEAD_DIM))
    return (mixed_rows, log_totals.reshape(heads_local, seq_len))


def attend_backward(queries, key_rows, value_rows, mixed_grad, log_totals, segment):
    seq_len = queries.shape[0]
    half_rows = seq_len // 2
    heads_local = queries.shape[1] // HEAD_DIM
    scaling = HEAD_DIM ** (-0.5)
    query_heads = head_view(queries, heads_local)
    key_heads = head_view(key_rows, heads_local)
    value_heads = head_view(value_rows, heads_local)
    grad_heads = head_view(mixed_grad, heads_local)

    def one_head(head_index):
        head_queries = lax.dynamic_index_in_dim(query_heads, head_index, 1, keepdims=False)
        head_keys = lax.dynamic_index_in_dim(key_heads, head_index, 1, keepdims=False)
        head_values = lax.dynamic_index_in_dim(value_heads, head_index, 1, keepdims=False)
        head_grads = lax.dynamic_index_in_dim(grad_heads, head_index, 1, keepdims=False)
        head_totals = lax.dynamic_index_in_dim(log_totals, head_index, 0, keepdims=False)

        def one_block(carry, block_index):
            key_grad, value_grad = carry
            row_start = block_index * half_rows
            block_queries = lax.dynamic_slice_in_dim(head_queries, row_start, half_rows, 0)
            block_grads = lax.dynamic_slice_in_dim(head_grads, row_start, half_rows, 0)
            block_totals = lax.dynamic_slice_in_dim(head_totals, row_start, half_rows, 0)
            block_segment = lax.dynamic_slice_in_dim(segment, row_start, half_rows, 0)
            scores = (
                jnp.einsum(
                    "qd,kd->qk", block_queries, head_keys, preferred_element_type=jnp.float32
                )
                * scaling
            )
            scores = jnp.where(block_segment[:, None] == segment[None, :], scores, NEGATIVE)
            weights = jnp.exp(scores - block_totals[:, None])
            low_weights = weights.astype(jnp.bfloat16)
            block_out = jnp.dot(
                low_weights, head_values, preferred_element_type=jnp.float32
            ).astype(jnp.bfloat16)
            weight_grads = jnp.einsum(
                "qd,kd->qk", block_grads, head_values, preferred_element_type=jnp.float32
            )
            row_terms = jnp.sum(weights * weight_grads, axis=-1, keepdims=True)
            score_grads = (weights * (weight_grads - row_terms)).astype(jnp.bfloat16)
            query_grad = (
                jnp.dot(score_grads, head_keys, preferred_element_type=jnp.float32) * scaling
            )
            key_grad = (
                key_grad
                + jnp.einsum(
                    "qk,qd->kd", score_grads, block_queries, preferred_element_type=jnp.float32
                )
                * scaling
            )
            value_grad = value_grad + jnp.einsum(
                "qk,qd->kd", low_weights, block_grads, preferred_element_type=jnp.float32
            )
            return ((key_grad, value_grad), (block_out, query_grad))

        empty = jnp.zeros((seq_len, HEAD_DIM), jnp.float32)
        (key_grad, value_grad), (block_outs, query_grads) = lax.scan(
            one_block, (empty, empty), jnp.arange(2, dtype=jnp.int32)
        )
        return (
            block_outs.reshape(seq_len, HEAD_DIM),
            query_grads.reshape(seq_len, HEAD_DIM),
            key_grad,
            value_grad,
        )

    results = lax.map(one_head, jnp.arange(heads_local, dtype=jnp.int32))
    return tuple((join_heads(item) for item in results))


def store_at(array, value, which, running):
    return array.at[which].set(jnp.where(running, value, array[which]))


def pipelined(
    inputs,
    cotangent,
    segment_ids,
    norm_gains,
    norm_biases,
    qkv_weight,
    qv_bias,
    out_weight,
    up_weight,
    up_bias,
    down_weight,
    out_biases,
):
    section_index = lax.axis_index("section")
    section_count = lax.axis_size("section")
    lane_index = lax.axis_index("tensor")
    micro_count, own_rows, model_width = inputs.shape
    seq_len = segment_ids.shape[1]
    cols_local = qkv_weight.shape[3]
    hidden_local = up_weight.shape[2]
    heads_local = cols_local // HEAD_DIM
    gain_rows = norm_gains[0]
    shift_rows = norm_biases[0]
    joined = jnp.concatenate([qkv_weight[0, 0], qkv_weight[0, 1], qkv_weight[0, 2]], axis=1)
    query_shift = lax.dynamic_slice_in_dim(qv_bias[0, 0], lane_index * cols_local, cols_local)
    value_shift = lax.dynamic_slice_in_dim(qv_bias[0, 1], lane_index * cols_local, cols_local)
    up_shift = lax.dynamic_slice_in_dim(up_bias[0], lane_index * hidden_local, hidden_local)
    out_matrix = out_weight[0]
    up_matrix = up_weight[0]
    down_matrix = down_weight[0]
    mixer_shift = out_biases[0, 0]
    feed_shift = out_biases[0, 1]

    def spread_rows(normed_rows, weight):
        return (
            None,
            jnp.dot(
                lax.all_gather(normed_rows, "tensor", axis=0, tiled=True),
                weight,
                preferred_element_type=jnp.float32,
            ),
        )

    def regather(normed_rows):
        return lax.all_gather(normed_rows, "tensor", axis=0, tiled=True)

    def gather_grads(grad_rows):
        return lax.all_gather(grad_rows.astype(jnp.bfloat16), "tensor", axis=0, tiled=True)

    def branch_sum(left_rows, weight):
        return lax.psum_scatter(
            jnp.dot(left_rows, weight, preferred_element_type=jnp.float32).astype(jnp.bfloat16),
            "tensor",
            scatter_dimension=0,
            tiled=True,
        ).astype(jnp.float32)

    def input_sum(grad_rows, weight):
        return lax.psum_scatter(
            jnp.einsum("sc,dc->sd", grad_rows, weight, preferred_element_type=jnp.float32).astype(
                jnp.bfloat16
            ),
            "tensor",
            scatter_dimension=0,
            tiled=True,
        ).astype(jnp.float32)

    def split_projected(projected):
        queries = (projected[:, :cols_local] + query_shift).astype(jnp.bfloat16)
        key_rows = projected[:, cols_local : 2 * cols_local].astype(jnp.bfloat16)
        value_rows = (projected[:, 2 * cols_local :] + value_shift).astype(jnp.bfloat16)
        return (queries, key_rows, value_rows)

    def layer_backward(block_in, middle, log_totals, segment, out_grad):
        residual = block_in.astype(jnp.float32)
        full_grad = gather_grads(out_grad)
        normed_two, scaled_two, inverse_two = norm_parts(middle, gain_rows[1], shift_rows[1])
        normed_two = normed_two.astype(jnp.bfloat16)
        full_two = regather(normed_two)
        hidden = jnp.dot(full_two, up_matrix, preferred_element_type=jnp.float32) + up_shift
        active, gelu_pullback = jax.vjp(gelu_exact, hidden)
        active = active.astype(jnp.bfloat16)
        down_grad = jnp.einsum("sf,sd->fd", active, full_grad, preferred_element_type=jnp.float32)
        active_grad = jnp.einsum(
            "sd,fd->sf", full_grad, down_matrix, preferred_element_type=jnp.float32
        )
        hidden_grad = gelu_pullback(active_grad)[0]
        up_shift_grad = jnp.sum(hidden_grad, axis=0)
        hidden_low = hidden_grad.astype(jnp.bfloat16)
        up_grad = jnp.einsum("sd,sf->df", full_two, hidden_low, preferred_element_type=jnp.float32)
        normed_grad_two = input_sum(hidden_low, up_matrix)
        feed_shift_grad = jnp.sum(out_grad, axis=0)
        middle_grad = out_grad + norm_back(normed_grad_two, scaled_two, inverse_two, gain_rows[1])
        gain_two = jnp.sum(normed_grad_two * scaled_two, axis=0)
        shift_two = jnp.sum(normed_grad_two, axis=0)
        full_mid_grad = gather_grads(middle_grad)
        normed_one, scaled_one, inverse_one = norm_parts(residual, gain_rows[0], shift_rows[0])
        normed_one = normed_one.astype(jnp.bfloat16)
        full_one = regather(normed_one)
        projected = jnp.dot(full_one, joined, preferred_element_type=jnp.float32)
        queries, key_rows, value_rows = split_projected(projected)
        mixed_grad = jnp.einsum(
            "sd,cd->sc", full_mid_grad, out_matrix, preferred_element_type=jnp.float32
        ).astype(jnp.bfloat16)
        mixed_rows, query_grad, key_grad, value_grad = attend_backward(
            queries, key_rows, value_rows, mixed_grad, log_totals, segment
        )
        out_grad_matrix = jnp.einsum(
            "sc,sd->cd", mixed_rows, full_mid_grad, preferred_element_type=jnp.float32
        )
        mixer_shift_grad = jnp.sum(middle_grad, axis=0)
        qkv_low = jnp.concatenate([query_grad, key_grad, value_grad], axis=1).astype(jnp.bfloat16)
        joined_grad = jnp.einsum("sd,sc->dc", full_one, qkv_low, preferred_element_type=jnp.float32)
        normed_grad_one = input_sum(qkv_low, joined)
        in_grad = middle_grad + norm_back(normed_grad_one, scaled_one, inverse_one, gain_rows[0])
        gain_one = jnp.sum(normed_grad_one * scaled_one, axis=0)
        shift_one = jnp.sum(normed_grad_one, axis=0)
        qv_local = jnp.stack([jnp.sum(query_grad, axis=0), jnp.sum(value_grad, axis=0)])
        qv_full = lax.dynamic_update_slice_in_dim(
            jnp.zeros((2, model_width), jnp.float32), qv_local, lane_index * cols_local, 1
        )
        up_full = lax.dynamic_update_slice_in_dim(
            jnp.zeros((up_bias.shape[1],), jnp.float32), up_shift_grad, lane_index * hidden_local, 0
        )
        weight_terms = (joined_grad, out_grad_matrix, up_grad, down_grad)
        small_terms = (
            jnp.stack([gain_one, gain_two]),
            jnp.stack([shift_one, shift_two]),
            qv_full,
            up_full,
            jnp.stack([mixer_shift_grad, feed_shift_grad]),
        )
        return (in_grad, weight_terms, small_terms)

    ticks = micro_count + section_count - 1
    received = jnp.zeros((own_rows, model_width), jnp.bfloat16)
    saved_in = jnp.zeros_like(inputs)
    saved_mid = jnp.zeros((micro_count, own_rows, model_width), jnp.float32)
    saved_totals = jnp.zeros((micro_count, heads_local, seq_len), jnp.float32)
    states = jnp.zeros_like(inputs)
    for tick in range(ticks):
        micro = tick - section_index
        running = (micro >= 0) & (micro < micro_count)
        which = jnp.clip(micro, 0, micro_count - 1)
        own_in = lax.dynamic_index_in_dim(inputs, which, 0, keepdims=False)
        block_in = jnp.where(section_index == 0, own_in, received)
        segment = lax.dynamic_index_in_dim(segment_ids, which, 0, keepdims=False)
        layer_residual = block_in.astype(jnp.float32)
        layer_normed_one = norm_parts(layer_residual, gain_rows[0], shift_rows[0])[0].astype(
            jnp.bfloat16
        )
        layer_full_one, layer_projected = spread_rows(layer_normed_one, joined)
        layer_queries, layer_key_rows, layer_value_rows = split_projected(layer_projected)
        layer_mixed_rows, layer_log_totals = attend_forward(
            layer_queries, layer_key_rows, layer_value_rows, segment
        )
        layer_middle = layer_residual + branch_sum(layer_mixed_rows, out_matrix) + mixer_shift
        layer_normed_two = norm_parts(layer_middle, gain_rows[1], shift_rows[1])[0].astype(
            jnp.bfloat16
        )
        layer_full_two, layer_hidden = spread_rows(layer_normed_two, up_matrix)
        layer_active = gelu_exact(layer_hidden + up_shift).astype(jnp.bfloat16)
        block_out = layer_middle + branch_sum(layer_active, down_matrix) + feed_shift
        block_out, middle, log_totals, full_one, full_two = (
            block_out,
            layer_middle,
            layer_log_totals,
            layer_full_one,
            layer_full_two,
        )
        handed = block_out.astype(jnp.bfloat16)
        saved_in = store_at(saved_in, block_in, which, running)
        saved_mid = store_at(saved_mid, middle, which, running)
        saved_totals = store_at(saved_totals, log_totals, which, running)
        states = store_at(states, handed, which, running)
        if tick + 1 < ticks:
            received = passed_along(handed, "section", 1)
    back_received = jnp.zeros((own_rows, model_width), jnp.bfloat16)
    weight_totals = (
        jnp.zeros(joined.shape, jnp.float32),
        jnp.zeros(out_matrix.shape, jnp.float32),
        jnp.zeros(up_matrix.shape, jnp.float32),
        jnp.zeros(down_matrix.shape, jnp.float32),
    )
    small_totals = (
        jnp.zeros((2, model_width), jnp.float32),
        jnp.zeros((2, model_width), jnp.float32),
        jnp.zeros((2, model_width), jnp.float32),
        jnp.zeros((up_bias.shape[1],), jnp.float32),
        jnp.zeros((2, model_width), jnp.float32),
    )
    grads_store = jnp.zeros((micro_count, own_rows, model_width), jnp.float32)
    for tick in range(ticks):
        micro = tick - (section_count - 1) + section_index
        running = (micro >= 0) & (micro < micro_count)
        which = jnp.clip(micro, 0, micro_count - 1)
        own_grad = lax.dynamic_index_in_dim(cotangent, which, 0, keepdims=False)
        out_grad = jnp.where(section_index == section_count - 1, own_grad, back_received).astype(
            jnp.float32
        )
        in_grad, weight_terms, small_terms = layer_backward(
            lax.dynamic_index_in_dim(saved_in, which, 0, keepdims=False),
            lax.dynamic_index_in_dim(saved_mid, which, 0, keepdims=False),
            lax.dynamic_index_in_dim(saved_totals, which, 0, keepdims=False),
            lax.dynamic_index_in_dim(segment_ids, which, 0, keepdims=False),
            out_grad,
        )
        joined_term, out_term, up_term, down_term = tuple(
            (jnp.where(running, term, 0.0) for term in weight_terms)
        )
        weight_terms = (joined_term, out_term, up_term, down_term)
        weight_totals = tuple((total + term for total, term in zip(weight_totals, weight_terms)))
        small_totals = tuple(
            (
                total + jnp.where(running, term, 0.0)
                for total, term in zip(small_totals, small_terms)
            )
        )
        grads_store = store_at(grads_store, in_grad, which, running)
        if tick + 1 < ticks:
            back_received = passed_along(in_grad.astype(jnp.bfloat16), "section", -1)
    joined_total, out_total, up_total, down_total = weight_totals
    summed = (
        lax.psum(joined_total.astype(jnp.bfloat16), "dp").astype(jnp.float32),
        lax.psum(out_total.astype(jnp.bfloat16), "dp").astype(jnp.float32),
        lax.psum(up_total.astype(jnp.bfloat16), "dp").astype(jnp.float32),
        lax.psum(down_total.astype(jnp.bfloat16), "dp").astype(jnp.float32),
    )
    gain_total, shift_total, qv_total, up_shift_total, out_shift_total = small_totals
    small_summed = lax.psum(
        (gain_total, shift_total, qv_total, up_shift_total, out_shift_total), ("dp", "tensor")
    )
    qkv_grad = summed[0].reshape(model_width, 3, cols_local).transpose(1, 0, 2)
    return (
        states[None],
        grads_store[None],
        small_summed[0][None],
        small_summed[1][None],
        qkv_grad[None],
        small_summed[2][None],
        summed[1][None],
        summed[2][None],
        small_summed[3][None],
        summed[3][None],
        small_summed[4][None],
    )


def solution(mesh):
    placed = (
        P("dp", "tensor", None),
        P("dp", "tensor", None),
        P("dp", None),
        P("section", None, None),
        P("section", None, None),
        P("section", None, None, "tensor"),
        P("section", None, None),
        P("section", "tensor", None),
        P("section", None, "tensor"),
        P("section", None),
        P("section", "tensor", None),
        P("section", None, None),
    )
    sizes = dict(mesh.shape)

    def on_device(inputs, *rest):
        each = inputs.shape[0] == sizes["section"] * sizes["tensor"]
        paired = sizes["section"] == 2 and sizes["tensor"] == 2 and sizes["dp"] % 2 == 0
        doubling = (sizes["dp"] // 2) & (sizes["dp"] // 2 - 1) == 0
        if each and paired and doubling:
            return one_sequence_each(inputs, *rest)
        return pipelined(inputs, *rest)

    return jax.shard_map(
        on_device,
        mesh=mesh,
        in_specs=placed,
        out_specs=(
            P("section", "dp", "tensor", None),
            P("section", "dp", "tensor", None),
            P("section", None, None),
            P("section", None, None),
            P("section", None, None, "tensor"),
            P("section", None, None),
            P("section", "tensor", None),
            P("section", None, "tensor"),
            P("section", None),
            P("section", "tensor", None),
            P("section", None, None),
        ),
        check_vma=False,
    )
```

```python
import functools
import math

import jax
import jax.numpy as jnp
from jax import lax
from jax.experimental import pallas as pl
from jax.experimental.pallas import tpu as pltpu
from jax.sharding import PartitionSpec as P

HEAD_DIM = 48
IMAGE_IDS = 5
IMAGE_MOST = 512
EPSILON = 1e-05
NEGATIVE = -1e30
TILE = 128
BLOCK = 256
EXTRA = 16
LOG2E = math.log2(math.e)
SCALING = HEAD_DIM ** (-0.5)
AXES = ("section", "dp", "tensor")
VMEM_LIMIT = 60 * 1024 * 1024
MESH = pl.DeviceIdType.MESH
F32 = jnp.float32
BF16 = jnp.bfloat16


def nn(left, right):
    return lax.dot_general(left, right, (((1,), (0,)), ((), ())), preferred_element_type=F32)


def nt(left, right):
    return lax.dot_general(left, right, (((1,), (1,)), ((), ())), preferred_element_type=F32)


def tn(left, right):
    return lax.dot_general(left, right, (((0,), (0,)), ((), ())), preferred_element_type=F32)


def normalise(rows):
    centre = rows - jnp.mean(rows, axis=-1, keepdims=True)
    inverse = lax.rsqrt(jnp.mean(centre * centre, axis=-1, keepdims=True) + EPSILON)
    return centre * inverse, inverse


def normalise_back(gradient, scaled, inverse, gain):
    upstream = gradient * gain
    return inverse * (
        upstream
        - jnp.mean(upstream, axis=-1, keepdims=True)
        - scaled * jnp.mean(upstream * scaled, axis=-1, keepdims=True)
    )


def gelu_pair(values):
    share = 0.5 + 0.5 * lax.erf(values * math.sqrt(0.5))
    bell = jnp.exp2(values * values * (-0.5 * LOG2E))
    return values * share, share + values * bell * (1.0 / math.sqrt(2 * math.pi))


def extra_rows(rows, width):
    at = lax.broadcasted_iota(jnp.int32, (EXTRA, width), 0)
    out = jnp.zeros((EXTRA, width), F32)
    for index, row in enumerate(rows):
        out = jnp.where(at == index, row, out)
    return out.astype(BF16)


def three_parts(row):
    first = row.astype(BF16).astype(F32)
    second = (row - first).astype(BF16).astype(F32)
    return [first, second, row - first - second]


def each_image(start_ref, tiles_ref, body):
    most = IMAGE_MOST // TILE + 1

    def image(index, carry):
        first = start_ref[index]
        tiles = tiles_ref[index]
        for count in range(1, most + 1):

            @pl.when(tiles == count)
            def _():
                body(index, pl.multiple_of(first * TILE, TILE), count * TILE)

        return carry

    lax.fori_loop(0, IMAGE_IDS, image, 0)


def run_copies(copies):
    for copy in copies:
        copy.start()


def wait_copies(copies):
    for copy in copies:
        copy.wait()


def slot_of(place_ref, index):
    return 2 * (place_ref[0] ^ (index // 2)) + (place_ref[1] ^ (index % 2))


def once(shape):
    zeros = (0,) * len(shape)
    return pl.BlockSpec(shape, lambda *_: zeros, pipeline_mode=pl.Buffered(1))


def anywhere(count):
    return [pl.BlockSpec(memory_space=pl.ANY)] * count


def settings(flops, collective=None):
    remote = {} if collective is None else dict(collective_id=collective, has_side_effects=True)
    return dict(
        compiler_params=pltpu.CompilerParams(vmem_limit_bytes=VMEM_LIMIT, **remote),
        cost_estimate=pl.CostEstimate(flops=flops, bytes_accessed=1_000_000, transcendentals=0),
    )


def blocks_of(ref, axis=0):
    return ref.shape[axis] // BLOCK


def block_at(index):
    return pl.ds(pl.multiple_of(index * BLOCK, BLOCK), BLOCK)


def big_blocks(rows):
    size = rows // 2
    return [slice(i * size, (i + 1) * size) for i in range(2)]


def attend_forward_image(index, at, width, heads, seg_ref, qkv_ref, store):
    win = pl.ds(at, width)
    mine = seg_ref[:, win] == index
    mask = jnp.where(mine, 0.0, NEGATIVE)
    one = jnp.ones((1, width), F32)
    query_extra = extra_rows([mask, one], width)
    key_extra = extra_rows([one, mask], width)
    value_extra = extra_rows([one], width)
    cols = heads * HEAD_DIM

    def rows_of(third, head):
        low = third * cols + head * HEAD_DIM
        return qkv_ref[low : low + HEAD_DIM, win]

    def scores(head):
        queries = jnp.concatenate([rows_of(0, head), query_extra], axis=0)
        keys = jnp.concatenate([rows_of(1, head), key_extra], axis=0)
        return tn(keys, queries)

    following = scores(0)
    for head in range(heads):
        current = following
        if head + 1 < heads:
            following = scores(head + 1)
        peak = jnp.max(current, axis=0, keepdims=True)
        weights = jnp.exp2(current - peak).astype(BF16)
        mixed = nn(jnp.concatenate([rows_of(2, head), value_extra], axis=0), weights)
        total = mixed[HEAD_DIM : HEAD_DIM + 1]
        store(head, win, mine, mixed[:HEAD_DIM] * (1.0 / total), peak + jnp.log2(total))


def attend_backward_image(index, at, width, heads, seg_ref, qkv_ref, mixed_ref, total_ref, mixed_grad, sums):
    win = pl.ds(at, width)
    mine = seg_ref[:, win] == index
    mask = jnp.where(mine, 0.0, NEGATIVE)
    one = jnp.ones((1, width), F32)
    key_extra = extra_rows([one, mask, one, one, one], width)
    value_extra = extra_rows([one, one, one], width)
    cols = heads * HEAD_DIM

    def span(third, head):
        low = third * cols + head * HEAD_DIM
        return slice(low, low + HEAD_DIM)

    def products(head):
        own = span(0, head)
        grads = mixed_grad[own, win]
        inner = jnp.sum(grads.astype(F32) * mixed_ref[own, win].astype(F32), axis=0, keepdims=True)
        query_extra = extra_rows([mask, one] + three_parts(-total_ref[head, :, win]), width)
        grad_extra = extra_rows(three_parts(-inner), width)
        keys = jnp.concatenate([qkv_ref[span(1, head), win], key_extra], axis=0)
        queries = jnp.concatenate([qkv_ref[own, win], query_extra], axis=0)
        values = jnp.concatenate([qkv_ref[span(2, head), win], value_extra], axis=0)
        return tn(keys, queries), tn(values, jnp.concatenate([grads, grad_extra], axis=0))

    following = products(0)
    for head in range(heads):
        scores, terms = following
        if head + 1 < heads:
            following = products(head + 1)
        weights = jnp.exp2(scores)
        score_grads = (weights * terms).astype(BF16)
        sums[span(0, head), win] += nn(qkv_ref[span(1, head), win], score_grads) * SCALING
        sums[span(1, head), win] += nt(qkv_ref[span(0, head), win], score_grads) * (1.0 / LOG2E)
        sums[span(2, head), win] += nt(mixed_grad[span(0, head), win], weights.astype(BF16))


def mixer_forward_kernel(
    place_ref, start_ref, tiles_ref, seg_ref, hidden_ref, norm_ref, qkv_shift_ref, *rest, pieces, out_pieces, heads
):
    first = out_pieces in (0, pieces)
    last = out_pieces > 0
    rest = list(rest)
    weights = [rest.pop(0) for _ in range(pieces)]
    if not first:
        normed_in = rest.pop(0)
        mixed_before = rest.pop(0)
    if last:
        out_weights = [rest.pop(0) for _ in range(out_pieces)]
        out_shift_ref = rest.pop(0)
    qkv_ref, mixed_ref, total_ref = rest.pop(0), rest.pop(0), rest.pop(0)
    if first:
        normed_out = rest.pop(0)
    if last:
        middle_ref = rest.pop(0)
    weight, normed, sems = rest.pop(0), rest.pop(0), rest.pop(0)
    if last:
        out_weight, mixed_all, out_sems = rest
    step = pl.program_id(0)
    cols = heads * HEAD_DIM
    before = out_pieces - pieces if last else 0
    copies = [
        pltpu.make_async_copy(
            weights[i].at[0 : 3 * cols], weight.at[i], sems.at[i]
        )
        for i in range(pieces)
    ]
    if not first:
        norm_copy = pltpu.make_async_copy(normed_in, normed, sems.at[pieces])
    out_copies = []
    if last:
        for i in range(out_pieces):
            out_copies.append(
                pltpu.make_async_copy(
                    out_weights[i].at[3 * cols : 4 * cols],
                    out_weight.at[i * cols : (i + 1) * cols],
                    out_sems.at[i],
                )
            )
        for i in range(before):
            out_copies.append(
                pltpu.make_async_copy(
                    mixed_before.at[i], mixed_all.at[i * cols : (i + 1) * cols], out_sems.at[out_pieces + i]
                )
            )

    @pl.when(step == 0)
    def _():
        if not first:
            norm_copy.start()
        run_copies(copies + out_copies)
        if first:

            def norm_block(i, carry):
                rows = block_at(i)
                scaled, _ = normalise(hidden_ref[rows, :].astype(F32))
                result = (scaled * norm_ref[0:1, :] + norm_ref[1:2, :]).astype(BF16)
                normed[rows, :] = result
                normed_out[rows, :] = result
                return carry

            lax.fori_loop(0, blocks_of(hidden_ref), norm_block, 0)
        else:
            norm_copy.wait()

    for index in range(pieces):

        @pl.when(step == index)
        def _():
            copies[index].wait()

    projected = nt(weight[step], normed[...]) + qkv_shift_ref[0]
    qkv_ref[0, 0:cols, :] = (projected[0:cols] * (SCALING * LOG2E)).astype(BF16)
    qkv_ref[0, cols : 3 * cols, :] = projected[cols : 3 * cols].astype(BF16)

    def store(head, win, mine, mixed, total):
        rows = slice(head * HEAD_DIM, (head + 1) * HEAD_DIM)
        old = mixed_ref[0, rows, win].astype(F32)
        mixed_ref[0, rows, win] = jnp.where(mine, mixed, old).astype(BF16)
        total_ref[head, :, win] = jnp.where(mine, total, total_ref[head, :, win])

    each_image(
        start_ref,
        tiles_ref,
        lambda index, at, width: attend_forward_image(
            index, at, width, heads, seg_ref, qkv_ref.at[0], store
        ),
    )
    if last:
        mixed_all[pl.ds(pl.multiple_of((before + step) * cols, cols), cols), :] = mixed_ref[0]

        @pl.when(step == pieces - 1)
        def _():
            wait_copies(out_copies)

            for rows in big_blocks(hidden_ref.shape[0]):
                branch = tn(mixed_all[:, rows], out_weight[...])
                middle_ref[rows, :] = hidden_ref[rows, :].astype(F32) + branch + out_shift_ref[...]


def mixer_forward(images, hidden, norm, qkv_shift, pieces, offset=0, before=None, out_pieces=(), out_shift=None):
    rows, width = hidden.shape
    count = len(pieces)
    cols = width // 4
    heads = cols // HEAD_DIM
    place, start, tiles, segment = images
    operands = list(pieces)
    outs = [
        jax.ShapeDtypeStruct((count, 3 * cols, rows), BF16),
        jax.ShapeDtypeStruct((count, cols, rows), BF16),
        jax.ShapeDtypeStruct((count * heads, 1, rows), F32),
    ]
    scratch = [
        pltpu.VMEM((count, 3 * cols, width), BF16),
        pltpu.VMEM((rows, width), BF16),
        pltpu.SemaphoreType.DMA((count + 1,)),
    ]
    if before is None:
        outs.append(jax.ShapeDtypeStruct((rows, width), BF16))
    else:
        operands += list(before)
    specs = anywhere(len(operands) + len(out_pieces))
    operands += list(out_pieces)
    if out_pieces:
        operands.append(out_shift)
        specs.append(once((1, width)))
        outs.append(jax.ShapeDtypeStruct((rows, width), F32))
        scratch += [
            pltpu.VMEM((width, width), BF16),
            pltpu.VMEM((width, rows), BF16),
            pltpu.SemaphoreType.DMA((2 * len(out_pieces),)),
        ]
    return pl.pallas_call(
        functools.partial(
            mixer_forward_kernel,
            pieces=count,
            out_pieces=len(out_pieces),
            heads=heads,
        ),
        grid_spec=pltpu.PrefetchScalarGridSpec(
            num_scalar_prefetch=3,
            grid=(count,),
            in_specs=[
                once((1, rows)),
                once((rows, width)),
                once((2, width)),
                pl.BlockSpec((1, 3 * cols, 1), lambda i, place, *_: (slot_of(place, i + offset), 0, 0)),
            ]
            + specs,
            out_specs=[
                pl.BlockSpec((1, 3 * cols, rows), lambda i, *_: (i, 0, 0)),
                pl.BlockSpec((1, cols, rows), lambda i, *_: (i, 0, 0)),
                pl.BlockSpec((heads, 1, rows), lambda i, *_: (i, 0, 0)),
            ]
            + [once((rows, width))] * (len(outs) - 3),
            scratch_shapes=scratch,
        ),
        out_shape=outs,
        name="mixer_forward",
        **settings(4_000_000_000),
    )(place, start, tiles, segment, hidden, norm, qkv_shift, *operands)


def feed_forward_kernel(place_ref, middle_ref, norm_ref, up_shift_ref, start_ref, *rest, pieces, offset, last):
    ups, downs = rest[:pieces], rest[pieces : 2 * pieces]
    out_ref, active_ref, slope_ref, up_weight, down_weight, sems = rest[2 * pieces :]
    step = pl.program_id(0)
    size = up_weight.shape[2]
    copies = []
    for i in range(pieces):
        copies.append(
            pltpu.make_async_copy(ups[i], up_weight.at[i], sems.at[0, i])
        )
        copies.append(
            pltpu.make_async_copy(downs[i], down_weight.at[i], sems.at[1, i])
        )

    @pl.when(step == 0)
    def _():
        run_copies(copies)

    scaled, _ = normalise(middle_ref[...])
    normed = (scaled * norm_ref[0:1, :] + norm_ref[1:2, :]).astype(BF16)
    total = start_ref[...] if offset else middle_ref[...] + start_ref[...]

    @pl.when(step == 0)
    def _():
        wait_copies(copies)

    def raise_by(index):
        return nn(normed, up_weight[index]) + up_shift_ref[slot_of(place_ref, offset + index)]

    following = raise_by(0)
    for index in range(pieces):
        raised = following
        if index + 1 < pieces:
            following = raise_by(index + 1)
        part = pl.ds(index * size, size)
        active, slope = gelu_pair(raised)
        active = active.astype(BF16)
        active_ref[:, part] = active
        slope_ref[:, part] = slope.astype(BF16)
        total = total + nn(active, down_weight[index])
    out_ref[...] = total.astype(out_ref.dtype)


def feed_forward(place, middle, norm, up_shift, begin, ups, downs, offset, last):
    rows, width = middle.shape
    pieces = len(ups)
    size = up_shift.shape[2]
    hidden = size * pieces
    return pl.pallas_call(
        functools.partial(
            feed_forward_kernel,
            pieces=pieces,
            offset=offset,
            last=last,
        ),
        grid_spec=pltpu.PrefetchScalarGridSpec(
            num_scalar_prefetch=1,
            grid=(rows // BLOCK,),
            in_specs=[
                pl.BlockSpec((BLOCK, width), lambda i, *_: (i, 0)),
                once((2, width)),
                once(up_shift.shape),
                pl.BlockSpec((BLOCK, width), lambda i, *_: (i, 0)) if offset else once((1, width)),
            ]
            + anywhere(2 * pieces),
            out_specs=[
                pl.BlockSpec((BLOCK, width), lambda i, *_: (i, 0)),
                pl.BlockSpec((BLOCK, hidden), lambda i, *_: (i, 0)),
                pl.BlockSpec((BLOCK, hidden), lambda i, *_: (i, 0)),
            ],
            scratch_shapes=[
                pltpu.VMEM((pieces, width, size), BF16),
                pltpu.VMEM((pieces, size, width), BF16),
                pltpu.SemaphoreType.DMA((2, pieces)),
            ],
        ),
        out_shape=[
            jax.ShapeDtypeStruct((rows, width), BF16 if last else F32),
            jax.ShapeDtypeStruct((rows, hidden), BF16),
            jax.ShapeDtypeStruct((rows, hidden), BF16),
        ],
        name="feed_forward",
        **settings(4_000_000_000),
    )(place, middle, norm, up_shift, begin, *ups, *downs)


ORDER = (1, 3, 0, 2)


class Neighbours:
    def __init__(self, count):
        self.section, self.group, self.lane = [lax.axis_index(axis) for axis in AXES]
        self.core = lax.rem(self.group, 2)
        self.z_index = self.group // 2
        self.count = count
        self.twin = (self.section, self.group + 1 - 2 * self.core, self.lane)
        self.beside = (self.section, self.group, 1 - self.lane)
        self.across = (1 - self.section, self.group, self.lane)
        self.far = (1 - self.section, self.group, 1 - self.lane)
        self.line = [self.along(step) for step in range(1, count)]

    def along(self, step):
        return (self.section, lax.rem(self.z_index + step + self.count, self.count) * 2 + self.core, self.lane)

    def slot_of(self, index):
        return 2 * (self.lane + (index // 2) * (1 - 2 * self.lane)) + self.core + (index % 2) * (1 - 2 * self.core)


def greet(devices):
    barrier = pltpu.get_barrier_semaphore()
    for device in devices:
        pl.semaphore_signal(barrier, inc=1, device_id=device, device_id_type=MESH)
    pl.semaphore_wait(barrier, len(devices))


class Remote:
    def __init__(self, sends, receives):
        self.sends, self.receives, self.slot = sends, receives, 0

    def reserve(self, number):
        self.slot += number
        return self.slot - number

    def copy(self, source, target, device, slot=None):
        slot = self.reserve(1) if slot is None else slot
        return pltpu.make_async_remote_copy(
            src_ref=source,
            dst_ref=target,
            send_sem=self.sends.at[slot],
            recv_sem=self.receives.at[slot],
            device_id=device,
            device_id_type=MESH,
        )


def sum_with_core(index, copies, grad_of, sent, came, put):
    slot = index % 2
    if index < 2:

        def keep(where, value):
            sent[(slot,) + where] = value.astype(BF16)

        grad_of(keep)
        copies[slot].start()
    else:
        copies[slot].wait_recv()

        def add(where, value):
            put(slot, where, (value + came[(slot,) + where].astype(F32)).astype(BF16))

        grad_of(add)
        copies[slot].wait_send()


def plane_copies(remote, near, sums, target, half, columns):
    size = sums.shape[1] // 2
    mine = pl.ds(pl.multiple_of(near.section * size, size), size)
    theirs = pl.ds(pl.multiple_of((1 - near.section) * size, size), size)
    return [
        remote.copy(sums.at[1, mine, columns], target.at[0, :, columns], near.beside),
        remote.copy(sums.at[0, theirs, columns], target.at[1, :, columns], near.across),
        remote.copy(sums.at[1, theirs, columns], target.at[2, :, columns], near.far),
    ]


def line_copies(remote, near, part, target, columns):
    size = part.shape[0] // near.count
    copies = []
    for i, device in enumerate(near.line):
        to = lax.rem(near.z_index + i + 1, near.count)
        rows = pl.ds(pl.multiple_of(to * size, size), size)
        copies.append(remote.copy(part.at[rows, columns], target.at[i, :, columns], device))
    return copies


def line_total(near, part, came, columns):
    size = came.shape[1]
    total = part[pl.ds(pl.multiple_of(near.z_index * size, size), size), columns].astype(F32)
    for i in range(near.count - 1):
        total = total + came[i, :, columns].astype(F32)
    return total


def feed_backward_kernel(grad_ref, middle_ref, norm_ref, *rest, columns, rider, line):
    pieces = 4
    rest = list(rest)
    actives = [rest.pop(0) for _ in range(pieces)]
    slopes = [rest.pop(0) for _ in range(pieces)]
    ups = [rest.pop(0) for _ in range(pieces)]
    downs = [rest.pop(0) for _ in range(pieces)]
    rider_ref = rest.pop(0) if rider else None
    keep_ref, beside_ref, across_ref, far_ref = [rest.pop(0) for _ in range(4)]
    up_shift_grad_ref, middle_grad_ref, small_ref = [rest.pop(0) for _ in range(3)]
    rider_out_ref = rest.pop(0) if rider else None
    (
        normed_t,
        grad_t,
        normed_grad,
        up_weight,
        down_weight,
        active,
        slope,
        low_grad,
        sent,
        came,
        sems,
        sends,
        receives,
    ) = rest[:13]
    step = pl.program_id(0)
    rows_all, width = grad_ref.shape
    size = up_weight.shape[2]
    blocks = blocks_of(grad_ref)
    near = Neighbours(line)
    remote = Remote(sends, receives)
    core_copies = [remote.copy(sent.at[slot], came.at[slot], near.twin) for slot in range(2)]
    devices = [near.twin]
    rider_copies = []
    if rider:
        rider_own, rider_came, rider_sem = rest[13:]
        devices += [near.beside, near.across, near.far]
        half = rider_own.shape[0]
        rider_copies = plane_copies(remote, near, rider_ref, rider_came, half, slice(None))
        rider_keep = pltpu.make_async_copy(
            rider_ref.at[0, pl.ds(pl.multiple_of(near.section * half, half), half)], rider_own, rider_sem.at[0]
        )
    copies = []
    for slot, i in enumerate(ORDER):
        own = pl.ds(columns[i] * size, size)
        at = slot % 2
        copies.append(
            [
                pltpu.make_async_copy(downs[i], down_weight.at[at], sems.at[0, at]),
                pltpu.make_async_copy(slopes[i].at[:, own], slope.at[at], sems.at[1, at]),
                pltpu.make_async_copy(ups[i], up_weight.at[at], sems.at[2, at]),
                pltpu.make_async_copy(actives[i].at[:, own], active.at[at], sems.at[3, at]),
            ]
        )

    @pl.when(step == 0)
    def _():
        run_copies(copies[0])
        greet(devices)
        if rider:
            run_copies(rider_copies)
            rider_keep.start()

        def prepare(i, carry):
            rows = block_at(i)
            scaled, _ = normalise(middle_ref[rows, :])
            normed = (scaled * norm_ref[0:1, :] + norm_ref[1:2, :]).astype(BF16)
            normed_t[:, rows] = normed.T
            grad_t[:, rows] = grad_ref[rows, :].T
            return carry

        lax.fori_loop(0, blocks, prepare, 0)

    for index in range(pieces):

        @pl.when(step == index)
        def _():
            at = index % 2
            wait_copies(copies[index])
            if index + 1 < pieces:
                run_copies(copies[index + 1])
            shift_grad = jnp.zeros((1, size), F32)
            for rows in big_blocks(rows_all):
                hidden_grad = nt(grad_ref[rows, :], down_weight[at]) * slope[at, rows, :].astype(F32)
                low = hidden_grad.astype(BF16)
                low_grad[rows, :] = low
                shift_grad = shift_grad + jnp.sum(hidden_grad, axis=0, keepdims=True)
                term = nt(low, up_weight[at])
                normed_grad[rows, :] = term if index == 0 else normed_grad[rows, :] + term
            up_shift_grad_ref[near.slot_of(ORDER[index])] = shift_grad

            def grad_of(put):
                for rows in big_blocks(width):
                    put((0, rows, slice(None)), nn(normed_t[rows, :], low_grad[...]))
                    put((1, rows, slice(None)), nn(grad_t[rows, :], active[at]))

            def put(slot, where, value):
                inner, outer = ((keep_ref, across_ref), (beside_ref, far_ref))[slot]

                @pl.when(near.section == where[0])
                def _():
                    inner[where[1:]] = value

                @pl.when(near.section != where[0])
                def _():
                    outer[where[1:]] = value

            sum_with_core(index, core_copies, grad_of, sent, came, put)

    @pl.when(step == pieces - 1)
    def _():
        def finish(i, sums):
            rows = block_at(i)
            scaled, inverse = normalise(middle_ref[rows, :])
            gradient = normed_grad[rows, :]
            upper = grad_ref[rows, :].astype(F32)
            middle_grad = upper + normalise_back(gradient, scaled, inverse, norm_ref[0:1, :])
            middle_grad_ref[rows, :] = middle_grad
            terms = (gradient * scaled, gradient, middle_grad, upper)
            return tuple(old + jnp.sum(term, axis=0, keepdims=True) for old, term in zip(sums, terms))

        zero = jnp.zeros((1, width), F32)
        sums = lax.fori_loop(0, blocks, finish, (zero, zero, zero, zero))
        for index, row in enumerate(sums):
            small_ref[index : index + 1, :] = row
        if rider:
            rider_keep.wait()
            wait_copies(rider_copies)
            total = rider_own[...].astype(F32)
            for i in range(3):
                total = total + rider_came[i].astype(F32)
            rider_out_ref[...] = total.astype(BF16)


def feed_backward(grad, middle, norm, actives, slopes, columns, ups, downs, collective, rider=None):
    rows, width = middle.shape
    pieces = len(ups)
    size = ups[0].shape[1]
    operands = [*actives, *slopes, *ups, *downs] + ([] if rider is None else [rider])
    outs = [jax.ShapeDtypeStruct((width, size), BF16)] * 4 + [
        jax.ShapeDtypeStruct((pieces, 1, size), F32),
        jax.ShapeDtypeStruct((rows, width), F32),
        jax.ShapeDtypeStruct((4, width), F32),
    ]
    scratch = [
        pltpu.VMEM((width, rows), BF16),
        pltpu.VMEM((width, rows), BF16),
        pltpu.VMEM((rows, width), F32),
        pltpu.VMEM((2, width, size), BF16),
        pltpu.VMEM((2, size, width), BF16),
        pltpu.VMEM((2, rows, size), BF16),
        pltpu.VMEM((2, rows, size), BF16),
        pltpu.VMEM((rows, size), BF16),
        pltpu.VMEM((2, 2, width, size), BF16),
        pltpu.VMEM((2, 2, width, size), BF16),
        pltpu.SemaphoreType.DMA((4, 2)),
        pltpu.SemaphoreType.DMA((8,)),
        pltpu.SemaphoreType.DMA((8,)),
    ]
    if rider is not None:
        half = rider.shape[1] // 2
        outs.append(jax.ShapeDtypeStruct((half, width), BF16))
        scratch += [
            pltpu.VMEM((half, width), BF16),
            pltpu.VMEM((3, half, width), BF16),
            pltpu.SemaphoreType.DMA((1,)),
        ]
    return pl.pallas_call(
        functools.partial(
            feed_backward_kernel, columns=columns, rider=rider is not None, line=lax.axis_size("dp") // 2
        ),
        grid=(pieces,),
        in_specs=[once((rows, width)), once((rows, width)), once((2, width))] + anywhere(len(operands)),
        out_specs=[once(out.shape) for out in outs],
        scratch_shapes=scratch,
        out_shape=outs,
        name="feed_backward",
        **settings(16_000_000_000, collective),
    )(grad, middle, norm, *operands)


def mixer_backward_kernel(
    place_ref, start_ref, tiles_ref, seg_ref, middle_grad_ref, qkv_ref_all, *rest, saved, heads
):
    pieces = len(saved)
    rest = [qkv_ref_all] + list(rest)
    qkvs = [rest.pop(0) for _ in range(pieces)]
    mixeds = [rest.pop(0) for _ in range(pieces)]
    log_totals = [rest.pop(0) for _ in range(pieces)]
    weights = [rest.pop(0) for _ in range(pieces)]
    projected_ref, qkv_shift_grad_ref = rest[:2]
    qkv, mixed, totals, out_weight, low_middle, mixed_grad, sums, sems = rest[2:]
    step = pl.program_id(0)
    cols = heads * HEAD_DIM
    copies = []
    for i in range(pieces):
        at = saved[i]
        copies.append(
            [
                pltpu.make_async_copy(weights[i].at[3 * cols : 4 * cols], out_weight.at[i], sems.at[0, i]),
                pltpu.make_async_copy(qkvs[i].at[at], qkv.at[i], sems.at[1, i]),
                pltpu.make_async_copy(mixeds[i].at[at], mixed.at[i], sems.at[2, i]),
                pltpu.make_async_copy(
                    log_totals[i].at[at * heads : (at + 1) * heads], totals.at[i], sems.at[3, i]
                ),
            ]
        )

    @pl.when(step == 0)
    def _():
        for group in copies:
            run_copies(group)
        low_middle[...] = middle_grad_ref[...].astype(BF16)

    for index in range(pieces):

        @pl.when(step == index)
        def _():
            wait_copies(copies[index])

    mixed_grad[...] = nt(out_weight[step], low_middle[...]).astype(BF16)
    sums[...] = jnp.zeros_like(sums)
    each_image(
        start_ref,
        tiles_ref,
        lambda index, at, span: attend_backward_image(
            index, at, span, heads, seg_ref, qkv.at[step], mixed.at[step], totals.at[step], mixed_grad, sums
        ),
    )
    gradient = sums[...]
    projected_ref[0] = gradient.astype(BF16)
    qkv_shift_grad_ref[0] = jnp.sum(gradient, axis=1, keepdims=True).T


def mixer_backward(images, middle_grad, qkvs, mixeds, log_totals, saved, weights):
    rows, width = middle_grad.shape
    count = len(weights)
    cols = width // 4
    heads = cols // HEAD_DIM
    place, start, tiles, segment = images
    operands = [*qkvs, *mixeds, *log_totals, *weights]
    return pl.pallas_call(
        functools.partial(mixer_backward_kernel, saved=saved, heads=heads),
        grid_spec=pltpu.PrefetchScalarGridSpec(
            num_scalar_prefetch=3,
            grid=(count,),
            in_specs=[once((1, rows)), once((rows, width))] + anywhere(len(operands)),
            out_specs=[
                pl.BlockSpec((1, 3 * cols, rows), lambda i, *_: (i, 0, 0)),
                pl.BlockSpec((1, 1, 3 * cols), lambda i, place, *_: (slot_of(place, i), 0, 0)),
            ],
            scratch_shapes=[
                pltpu.VMEM((count, 3 * cols, rows), BF16),
                pltpu.VMEM((count, cols, rows), BF16),
                pltpu.VMEM((count, heads, 1, rows), F32),
                pltpu.VMEM((count, cols, width), BF16),
                pltpu.VMEM((rows, width), BF16),
                pltpu.VMEM((cols, rows), BF16),
                pltpu.VMEM((3 * cols, rows), F32),
                pltpu.SemaphoreType.DMA((4, count)),
            ],
        ),
        out_shape=[
            jax.ShapeDtypeStruct((count, 3 * cols, rows), BF16),
            jax.ShapeDtypeStruct((count, 1, 3 * cols), F32),
        ],
        name="mixer_backward",
        **settings(16_000_000_000),
    )(place, start, tiles, segment, middle_grad, *operands)


class Line:
    def __init__(self, remote, near, ref, size, columns):
        self.near = near
        self.copies = []
        for hop in range(near.count - 1):
            pair = []
            for sign in (1, -1):
                origin = lax.rem(near.z_index - sign * hop + near.count, near.count)
                chunk = ref.at[near.core, :, pl.ds(pl.multiple_of(origin * size, size), size), columns]
                pair.append((sign, remote.copy(chunk, chunk, near.along(sign))))
            self.copies.append(pair)

    def each(self, hop, ahead, act):
        for sign, copy in self.copies[hop]:
            origin = self.near.z_index - sign * (hop + 1 - ahead)
            target = self.near.z_index + sign * ahead

            @pl.when((origin >= 0) & (origin < self.near.count) & (target >= 0) & (target < self.near.count))
            def _():
                act(copy)

    def start(self, hop):
        self.each(hop, 1, lambda copy: copy.start())

    def receive(self, hop):
        self.each(hop, 0, lambda copy: copy.wait_recv())

    def finish(self):
        for hop in range(self.near.count - 1):
            self.each(hop, 1, lambda copy: copy.wait_send())


def input_backward_kernel(hidden_ref, middle_grad_ref, norm_ref, projected, normed_in, *rest, saved, line, last):
    pieces = len(saved)
    rest = list(rest)
    mixeds = [rest.pop(0) for _ in range(pieces)]
    weights = [rest.pop(0) for _ in range(pieces)]
    feed_terms = [rest.pop(0) for _ in range(4)]
    if last:
        mixer_part1, feed_total1, other_grad = [rest.pop(0) for _ in range(3)]
        small_refs = [rest.pop(0) for _ in range(7)]
        feed_result, mixer_result, parts_result, vector_out = [rest.pop(0) for _ in range(4)]
    else:
        sums_ref, in_grad_ref, small_ref, feed_total_ref = [rest.pop(0) for _ in range(4)]
    projected_grad, mixed, normed, low_middle, weight, sent, came = [rest.pop(0) for _ in range(7)]
    feed_part, feed_came, sems, sends, receives = [rest.pop(0) for _ in range(5)]
    rows_all, width = hidden_ref.shape
    count = projected.shape[1]
    near = Neighbours(line)
    remote = Remote(sends, receives)
    everything = slice(None)
    devices = [near.twin] + near.line
    if last:
        devices += [near.beside, near.across, near.far]
        sums_ref, in_grad_ref = rest.pop(0), rest.pop(0)
    copies = []
    for i in range(pieces):
        copies.append(
            [
                pltpu.make_async_copy(
                    projected.at[i], projected_grad.at[i * count : (i + 1) * count], sems.at[0, i]
                ),
                pltpu.make_async_copy(mixeds[i].at[saved[i]], mixed.at[i], sems.at[1, i]),
                pltpu.make_async_copy(
                    weights[i].at[0:count], weight.at[i * count : (i + 1) * count], sems.at[2, i]
                ),
            ]
        )
    norm_copy = pltpu.make_async_copy(normed_in, normed, sems.at[3, 0])
    norm_copy.start()
    for i in ORDER:
        run_copies(copies[i])
    greet(devices)

    total = feed_terms[0][...].astype(F32)
    for term in feed_terms[1:]:
        total = total + term[...].astype(F32)
    feed_part[...] = total.astype(BF16)
    feed_line = line_copies(remote, near, feed_part, feed_came, everything)
    run_copies(feed_line)
    if last:
        part1_came = rest.pop(0)
        part1_line = line_copies(remote, near, mixer_part1, part1_came, everything)
        run_copies(part1_line)

    core_copies = [remote.copy(sent.at[slot], came.at[slot], near.twin) for slot in range(2)]
    low_middle[...] = middle_grad_ref[...].astype(BF16)
    norm_copy.wait()
    for index, piece in enumerate(ORDER):
        wait_copies(copies[piece])

        def grad_of(put, piece=piece):
            own = slice(piece * count, (piece + 1) * count)
            put((slice(0, count), everything), nn(projected_grad[own, :], normed[...]))
            put((slice(count, width), everything), nn(mixed[piece], low_middle[...]))

        def put(slot, where, value):
            sums_ref[(slot,) + where] = value

        sum_with_core(index, core_copies, grad_of, sent, came, put)

    if last:
        (
            mixer_came,
            mixer_part,
            line_came,
            feed_own,
            feed_other,
            mixer_own,
            mixer_other,
            feed_out,
            mixer_out,
            parts_out,
            vector,
            vector_came,
            locals_,
        ) = rest
        chunk_width = width // 2
        chunks = [slice(i * chunk_width, (i + 1) * chunk_width) for i in range(2)]
        plane = [plane_copies(remote, near, sums_ref, mixer_came, None, chunk) for chunk in chunks]
        for group in plane:
            run_copies(group)

    gain = jnp.zeros((1, width), F32)
    shift = jnp.zeros((1, width), F32)
    for rows in big_blocks(rows_all):
        scaled, inverse = normalise(hidden_ref[rows, :].astype(F32))
        gradient = tn(projected_grad[:, rows], weight[...])
        in_grad = middle_grad_ref[rows, :] + normalise_back(gradient, scaled, inverse, norm_ref[0:1, :])
        in_grad_ref[rows, :] = in_grad.astype(BF16)
        gain = gain + jnp.sum(gradient * scaled, axis=0, keepdims=True)
        shift = shift + jnp.sum(gradient, axis=0, keepdims=True)

    if not last:
        small_ref[0:1, :] = gain
        small_ref[1:2, :] = shift
        wait_copies(feed_line)
        feed_total_ref[...] = line_total(near, feed_part, feed_came, everything).astype(BF16)
        return

    first = near.section == 0

    def local(source, target, slot):
        return pltpu.make_async_copy(source, target, locals_.at[slot])

    def place_total(total0, total1, own_ref, other_ref, out_ref, chunk, slot):
        own_ref[:, chunk] = jnp.where(first, total0, total1).astype(BF16)
        other_ref[:, chunk] = jnp.where(first, total1, total0).astype(BF16)
        size = own_ref.shape[0]
        rows = pl.ds(pl.multiple_of(near.z_index * size, size), size)
        spot = out_ref.at[near.core, near.section, rows, chunk]
        keep = local(own_ref.at[:, chunk], spot, slot)
        keep.start()
        send = remote.copy(other_ref.at[:, chunk], spot, near.across)
        send.start()
        return [keep, send]

    small0, ups0, shifts0, small1, ups1, shifts1, in_small1 = small_refs
    vector[...] = jnp.zeros_like(vector)
    ins = ((gain, shift), (in_small1[0:1, :], in_small1[1:2, :]))
    for layer, (small, ups, shifts) in enumerate(((small0, ups0, shifts0), (small1, ups1, shifts1))):
        rows = [ins[layer][0], small[0:1, :], ins[layer][1], small[1:2, :], small[2:3, :], small[3:4, :]]
        for i, row in enumerate(rows):
            vector[layer, i : i + 1, :] = row
        for i in range(pieces):
            vector[layer, 8 + i : 9 + i, :] = ups[i]
            vector[layer, 12 + i : 13 + i, 0:count] = shifts[i]

    def vector_round(devices, at):
        group = [remote.copy(vector, vector_came.at[at + i], device) for i, device in enumerate(devices)]
        run_copies(group)
        return group

    def vector_sum(group, at):
        wait_copies(group)
        total = vector[...]
        for i in range(len(group)):
            total = total + vector_came[at + i]
        vector[...] = total

    pending = vector_round([near.twin], 0)
    wait_copies(feed_line)
    feed_total = line_total(near, feed_part, feed_came, everything)
    feed_pair = place_total(
        feed_total, feed_total1[...].astype(F32), feed_own, feed_other, feed_out, everything, 0
    )
    vector_sum(pending, 0)
    pending = vector_round([near.beside], 1)
    wait_copies(part1_line)
    half = mixer_part.shape[0]
    mine = pl.ds(pl.multiple_of(near.section * half, half), half)
    spreads = []
    for group, chunk in zip(plane, chunks):
        wait_copies(group)
        part = sums_ref[0, mine, chunk].astype(F32)
        for i in range(3):
            part = part + mixer_came[i, :, chunk].astype(F32)
        mixer_part[:, chunk] = part.astype(BF16)
        spreads.append(line_copies(remote, near, mixer_part, line_came, chunk))
        run_copies(spreads[-1])
    rows = rows_all // 2
    inner = pl.ds(pl.multiple_of(near.lane * rows, rows), rows)
    outer = pl.ds(pl.multiple_of((1 - near.lane) * rows, rows), rows)
    spot = parts_out.at[2 * near.section + near.lane]
    at = remote.reserve(3)

    def grad_copies(own, other):
        return [
            remote.copy(own.at[outer], spot, near.beside, at),
            remote.copy(other.at[inner], spot, near.across, at + 1),
            remote.copy(other.at[outer], spot, near.far, at + 2),
        ]

    @pl.when(first)
    def _():
        run_copies([local(in_grad_ref.at[inner], spot, 3)] + grad_copies(in_grad_ref, other_grad))

    @pl.when(near.section == 1)
    def _():
        run_copies([local(other_grad.at[inner], spot, 3)] + grad_copies(other_grad, in_grad_ref))

    feed_size, mixer_size = feed_own.shape[0], mixer_own.shape[0]
    feed_chain = Line(remote, near, feed_out, feed_size, everything)
    mixer_chains = [Line(remote, near, mixer_out, mixer_size, chunk) for chunk in chunks]
    wait_copies(feed_pair)
    feed_chain.start(0)
    vector_sum(pending, 1)
    pending = vector_round([near.across], 2)
    pairs = []
    for i, chunk in enumerate(chunks):
        wait_copies(spreads[i])
        total0 = line_total(near, mixer_part, line_came, chunk)
        total1 = line_total(near, mixer_part1, part1_came, chunk)
        pairs.append(place_total(total0, total1, mixer_own, mixer_other, mixer_out, chunk, 1 + i))
    vector_sum(pending, 2)
    pending = vector_round(near.line, 3)
    feed_chain.receive(0)
    feed_chain.start(1)
    for pair, chain in zip(pairs, mixer_chains):
        wait_copies(pair)
        chain.start(0)
    vector_sum(pending, 3)
    vector_out[...] = jnp.where(first, vector[0], vector[1])
    for hop in range(1, line - 1):
        feed_chain.receive(hop)
        if hop + 1 < line - 1:
            feed_chain.start(hop + 1)
        for chain in mixer_chains:
            chain.receive(hop - 1)
            chain.start(hop)
    feed_twin = remote.copy(feed_out.at[near.core], feed_out.at[near.core], near.twin)
    feed_twin.start()
    for chain in mixer_chains:
        chain.receive(line - 2)
    mixer_twin = remote.copy(mixer_out.at[near.core], mixer_out.at[near.core], near.twin)
    mixer_twin.start()
    feed_twin.wait()
    feed_chain.finish()
    results = [local(feed_out, feed_result, 4), local(parts_out, parts_result, 5), local(mixer_out, mixer_result, 6)]
    results[0].start()
    for copy in grad_copies(in_grad_ref, other_grad):
        copy.wait()
    local(in_grad_ref.at[inner], spot, 3).wait()
    results[1].start()
    mixer_twin.wait()
    for chain in mixer_chains:
        chain.finish()
    results[2].start()
    wait_copies(results)


def input_backward(
    hidden, middle_grad, norm, projected, normed, mixeds, saved, weights, feed_terms, collective, finish=None
):
    rows, width = hidden.shape
    number, count, _ = projected.shape
    line = lax.axis_size("dp") // 2
    vmem = pl.BlockSpec(memory_space=pltpu.VMEM)
    far = pl.BlockSpec(memory_space=pl.ANY)
    operands = [hidden, middle_grad, norm, projected, normed, *mixeds, *weights, *feed_terms]
    specs = [vmem] * 3 + [far] * (2 + 2 * number) + [vmem] * 4
    feed_rows, half = width // line, width // 2
    mixer_rows = half // line
    scratch = [
        pltpu.VMEM((number * count, rows), BF16),
        pltpu.VMEM((number, width - count, rows), BF16),
        pltpu.VMEM((rows, width), BF16),
        pltpu.VMEM((rows, width), BF16),
        pltpu.VMEM((number * count, width), BF16),
        pltpu.VMEM((2, width, width), BF16),
        pltpu.VMEM((2, width, width), BF16),
        pltpu.VMEM((width, width), BF16),
        pltpu.VMEM((line - 1, feed_rows, width), BF16),
        pltpu.SemaphoreType.DMA((4, number)),
        pltpu.SemaphoreType.DMA((64,)),
        pltpu.SemaphoreType.DMA((64,)),
    ]
    if finish is None:
        outs = [
            jax.ShapeDtypeStruct((2, width, width), BF16),
            jax.ShapeDtypeStruct((rows, width), BF16),
            jax.ShapeDtypeStruct((2, width), F32),
            jax.ShapeDtypeStruct((feed_rows, width), BF16),
        ]
        out_specs = [vmem] * 4
    else:
        operands += list(finish)
        specs += [vmem, vmem, far] + [vmem] * (len(finish) - 3)
        outs = [
            jax.ShapeDtypeStruct((2, 2, width, width), BF16),
            jax.ShapeDtypeStruct((2, 2, half, width), BF16),
            jax.ShapeDtypeStruct((4, rows // 2, width), BF16),
            jax.ShapeDtypeStruct((16, width), F32),
        ]
        out_specs = [far] * 3 + [vmem]
        scratch += [
            pltpu.VMEM((2, width, width), BF16),
            pltpu.VMEM((rows, width), BF16),
            pltpu.VMEM((line - 1, mixer_rows, width), BF16),
            pltpu.VMEM((3, half, width), BF16),
            pltpu.VMEM((half, width), BF16),
            pltpu.VMEM((line - 1, mixer_rows, width), BF16),
            pltpu.VMEM((feed_rows, width), BF16),
            pltpu.VMEM((feed_rows, width), BF16),
            pltpu.VMEM((mixer_rows, width), BF16),
            pltpu.VMEM((mixer_rows, width), BF16),
            pltpu.VMEM((2, 2, width, width), BF16),
            pltpu.VMEM((2, 2, half, width), BF16),
            pltpu.VMEM((4, rows // 2, width), BF16),
            pltpu.VMEM((2, 16, width), F32),
            pltpu.VMEM((2 + line, 2, 16, width), F32),
            pltpu.SemaphoreType.DMA((8,)),
        ]
    return pl.pallas_call(
        functools.partial(input_backward_kernel, saved=saved, line=line, last=finish is not None),
        in_specs=specs,
        out_specs=out_specs,
        scratch_shapes=scratch,
        out_shape=outs,
        name="input_backward",
        **settings(8_000_000_000, collective),
    )(*operands)


def place_states_kernel(place_ref, *rest):
    parts, out_ref, held, sems = rest[:4], rest[4], rest[5], rest[6]
    inward = [pltpu.make_async_copy(part, held.at[i], sems.at[0, i]) for i, part in enumerate(parts)]
    outward = [
        pltpu.make_async_copy(held.at[i], out_ref.at[place_ref[2] ^ i], sems.at[1, i]) for i in range(len(parts))
    ]
    run_copies(inward)
    for first, second in zip(inward, outward):
        first.wait()
        second.start()
    wait_copies(outward)


def place_states(place, parts):
    far = pl.BlockSpec(memory_space=pl.ANY)
    return pl.pallas_call(
        place_states_kernel,
        grid_spec=pltpu.PrefetchScalarGridSpec(
            num_scalar_prefetch=1,
            grid=(1,),
            in_specs=[far] * 4,
            out_specs=far,
            scratch_shapes=[
                pltpu.VMEM((4,) + parts[0].shape, BF16),
                pltpu.SemaphoreType.DMA((2, 4)),
            ],
        ),
        out_shape=jax.ShapeDtypeStruct((4,) + parts[0].shape, BF16),
        name="place_states",
        **settings(1_000_000),
    )(place, *parts)


def widen_kernel(low_ref, out_ref):
    out_ref[...] = low_ref[...].astype(F32)


def widen(parts):
    number, rows, width = parts.shape
    spec = pl.BlockSpec((1, rows, width), lambda i: (i, 0, 0))
    return pl.pallas_call(
        widen_kernel,
        grid=(number,),
        in_specs=[spec],
        out_specs=spec,
        out_shape=jax.ShapeDtypeStruct(parts.shape, F32),
        name="widen",
        **settings(1_000_000),
    )(parts)


def unpack_kernel(feed_ref, mixer_ref, qkv_ref, out_ref, up_ref, down_ref):
    width = feed_ref.shape[2]
    part = width // 4
    for core in range(2):
        up_ref[:, core * width : (core + 1) * width] = feed_ref[core, 0].astype(F32)
        down_ref[core * width : (core + 1) * width, :] = feed_ref[core, 1].astype(F32).T
        out_ref[core * part : (core + 1) * part, :] = mixer_ref[core, 3 * part :, :].astype(F32)
    for third in range(3):
        rows = slice(third * part, (third + 1) * part)
        both = jnp.concatenate([mixer_ref[0, rows, :], mixer_ref[1, rows, :]], axis=0)
        qkv_ref[third] = both.astype(F32).T


def unpack(feed, mixer):
    width = feed.shape[2]
    half = width // 2
    return pl.pallas_call(
        unpack_kernel,
        out_shape=[
            jax.ShapeDtypeStruct((3, width, half), F32),
            jax.ShapeDtypeStruct((half, width), F32),
            jax.ShapeDtypeStruct((width, 2 * width), F32),
            jax.ShapeDtypeStruct((2 * width, width), F32),
        ],
        name="unpack",
        compiler_params=pltpu.CompilerParams(vmem_limit_bytes=VMEM_LIMIT),
    )(feed, mixer)


def route(change):
    shape = [lax.axis_size(axis) for axis in AXES]
    pairs = []
    for s in range(shape[0]):
        for d in range(shape[1]):
            for t in range(shape[2]):
                to = change(s, d, t)
                if to is not None:
                    pairs.append(((s * shape[1] + d) * shape[2] + t, (to[0] * shape[1] + to[1]) * shape[2] + to[2]))
    return pairs


def moved(block, change):
    return lax.ppermute(block, AXES, route(change))


def over_tensor(s, d, t):
    return (s, d, 1 - t)


def over_section(s, d, t):
    return (1 - s, d, t)


def over_both(s, d, t):
    return (1 - s, d, 1 - t)


def over_core(s, d, t):
    return (s, d ^ 1, t)


def along_z(distance):
    count = lax.axis_size("dp") // 2
    return lambda s, d, t: (s, (d // 2 + distance) % count * 2 + d % 2, t)


def tie(*values):
    return lax.optimization_barrier(values)


def take_part(block, which, count, axis=0):
    size = block.shape[axis] // count
    return lax.dynamic_slice_in_dim(block, which * size, size, axis)


def added(*terms):
    total = terms[0].astype(F32)
    for term in terms[1:]:
        total = total + term.astype(F32)
    return total.astype(terms[0].dtype)


def reordered(pieces, lane, core):
    pieces = jnp.where(lane == 0, pieces, pieces[jnp.array([2, 3, 0, 1])])
    return jnp.where(core == 0, pieces, pieces[jnp.array([1, 0, 3, 2])])


def one_sequence_each(
    inputs,
    cotangent,
    segment_ids,
    norm_gains,
    norm_biases,
    qkv_weight,
    qv_bias,
    out_weight,
    up_weight,
    up_bias,
    down_weight,
    out_biases,
):
    section = lax.axis_index("section")
    group = lax.axis_index("dp")
    lane = lax.axis_index("tensor")
    core = group % 2
    z_index = group // 2
    z_count = lax.axis_size("dp") // 2
    width = inputs.shape[2]
    hidden = up_bias.shape[1]
    cols = qkv_weight.shape[3]
    part = cols // 2
    mine = 2 * section + lane

    def own_half(array, axis):
        return take_part(array, core, 2, axis)

    mixer_own = jnp.concatenate(
        [
            own_half(qkv_weight[0], 2).transpose(0, 2, 1).reshape(3 * part, width),
            own_half(out_weight[0], 0),
        ],
        axis=0,
    )
    up_own = own_half(up_weight[0], 1)
    down_own = own_half(down_weight[0], 0)
    small = jnp.concatenate(
        [item.reshape(-1) for item in (norm_gains, norm_biases, qv_bias, up_bias, out_biases)]
    )

    def sequence_halves(array):
        kept = lax.dynamic_index_in_dim(array, mine, 0, keepdims=False)
        sent = lax.dynamic_index_in_dim(array, 2 * section + 1 - lane, 0, keepdims=False)
        return kept, sent

    def joined(kept, came):
        return jnp.where(lane == 0, jnp.concatenate([kept, came], 0), jnp.concatenate([came, kept], 0))

    segment = lax.dynamic_index_in_dim(segment_ids, mine, 0, keepdims=True)
    ids = jnp.arange(IMAGE_IDS, dtype=jnp.int32)[:, None]
    begin = jnp.sum((segment < ids).astype(jnp.int32), axis=1)
    end = jnp.sum((segment <= ids).astype(jnp.int32), axis=1)
    start = begin // TILE
    place = jnp.stack([lane, core, mine]).astype(jnp.int32)
    images = (place, start, (end - 1) // TILE - start + 1, segment)

    def params(vector):
        gains = vector[: 2 * width].reshape(2, width)
        shifts = vector[2 * width : 4 * width].reshape(2, width)
        qv = vector[4 * width : 6 * width].reshape(2, 4, part)
        up_shift = vector[6 * width : 6 * width + hidden].reshape(4, 1, hidden // 4)
        outs = vector[6 * width + hidden :].reshape(2, 1, width)
        zero = jnp.zeros((4, part), F32)
        qkv_shift = jnp.concatenate([qv[0], zero, qv[1]], axis=1)
        norms = [jnp.stack([gains[i], shifts[i]]) for i in range(2)]
        return norms, qkv_shift[:, :, None], up_shift, outs

    def by_layer(own, came):
        return jnp.where(section == 0, own, came), jnp.where(section == 1, own, came)

    kept, sent = sequence_halves(inputs)
    came, mixer_came, small_came = tie(
        moved(sent, over_tensor), moved(mixer_own, over_section), moved(small, over_section)
    )
    state = joined(kept, came)
    mixers = by_layer(mixer_own, mixer_came)
    layer_params = [params(vector) for vector in by_layer(small, small_came)]
    mixer_pieces = [[mixers[0], moved(mixers[0], over_core)], None]
    norms, qkv_shift, up_shift, outs = layer_params[0]
    mixer_a, beside, up_came = tie(
        mixer_forward(images, state, norms[0], qkv_shift, mixer_pieces[0]),
        moved(mixers[0], over_tensor),
        moved(up_own, over_section),
    )
    ups = by_layer(up_own, up_came)
    mixer_pieces[0] = mixer_pieces[0] + [beside, moved(beside, over_core)]
    mixer_b, up_beside, up_twin, down_came = tie(
        mixer_forward(
            images,
            state,
            norms[0],
            qkv_shift,
            mixer_pieces[0][2:],
            2,
            (mixer_a[3], mixer_a[1]),
            mixer_pieces[0],
            outs[0],
        ),
        moved(ups[0], over_tensor),
        moved(ups[0], over_core),
        moved(down_own, over_section),
    )
    downs = by_layer(down_own, down_came)
    down_twin = moved(downs[0], over_core)
    feed_a, down_beside, up_corner = tie(
        feed_forward(
            place, mixer_b[3], norms[1], up_shift, outs[1], [ups[0], up_twin], [downs[0], down_twin], 0, False
        ),
        moved(downs[0], over_tensor),
        moved(up_beside, over_core),
    )
    up_pieces = [[ups[0], up_twin, up_beside, up_corner], None]
    down_pieces = [[downs[0], down_twin, down_beside, moved(down_beside, over_core)], None]
    feed_b, beside, twin = tie(
        feed_forward(
            place, mixer_b[3], norms[1], up_shift, feed_a[0], up_pieces[0][2:], down_pieces[0][2:], 2, True
        ),
        moved(mixers[1], over_tensor),
        moved(mixers[1], over_core),
    )
    first_out = feed_b[0]
    saved = [
        dict(
            state=state,
            normed=mixer_a[3],
            qkv=[mixer_a[0], mixer_a[0], mixer_b[0], mixer_b[0]],
            mixed=[mixer_a[1], mixer_a[1], mixer_b[1], mixer_b[1]],
            totals=[mixer_a[2], mixer_a[2], mixer_b[2], mixer_b[2]],
            at=[0, 1, 0, 1],
            middle=mixer_b[3],
            active=[feed_a[1], feed_a[1], feed_b[1], feed_b[1]],
            slope=[feed_a[2], feed_a[2], feed_b[2], feed_b[2]],
        )
    ]
    norms, qkv_shift, up_shift, outs = layer_params[1]
    mixer_pieces[1] = [mixers[1], twin, beside, moved(beside, over_core)]
    mixer_a, up_beside, up_twin, down_beside, down_twin = tie(
        mixer_forward(images, first_out, norms[0], qkv_shift, mixer_pieces[1], 0, None, mixer_pieces[1], outs[0]),
        moved(ups[1], over_tensor),
        moved(ups[1], over_core),
        moved(downs[1], over_tensor),
        moved(downs[1], over_core),
    )
    up_pieces[1] = [ups[1], up_twin, up_beside, moved(up_beside, over_core)]
    down_pieces[1] = [downs[1], down_twin, down_beside, moved(down_beside, over_core)]
    grad_kept, grad_sent = sequence_halves(cotangent)
    feed_a, grad_came = tie(
        feed_forward(place, mixer_a[4], norms[1], up_shift, outs[1], up_pieces[1], down_pieces[1], 0, True),
        moved(grad_sent, over_tensor),
    )
    second_out = feed_a[0]
    saved.append(
        dict(
            state=first_out,
            normed=mixer_a[3],
            qkv=[mixer_a[0]] * 4,
            mixed=[mixer_a[1]] * 4,
            totals=[mixer_a[2]] * 4,
            at=[0, 1, 2, 3],
            middle=mixer_a[4],
            active=[feed_a[1]] * 4,
            slope=[feed_a[2]] * 4,
        )
    )
    grad = joined(grad_kept, grad_came)

    def exchange(own, other):
        return [
            take_part(own, lane, 2),
            moved(take_part(own, 1 - lane, 2), over_tensor),
            moved(take_part(other, lane, 2), over_section),
            moved(take_part(other, 1 - lane, 2), over_both),
        ]

    out_parts = exchange(
        jnp.where(section == 0, first_out, second_out), jnp.where(section == 0, second_out, first_out)
    )

    def feed_back(layer, grad, rider=None):
        kept = saved[layer]
        return feed_backward(
            grad,
            kept["middle"],
            layer_params[layer][0][1],
            kept["active"],
            kept["slope"],
            kept["at"],
            up_pieces[layer],
            down_pieces[layer],
            layer,
            rider,
        )

    def mixer_back(layer, middle_grad):
        kept = saved[layer]
        return mixer_backward(
            images, middle_grad, kept["qkv"], kept["mixed"], kept["totals"], kept["at"], mixer_pieces[layer]
        )

    def input_back(layer, middle_grad, projected, feed_terms, finish=None):
        kept = saved[layer]
        return input_backward(
            kept["state"],
            middle_grad,
            layer_params[layer][0][0],
            projected,
            kept["normed"],
            kept["mixed"],
            kept["at"],
            mixer_pieces[layer],
            feed_terms,
            2 + layer,
            finish,
        )

    def send_plane(blocks):
        return [
            moved(block, change) for block, change in zip(blocks, (over_tensor, over_section, over_both))
        ]

    feed1, out_parts = tie(feed_back(1, grad), out_parts)
    mixer1, came = tie(mixer_back(1, feed1[5]), send_plane(feed1[1:4]))
    mixer_sums1, in_grad1, in_small1, feed_total1 = input_back(1, feed1[5], mixer1[0], [feed1[0], *came])
    feed0 = feed_back(0, in_grad1, mixer_sums1)
    mixer0, came = tie(mixer_back(0, feed0[5]), send_plane(feed0[1:4]))
    feed_sum, mixer_sum, in_parts, vector = input_back(
        0,
        feed0[5],
        mixer0[0],
        [feed0[0], *came],
        [
            feed0[7],
            feed_total1,
            in_grad1,
            feed0[6],
            feed0[4],
            mixer0[1],
            feed1[6],
            feed1[4],
            mixer1[1],
            in_small1,
        ],
    )
    qkv_grad, out_grad, up_grad, down_grad = unpack(feed_sum, mixer_sum.reshape(2, 4 * part, width))
    states = place_states(place, out_parts)
    grads = widen(in_parts)
    qv_grad = vector[12:16, : 3 * part].reshape(4, 3, part)
    return (
        states[None],
        grads[None],
        vector[0:2][None],
        vector[2:4][None],
        qkv_grad[None],
        jnp.stack([qv_grad[:, 0].reshape(width), qv_grad[:, 2].reshape(width)])[None],
        out_grad[None],
        up_grad[None],
        vector[8:12].reshape(1, hidden),
        down_grad[None],
        vector[4:6][None],
    )


def passed_along(block, axis, distance):
    devices = range(lax.axis_size(axis))
    route = [(i - distance, i) for i in devices if i - distance in devices]
    return lax.ppermute(block, axis, route)


def norm_parts(token_rows, gain_row, shift_row):
    centre = token_rows - jnp.mean(token_rows, axis=-1, keepdims=True)
    inverse = lax.rsqrt(jnp.mean(centre * centre, axis=-1, keepdims=True) + EPSILON)
    scaled = centre * inverse
    return (scaled * gain_row + shift_row, scaled, inverse)


def norm_back(gradient, scaled, inverse, gain_row):
    upstream = gradient * gain_row
    return inverse * (
        upstream
        - jnp.mean(upstream, axis=-1, keepdims=True)
        - scaled * jnp.mean(upstream * scaled, axis=-1, keepdims=True)
    )


def gelu_exact(values):
    return jax.nn.gelu(values, approximate=False)


def head_view(matrix, heads_local):
    return matrix.reshape(matrix.shape[0], heads_local, HEAD_DIM)


def join_heads(stacked):
    return stacked.transpose(1, 0, 2).reshape(stacked.shape[1], stacked.shape[0] * stacked.shape[2])


def attend_forward(queries, key_rows, value_rows, segment):
    seq_len = queries.shape[0]
    half_rows = seq_len // 2
    heads_local = queries.shape[1] // HEAD_DIM
    scaling = HEAD_DIM ** (-0.5)
    query_heads = head_view(queries, heads_local)
    key_heads = head_view(key_rows, heads_local)
    value_heads = head_view(value_rows, heads_local)

    def one_item(item):
        head_index = item // 2
        row_start = item % 2 * half_rows
        head_keys = lax.dynamic_index_in_dim(key_heads, head_index, 1, keepdims=False)
        head_values = lax.dynamic_index_in_dim(value_heads, head_index, 1, keepdims=False)
        head_queries = lax.dynamic_index_in_dim(query_heads, head_index, 1, keepdims=False)
        block_queries = lax.dynamic_slice_in_dim(head_queries, row_start, half_rows, 0)
        block_segment = lax.dynamic_slice_in_dim(segment, row_start, half_rows, 0)
        scores = (
            jnp.einsum("qd,kd->qk", block_queries, head_keys, preferred_element_type=jnp.float32)
            * scaling
        )
        scores = jnp.where(block_segment[:, None] == segment[None, :], scores, NEGATIVE)
        row_peak = jnp.max(scores, axis=-1, keepdims=True)
        expanded = jnp.exp(scores - row_peak)
        denominator = jnp.sum(expanded, axis=-1, keepdims=True)
        weights = (expanded / denominator).astype(jnp.bfloat16)
        block_out = jnp.dot(weights, head_values, preferred_element_type=jnp.float32).astype(
            jnp.bfloat16
        )
        return (block_out, row_peak[:, 0] + jnp.log(denominator[:, 0]))

    outputs, log_totals = lax.map(one_item, jnp.arange(2 * heads_local, dtype=jnp.int32))
    mixed_rows = join_heads(outputs.reshape(heads_local, seq_len, HEAD_DIM))
    return (mixed_rows, log_totals.reshape(heads_local, seq_len))


def attend_backward(queries, key_rows, value_rows, mixed_grad, log_totals, segment):
    seq_len = queries.shape[0]
    half_rows = seq_len // 2
    heads_local = queries.shape[1] // HEAD_DIM
    scaling = HEAD_DIM ** (-0.5)
    query_heads = head_view(queries, heads_local)
    key_heads = head_view(key_rows, heads_local)
    value_heads = head_view(value_rows, heads_local)
    grad_heads = head_view(mixed_grad, heads_local)

    def one_head(head_index):
        head_queries = lax.dynamic_index_in_dim(query_heads, head_index, 1, keepdims=False)
        head_keys = lax.dynamic_index_in_dim(key_heads, head_index, 1, keepdims=False)
        head_values = lax.dynamic_index_in_dim(value_heads, head_index, 1, keepdims=False)
        head_grads = lax.dynamic_index_in_dim(grad_heads, head_index, 1, keepdims=False)
        head_totals = lax.dynamic_index_in_dim(log_totals, head_index, 0, keepdims=False)

        def one_block(carry, block_index):
            key_grad, value_grad = carry
            row_start = block_index * half_rows
            block_queries = lax.dynamic_slice_in_dim(head_queries, row_start, half_rows, 0)
            block_grads = lax.dynamic_slice_in_dim(head_grads, row_start, half_rows, 0)
            block_totals = lax.dynamic_slice_in_dim(head_totals, row_start, half_rows, 0)
            block_segment = lax.dynamic_slice_in_dim(segment, row_start, half_rows, 0)
            scores = (
                jnp.einsum(
                    "qd,kd->qk", block_queries, head_keys, preferred_element_type=jnp.float32
                )
                * scaling
            )
            scores = jnp.where(block_segment[:, None] == segment[None, :], scores, NEGATIVE)
            weights = jnp.exp(scores - block_totals[:, None])
            low_weights = weights.astype(jnp.bfloat16)
            block_out = jnp.dot(
                low_weights, head_values, preferred_element_type=jnp.float32
            ).astype(jnp.bfloat16)
            weight_grads = jnp.einsum(
                "qd,kd->qk", block_grads, head_values, preferred_element_type=jnp.float32
            )
            row_terms = jnp.sum(weights * weight_grads, axis=-1, keepdims=True)
            score_grads = (weights * (weight_grads - row_terms)).astype(jnp.bfloat16)
            query_grad = (
                jnp.dot(score_grads, head_keys, preferred_element_type=jnp.float32) * scaling
            )
            key_grad = (
                key_grad
                + jnp.einsum(
                    "qk,qd->kd", score_grads, block_queries, preferred_element_type=jnp.float32
                )
                * scaling
            )
            value_grad = value_grad + jnp.einsum(
                "qk,qd->kd", low_weights, block_grads, preferred_element_type=jnp.float32
            )
            return ((key_grad, value_grad), (block_out, query_grad))

        empty = jnp.zeros((seq_len, HEAD_DIM), jnp.float32)
        (key_grad, value_grad), (block_outs, query_grads) = lax.scan(
            one_block, (empty, empty), jnp.arange(2, dtype=jnp.int32)
        )
        return (
            block_outs.reshape(seq_len, HEAD_DIM),
            query_grads.reshape(seq_len, HEAD_DIM),
            key_grad,
            value_grad,
        )

    results = lax.map(one_head, jnp.arange(heads_local, dtype=jnp.int32))
    return tuple((join_heads(item) for item in results))


def store_at(array, value, which, running):
    return array.at[which].set(jnp.where(running, value, array[which]))


def pipelined(
    inputs,
    cotangent,
    segment_ids,
    norm_gains,
    norm_biases,
    qkv_weight,
    qv_bias,
    out_weight,
    up_weight,
    up_bias,
    down_weight,
    out_biases,
):
    section_index = lax.axis_index("section")
    section_count = lax.axis_size("section")
    lane_index = lax.axis_index("tensor")
    micro_count, own_rows, model_width = inputs.shape
    seq_len = segment_ids.shape[1]
    cols_local = qkv_weight.shape[3]
    hidden_local = up_weight.shape[2]
    heads_local = cols_local // HEAD_DIM
    gain_rows = norm_gains[0]
    shift_rows = norm_biases[0]
    joined = jnp.concatenate([qkv_weight[0, 0], qkv_weight[0, 1], qkv_weight[0, 2]], axis=1)
    query_shift = lax.dynamic_slice_in_dim(qv_bias[0, 0], lane_index * cols_local, cols_local)
    value_shift = lax.dynamic_slice_in_dim(qv_bias[0, 1], lane_index * cols_local, cols_local)
    up_shift = lax.dynamic_slice_in_dim(up_bias[0], lane_index * hidden_local, hidden_local)
    out_matrix = out_weight[0]
    up_matrix = up_weight[0]
    down_matrix = down_weight[0]
    mixer_shift = out_biases[0, 0]
    feed_shift = out_biases[0, 1]

    def spread_rows(normed_rows, weight):
        return (
            None,
            jnp.dot(
                lax.all_gather(normed_rows, "tensor", axis=0, tiled=True),
                weight,
                preferred_element_type=jnp.float32,
            ),
        )

    def regather(normed_rows):
        return lax.all_gather(normed_rows, "tensor", axis=0, tiled=True)

    def gather_grads(grad_rows):
        return lax.all_gather(grad_rows.astype(jnp.bfloat16), "tensor", axis=0, tiled=True)

    def branch_sum(left_rows, weight):
        return lax.psum_scatter(
            jnp.dot(left_rows, weight, preferred_element_type=jnp.float32).astype(jnp.bfloat16),
            "tensor",
            scatter_dimension=0,
            tiled=True,
        ).astype(jnp.float32)

    def input_sum(grad_rows, weight):
        return lax.psum_scatter(
            jnp.einsum("sc,dc->sd", grad_rows, weight, preferred_element_type=jnp.float32).astype(
                jnp.bfloat16
            ),
            "tensor",
            scatter_dimension=0,
            tiled=True,
        ).astype(jnp.float32)

    def split_projected(projected):
        queries = (projected[:, :cols_local] + query_shift).astype(jnp.bfloat16)
        key_rows = projected[:, cols_local : 2 * cols_local].astype(jnp.bfloat16)
        value_rows = (projected[:, 2 * cols_local :] + value_shift).astype(jnp.bfloat16)
        return (queries, key_rows, value_rows)

    def layer_backward(block_in, middle, log_totals, segment, out_grad):
        residual = block_in.astype(jnp.float32)
        full_grad = gather_grads(out_grad)
        normed_two, scaled_two, inverse_two = norm_parts(middle, gain_rows[1], shift_rows[1])
        normed_two = normed_two.astype(jnp.bfloat16)
        full_two = regather(normed_two)
        hidden = jnp.dot(full_two, up_matrix, preferred_element_type=jnp.float32) + up_shift
        active, gelu_pullback = jax.vjp(gelu_exact, hidden)
        active = active.astype(jnp.bfloat16)
        down_grad = jnp.einsum("sf,sd->fd", active, full_grad, preferred_element_type=jnp.float32)
        active_grad = jnp.einsum(
            "sd,fd->sf", full_grad, down_matrix, preferred_element_type=jnp.float32
        )
        hidden_grad = gelu_pullback(active_grad)[0]
        up_shift_grad = jnp.sum(hidden_grad, axis=0)
        hidden_low = hidden_grad.astype(jnp.bfloat16)
        up_grad = jnp.einsum("sd,sf->df", full_two, hidden_low, preferred_element_type=jnp.float32)
        normed_grad_two = input_sum(hidden_low, up_matrix)
        feed_shift_grad = jnp.sum(out_grad, axis=0)
        middle_grad = out_grad + norm_back(normed_grad_two, scaled_two, inverse_two, gain_rows[1])
        gain_two = jnp.sum(normed_grad_two * scaled_two, axis=0)
        shift_two = jnp.sum(normed_grad_two, axis=0)
        full_mid_grad = gather_grads(middle_grad)
        normed_one, scaled_one, inverse_one = norm_parts(residual, gain_rows[0], shift_rows[0])
        normed_one = normed_one.astype(jnp.bfloat16)
        full_one = regather(normed_one)
        projected = jnp.dot(full_one, joined, preferred_element_type=jnp.float32)
        queries, key_rows, value_rows = split_projected(projected)
        mixed_grad = jnp.einsum(
            "sd,cd->sc", full_mid_grad, out_matrix, preferred_element_type=jnp.float32
        ).astype(jnp.bfloat16)
        mixed_rows, query_grad, key_grad, value_grad = attend_backward(
            queries, key_rows, value_rows, mixed_grad, log_totals, segment
        )
        out_grad_matrix = jnp.einsum(
            "sc,sd->cd", mixed_rows, full_mid_grad, preferred_element_type=jnp.float32
        )
        mixer_shift_grad = jnp.sum(middle_grad, axis=0)
        qkv_low = jnp.concatenate([query_grad, key_grad, value_grad], axis=1).astype(jnp.bfloat16)
        joined_grad = jnp.einsum("sd,sc->dc", full_one, qkv_low, preferred_element_type=jnp.float32)
        normed_grad_one = input_sum(qkv_low, joined)
        in_grad = middle_grad + norm_back(normed_grad_one, scaled_one, inverse_one, gain_rows[0])
        gain_one = jnp.sum(normed_grad_one * scaled_one, axis=0)
        shift_one = jnp.sum(normed_grad_one, axis=0)
        qv_local = jnp.stack([jnp.sum(query_grad, axis=0), jnp.sum(value_grad, axis=0)])
        qv_full = lax.dynamic_update_slice_in_dim(
            jnp.zeros((2, model_width), jnp.float32), qv_local, lane_index * cols_local, 1
        )
        up_full = lax.dynamic_update_slice_in_dim(
            jnp.zeros((up_bias.shape[1],), jnp.float32), up_shift_grad, lane_index * hidden_local, 0
        )
        weight_terms = (joined_grad, out_grad_matrix, up_grad, down_grad)
        small_terms = (
            jnp.stack([gain_one, gain_two]),
            jnp.stack([shift_one, shift_two]),
            qv_full,
            up_full,
            jnp.stack([mixer_shift_grad, feed_shift_grad]),
        )
        return (in_grad, weight_terms, small_terms)

    ticks = micro_count + section_count - 1
    received = jnp.zeros((own_rows, model_width), jnp.bfloat16)
    saved_in = jnp.zeros_like(inputs)
    saved_mid = jnp.zeros((micro_count, own_rows, model_width), jnp.float32)
    saved_totals = jnp.zeros((micro_count, heads_local, seq_len), jnp.float32)
    states = jnp.zeros_like(inputs)
    for tick in range(ticks):
        micro = tick - section_index
        running = (micro >= 0) & (micro < micro_count)
        which = jnp.clip(micro, 0, micro_count - 1)
        own_in = lax.dynamic_index_in_dim(inputs, which, 0, keepdims=False)
        block_in = jnp.where(section_index == 0, own_in, received)
        segment = lax.dynamic_index_in_dim(segment_ids, which, 0, keepdims=False)
        layer_residual = block_in.astype(jnp.float32)
        layer_normed_one = norm_parts(layer_residual, gain_rows[0], shift_rows[0])[0].astype(
            jnp.bfloat16
        )
        layer_full_one, layer_projected = spread_rows(layer_normed_one, joined)
        layer_queries, layer_key_rows, layer_value_rows = split_projected(layer_projected)
        layer_mixed_rows, layer_log_totals = attend_forward(
            layer_queries, layer_key_rows, layer_value_rows, segment
        )
        layer_middle = layer_residual + branch_sum(layer_mixed_rows, out_matrix) + mixer_shift
        layer_normed_two = norm_parts(layer_middle, gain_rows[1], shift_rows[1])[0].astype(
            jnp.bfloat16
        )
        layer_full_two, layer_hidden = spread_rows(layer_normed_two, up_matrix)
        layer_active = gelu_exact(layer_hidden + up_shift).astype(jnp.bfloat16)
        block_out = layer_middle + branch_sum(layer_active, down_matrix) + feed_shift
        block_out, middle, log_totals, full_one, full_two = (
            block_out,
            layer_middle,
            layer_log_totals,
            layer_full_one,
            layer_full_two,
        )
        handed = block_out.astype(jnp.bfloat16)
        saved_in = store_at(saved_in, block_in, which, running)
        saved_mid = store_at(saved_mid, middle, which, running)
        saved_totals = store_at(saved_totals, log_totals, which, running)
        states = store_at(states, handed, which, running)
        if tick + 1 < ticks:
            received = passed_along(handed, "section", 1)
    back_received = jnp.zeros((own_rows, model_width), jnp.bfloat16)
    weight_totals = (
        jnp.zeros(joined.shape, jnp.float32),
        jnp.zeros(out_matrix.shape, jnp.float32),
        jnp.zeros(up_matrix.shape, jnp.float32),
        jnp.zeros(down_matrix.shape, jnp.float32),
    )
    small_totals = (
        jnp.zeros((2, model_width), jnp.float32),
        jnp.zeros((2, model_width), jnp.float32),
        jnp.zeros((2, model_width), jnp.float32),
        jnp.zeros((up_bias.shape[1],), jnp.float32),
        jnp.zeros((2, model_width), jnp.float32),
    )
    grads_store = jnp.zeros((micro_count, own_rows, model_width), jnp.float32)
    for tick in range(ticks):
        micro = tick - (section_count - 1) + section_index
        running = (micro >= 0) & (micro < micro_count)
        which = jnp.clip(micro, 0, micro_count - 1)
        own_grad = lax.dynamic_index_in_dim(cotangent, which, 0, keepdims=False)
        out_grad = jnp.where(section_index == section_count - 1, own_grad, back_received).astype(
            jnp.float32
        )
        in_grad, weight_terms, small_terms = layer_backward(
            lax.dynamic_index_in_dim(saved_in, which, 0, keepdims=False),
            lax.dynamic_index_in_dim(saved_mid, which, 0, keepdims=False),
            lax.dynamic_index_in_dim(saved_totals, which, 0, keepdims=False),
            lax.dynamic_index_in_dim(segment_ids, which, 0, keepdims=False),
            out_grad,
        )
        joined_term, out_term, up_term, down_term = tuple(
            (jnp.where(running, term, 0.0) for term in weight_terms)
        )
        weight_terms = (joined_term, out_term, up_term, down_term)
        weight_totals = tuple((total + term for total, term in zip(weight_totals, weight_terms)))
        small_totals = tuple(
            (
                total + jnp.where(running, term, 0.0)
                for total, term in zip(small_totals, small_terms)
            )
        )
        grads_store = store_at(grads_store, in_grad, which, running)
        if tick + 1 < ticks:
            back_received = passed_along(in_grad.astype(jnp.bfloat16), "section", -1)
    joined_total, out_total, up_total, down_total = weight_totals
    summed = (
        lax.psum(joined_total.astype(jnp.bfloat16), "dp").astype(jnp.float32),
        lax.psum(out_total.astype(jnp.bfloat16), "dp").astype(jnp.float32),
        lax.psum(up_total.astype(jnp.bfloat16), "dp").astype(jnp.float32),
        lax.psum(down_total.astype(jnp.bfloat16), "dp").astype(jnp.float32),
    )
    gain_total, shift_total, qv_total, up_shift_total, out_shift_total = small_totals
    small_summed = lax.psum(
        (gain_total, shift_total, qv_total, up_shift_total, out_shift_total), ("dp", "tensor")
    )
    qkv_grad = summed[0].reshape(model_width, 3, cols_local).transpose(1, 0, 2)
    return (
        states[None],
        grads_store[None],
        small_summed[0][None],
        small_summed[1][None],
        qkv_grad[None],
        small_summed[2][None],
        summed[1][None],
        summed[2][None],
        small_summed[3][None],
        summed[3][None],
        small_summed[4][None],
    )


def solution(mesh):
    placed = (
        P("dp", "tensor", None),
        P("dp", "tensor", None),
        P("dp", None),
        P("section", None, None),
        P("section", None, None),
        P("section", None, None, "tensor"),
        P("section", None, None),
        P("section", "tensor", None),
        P("section", None, "tensor"),
        P("section", None),
        P("section", "tensor", None),
        P("section", None, None),
    )
    sizes = dict(mesh.shape)

    def on_device(inputs, *rest):
        each = inputs.shape[0] == sizes["section"] * sizes["tensor"]
        paired = sizes["section"] == 2 and sizes["tensor"] == 2 and sizes["dp"] % 2 == 0
        doubling = (sizes["dp"] // 2) & (sizes["dp"] // 2 - 1) == 0
        if each and paired and doubling:
            return one_sequence_each(inputs, *rest)
        return pipelined(inputs, *rest)

    return jax.shard_map(
        on_device,
        mesh=mesh,
        in_specs=placed,
        out_specs=(
            P("section", "dp", "tensor", None),
            P("section", "dp", "tensor", None),
            P("section", None, None),
            P("section", None, None),
            P("section", None, None, "tensor"),
            P("section", None, None),
            P("section", "tensor", None),
            P("section", None, "tensor"),
            P("section", None),
            P("section", "tensor", None),
            P("section", None, None),
        ),
        check_vma=False,
    )
```

```python
import functools
import math

import jax
import jax.numpy as jnp
from jax import lax
from jax.experimental import pallas as pl
from jax.experimental.pallas import tpu as pltpu
from jax.sharding import PartitionSpec as P

HEAD_DIM = 48
IMAGE_IDS = 5
IMAGE_MOST = 512
EPSILON = 1e-05
NEGATIVE = -1e30
TILE = 128
BLOCK = 256
EXTRA = 16
LOG2E = math.log2(math.e)
SCALING = HEAD_DIM ** (-0.5)
AXES = ("section", "dp", "tensor")
VMEM_LIMIT = 60 * 1024 * 1024
MESH = pl.DeviceIdType.MESH
F32 = jnp.float32
BF16 = jnp.bfloat16


def nn(left, right):
    return lax.dot_general(left, right, (((1,), (0,)), ((), ())), preferred_element_type=F32)


def nt(left, right):
    return lax.dot_general(left, right, (((1,), (1,)), ((), ())), preferred_element_type=F32)


def tn(left, right):
    return lax.dot_general(left, right, (((0,), (0,)), ((), ())), preferred_element_type=F32)


def normalise(rows):
    centre = rows - jnp.mean(rows, axis=-1, keepdims=True)
    inverse = lax.rsqrt(jnp.mean(centre * centre, axis=-1, keepdims=True) + EPSILON)
    return centre * inverse, inverse


def normalise_back(gradient, scaled, inverse, gain):
    upstream = gradient * gain
    return inverse * (
        upstream
        - jnp.mean(upstream, axis=-1, keepdims=True)
        - scaled * jnp.mean(upstream * scaled, axis=-1, keepdims=True)
    )


def gelu_pair(values):
    share = 0.5 + 0.5 * lax.erf(values * math.sqrt(0.5))
    bell = jnp.exp2(values * values * (-0.5 * LOG2E))
    return values * share, share + values * bell * (1.0 / math.sqrt(2 * math.pi))


def extra_rows(rows, width):
    at = lax.broadcasted_iota(jnp.int32, (EXTRA, width), 0)
    out = jnp.zeros((EXTRA, width), F32)
    for index, row in enumerate(rows):
        out = jnp.where(at == index, row, out)
    return out.astype(BF16)


def three_parts(row):
    first = row.astype(BF16).astype(F32)
    second = (row - first).astype(BF16).astype(F32)
    return [first, second, row - first - second]


def each_image(start_ref, tiles_ref, body):
    most = IMAGE_MOST // TILE + 1

    def image(index, carry):
        first = start_ref[index]
        tiles = tiles_ref[index]
        for count in range(1, most + 1):

            @pl.when(tiles == count)
            def _():
                body(index, pl.multiple_of(first * TILE, TILE), count * TILE)

        return carry

    lax.fori_loop(0, IMAGE_IDS, image, 0)


def run_copies(copies):
    for copy in copies:
        copy.start()


def wait_copies(copies):
    for copy in copies:
        copy.wait()


def slot_of(place_ref, index):
    return 2 * (place_ref[0] ^ (index // 2)) + (place_ref[1] ^ (index % 2))


def once(shape):
    zeros = (0,) * len(shape)
    return pl.BlockSpec(shape, lambda *_: zeros, pipeline_mode=pl.Buffered(1))


def anywhere(count):
    return [pl.BlockSpec(memory_space=pl.ANY)] * count


def settings(flops, collective=None):
    remote = {} if collective is None else dict(collective_id=collective, has_side_effects=True)
    return dict(
        compiler_params=pltpu.CompilerParams(vmem_limit_bytes=VMEM_LIMIT, **remote),
        cost_estimate=pl.CostEstimate(flops=flops, bytes_accessed=1_000_000, transcendentals=0),
    )


def blocks_of(ref, axis=0):
    return ref.shape[axis] // BLOCK


def block_at(index):
    return pl.ds(pl.multiple_of(index * BLOCK, BLOCK), BLOCK)


def big_blocks(rows):
    size = rows // 2
    return [slice(i * size, (i + 1) * size) for i in range(2)]


def attend_forward_image(index, at, width, heads, seg_ref, qkv_ref, store):
    win = pl.ds(at, width)
    mine = seg_ref[:, win] == index
    mask = jnp.where(mine, 0.0, NEGATIVE)
    one = jnp.ones((1, width), F32)
    query_extra = extra_rows([mask, one], width)
    key_extra = extra_rows([one, mask], width)
    value_extra = extra_rows([one], width)
    cols = heads * HEAD_DIM

    def rows_of(third, head):
        low = third * cols + head * HEAD_DIM
        return qkv_ref[low : low + HEAD_DIM, win]

    def scores(head):
        queries = jnp.concatenate([rows_of(0, head), query_extra], axis=0)
        keys = jnp.concatenate([rows_of(1, head), key_extra], axis=0)
        return tn(keys, queries)

    following = scores(0)
    for head in range(heads):
        current = following
        if head + 1 < heads:
            following = scores(head + 1)
        peak = jnp.max(current, axis=0, keepdims=True)
        weights = jnp.exp2(current - peak).astype(BF16)
        mixed = nn(jnp.concatenate([rows_of(2, head), value_extra], axis=0), weights)
        total = mixed[HEAD_DIM : HEAD_DIM + 1]
        store(head, win, mine, mixed[:HEAD_DIM] * (1.0 / total), peak + jnp.log2(total))


def attend_backward_image(index, at, width, heads, seg_ref, qkv_ref, mixed_ref, total_ref, mixed_grad, sums):
    win = pl.ds(at, width)
    mine = seg_ref[:, win] == index
    mask = jnp.where(mine, 0.0, NEGATIVE)
    one = jnp.ones((1, width), F32)
    key_extra = extra_rows([one, mask, one, one, one], width)
    value_extra = extra_rows([one, one, one], width)
    cols = heads * HEAD_DIM

    def span(third, head):
        low = third * cols + head * HEAD_DIM
        return slice(low, low + HEAD_DIM)

    def products(head):
        own = span(0, head)
        grads = mixed_grad[own, win]
        inner = jnp.sum(grads.astype(F32) * mixed_ref[own, win].astype(F32), axis=0, keepdims=True)
        query_extra = extra_rows([mask, one] + three_parts(-total_ref[head, :, win]), width)
        grad_extra = extra_rows(three_parts(-inner), width)
        keys = jnp.concatenate([qkv_ref[span(1, head), win], key_extra], axis=0)
        queries = jnp.concatenate([qkv_ref[own, win], query_extra], axis=0)
        values = jnp.concatenate([qkv_ref[span(2, head), win], value_extra], axis=0)
        return tn(keys, queries), tn(values, jnp.concatenate([grads, grad_extra], axis=0))

    following = products(0)
    for head in range(heads):
        scores, terms = following
        if head + 1 < heads:
            following = products(head + 1)
        weights = jnp.exp2(scores)
        score_grads = (weights * terms).astype(BF16)
        sums[span(0, head), win] += nn(qkv_ref[span(1, head), win], score_grads) * SCALING
        sums[span(1, head), win] += nt(qkv_ref[span(0, head), win], score_grads) * (1.0 / LOG2E)
        sums[span(2, head), win] += nt(mixed_grad[span(0, head), win], weights.astype(BF16))


def mixer_forward_kernel(
    place_ref, start_ref, tiles_ref, seg_ref, hidden_ref, norm_ref, qkv_shift_ref, *rest, pieces, out_pieces, heads
):
    first = out_pieces in (0, pieces)
    last = out_pieces > 0
    rest = list(rest)
    weights = [rest.pop(0) for _ in range(pieces)]
    if not first:
        normed_in = rest.pop(0)
        mixed_before = rest.pop(0)
    if last:
        out_weights = [rest.pop(0) for _ in range(out_pieces)]
        out_shift_ref = rest.pop(0)
    qkv_ref, mixed_ref, total_ref = rest.pop(0), rest.pop(0), rest.pop(0)
    if first:
        normed_out = rest.pop(0)
    if last:
        middle_ref = rest.pop(0)
    weight, normed, sems = rest.pop(0), rest.pop(0), rest.pop(0)
    if last:
        out_weight, mixed_all, out_sems = rest
    step = pl.program_id(0)
    cols = heads * HEAD_DIM
    before = out_pieces - pieces if last else 0
    copies = [
        pltpu.make_async_copy(
            weights[i].at[0 : 3 * cols], weight.at[i], sems.at[i]
        )
        for i in range(pieces)
    ]
    if not first:
        norm_copy = pltpu.make_async_copy(normed_in, normed, sems.at[pieces])
    out_copies = []
    if last:
        for i in range(out_pieces):
            out_copies.append(
                pltpu.make_async_copy(
                    out_weights[i].at[3 * cols : 4 * cols],
                    out_weight.at[i * cols : (i + 1) * cols],
                    out_sems.at[i],
                )
            )
        for i in range(before):
            out_copies.append(
                pltpu.make_async_copy(
                    mixed_before.at[i], mixed_all.at[i * cols : (i + 1) * cols], out_sems.at[out_pieces + i]
                )
            )

    @pl.when(step == 0)
    def _():
        if not first:
            norm_copy.start()
        run_copies(copies + out_copies)
        if first:

            def norm_block(i, carry):
                rows = block_at(i)
                scaled, _ = normalise(hidden_ref[rows, :].astype(F32))
                result = (scaled * norm_ref[0:1, :] + norm_ref[1:2, :]).astype(BF16)
                normed[rows, :] = result
                normed_out[rows, :] = result
                return carry

            lax.fori_loop(0, blocks_of(hidden_ref), norm_block, 0)
        else:
            norm_copy.wait()

    for index in range(pieces):

        @pl.when(step == index)
        def _():
            copies[index].wait()

    projected = nt(weight[step], normed[...]) + qkv_shift_ref[0]
    qkv_ref[0, 0:cols, :] = (projected[0:cols] * (SCALING * LOG2E)).astype(BF16)
    qkv_ref[0, cols : 3 * cols, :] = projected[cols : 3 * cols].astype(BF16)

    def store(head, win, mine, mixed, total):
        rows = slice(head * HEAD_DIM, (head + 1) * HEAD_DIM)
        old = mixed_ref[0, rows, win].astype(F32)
        mixed_ref[0, rows, win] = jnp.where(mine, mixed, old).astype(BF16)
        total_ref[head, :, win] = jnp.where(mine, total, total_ref[head, :, win])

    each_image(
        start_ref,
        tiles_ref,
        lambda index, at, width: attend_forward_image(
            index, at, width, heads, seg_ref, qkv_ref.at[0], store
        ),
    )
    if last:
        mixed_all[pl.ds(pl.multiple_of((before + step) * cols, cols), cols), :] = mixed_ref[0]

        @pl.when(step == pieces - 1)
        def _():
            wait_copies(out_copies)

            for rows in big_blocks(hidden_ref.shape[0]):
                branch = tn(mixed_all[:, rows], out_weight[...])
                middle_ref[rows, :] = hidden_ref[rows, :].astype(F32) + branch + out_shift_ref[...]


def mixer_forward(images, hidden, norm, qkv_shift, pieces, offset=0, before=None, out_pieces=(), out_shift=None):
    rows, width = hidden.shape
    count = len(pieces)
    cols = width // 4
    heads = cols // HEAD_DIM
    place, start, tiles, segment = images
    operands = list(pieces)
    outs = [
        jax.ShapeDtypeStruct((count, 3 * cols, rows), BF16),
        jax.ShapeDtypeStruct((count, cols, rows), BF16),
        jax.ShapeDtypeStruct((count * heads, 1, rows), F32),
    ]
    scratch = [
        pltpu.VMEM((count, 3 * cols, width), BF16),
        pltpu.VMEM((rows, width), BF16),
        pltpu.SemaphoreType.DMA((count + 1,)),
    ]
    if before is None:
        outs.append(jax.ShapeDtypeStruct((rows, width), BF16))
    else:
        operands += list(before)
    specs = anywhere(len(operands) + len(out_pieces))
    operands += list(out_pieces)
    if out_pieces:
        operands.append(out_shift)
        specs.append(once((1, width)))
        outs.append(jax.ShapeDtypeStruct((rows, width), F32))
        scratch += [
            pltpu.VMEM((width, width), BF16),
            pltpu.VMEM((width, rows), BF16),
            pltpu.SemaphoreType.DMA((2 * len(out_pieces),)),
        ]
    return pl.pallas_call(
        functools.partial(
            mixer_forward_kernel,
            pieces=count,
            out_pieces=len(out_pieces),
            heads=heads,
        ),
        grid_spec=pltpu.PrefetchScalarGridSpec(
            num_scalar_prefetch=3,
            grid=(count,),
            in_specs=[
                once((1, rows)),
                once((rows, width)),
                once((2, width)),
                pl.BlockSpec((1, 3 * cols, 1), lambda i, place, *_: (slot_of(place, i + offset), 0, 0)),
            ]
            + specs,
            out_specs=[
                pl.BlockSpec((1, 3 * cols, rows), lambda i, *_: (i, 0, 0)),
                pl.BlockSpec((1, cols, rows), lambda i, *_: (i, 0, 0)),
                pl.BlockSpec((heads, 1, rows), lambda i, *_: (i, 0, 0)),
            ]
            + [once((rows, width))] * (len(outs) - 3),
            scratch_shapes=scratch,
        ),
        out_shape=outs,
        name="mixer_forward",
        **settings(4_000_000_000),
    )(place, start, tiles, segment, hidden, norm, qkv_shift, *operands)


def feed_forward_kernel(place_ref, middle_ref, norm_ref, up_shift_ref, start_ref, *rest, pieces, offset, last):
    ups, downs = rest[:pieces], rest[pieces : 2 * pieces]
    out_ref, active_ref, slope_ref, up_weight, down_weight, sems = rest[2 * pieces :]
    step = pl.program_id(0)
    size = up_weight.shape[2]
    copies = []
    for i in range(pieces):
        copies.append(
            pltpu.make_async_copy(ups[i], up_weight.at[i], sems.at[0, i])
        )
        copies.append(
            pltpu.make_async_copy(downs[i], down_weight.at[i], sems.at[1, i])
        )

    @pl.when(step == 0)
    def _():
        run_copies(copies)

    scaled, _ = normalise(middle_ref[...])
    normed = (scaled * norm_ref[0:1, :] + norm_ref[1:2, :]).astype(BF16)
    total = start_ref[...] if offset else middle_ref[...] + start_ref[...]

    @pl.when(step == 0)
    def _():
        wait_copies(copies)

    def raise_by(index):
        return nn(normed, up_weight[index]) + up_shift_ref[slot_of(place_ref, offset + index)]

    following = raise_by(0)
    for index in range(pieces):
        raised = following
        if index + 1 < pieces:
            following = raise_by(index + 1)
        part = pl.ds(index * size, size)
        active, slope = gelu_pair(raised)
        active = active.astype(BF16)
        active_ref[:, part] = active
        slope_ref[:, part] = slope.astype(BF16)
        total = total + nn(active, down_weight[index])
    out_ref[...] = total.astype(out_ref.dtype)


def feed_forward(place, middle, norm, up_shift, begin, ups, downs, offset, last):
    rows, width = middle.shape
    pieces = len(ups)
    size = up_shift.shape[2]
    hidden = size * pieces
    return pl.pallas_call(
        functools.partial(
            feed_forward_kernel,
            pieces=pieces,
            offset=offset,
            last=last,
        ),
        grid_spec=pltpu.PrefetchScalarGridSpec(
            num_scalar_prefetch=1,
            grid=(rows // BLOCK,),
            in_specs=[
                pl.BlockSpec((BLOCK, width), lambda i, *_: (i, 0)),
                once((2, width)),
                once(up_shift.shape),
                pl.BlockSpec((BLOCK, width), lambda i, *_: (i, 0)) if offset else once((1, width)),
            ]
            + anywhere(2 * pieces),
            out_specs=[
                pl.BlockSpec((BLOCK, width), lambda i, *_: (i, 0)),
                pl.BlockSpec((BLOCK, hidden), lambda i, *_: (i, 0)),
                pl.BlockSpec((BLOCK, hidden), lambda i, *_: (i, 0)),
            ],
            scratch_shapes=[
                pltpu.VMEM((pieces, width, size), BF16),
                pltpu.VMEM((pieces, size, width), BF16),
                pltpu.SemaphoreType.DMA((2, pieces)),
            ],
        ),
        out_shape=[
            jax.ShapeDtypeStruct((rows, width), BF16 if last else F32),
            jax.ShapeDtypeStruct((rows, hidden), BF16),
            jax.ShapeDtypeStruct((rows, hidden), BF16),
        ],
        name="feed_forward",
        **settings(4_000_000_000),
    )(place, middle, norm, up_shift, begin, *ups, *downs)


ORDER = (1, 3, 0, 2)


class Neighbours:
    def __init__(self, count):
        self.section, self.group, self.lane = [lax.axis_index(axis) for axis in AXES]
        self.core = lax.rem(self.group, 2)
        self.z_index = self.group // 2
        self.count = count
        self.twin = (self.section, self.group + 1 - 2 * self.core, self.lane)
        self.beside = (self.section, self.group, 1 - self.lane)
        self.across = (1 - self.section, self.group, self.lane)
        self.far = (1 - self.section, self.group, 1 - self.lane)
        self.line = [self.along(step) for step in range(1, count)]

    def along(self, step):
        return (self.section, lax.rem(self.z_index + step + self.count, self.count) * 2 + self.core, self.lane)

    def slot_of(self, index):
        return 2 * (self.lane + (index // 2) * (1 - 2 * self.lane)) + self.core + (index % 2) * (1 - 2 * self.core)


def greet(devices):
    barrier = pltpu.get_barrier_semaphore()
    for device in devices:
        pl.semaphore_signal(barrier, inc=1, device_id=device, device_id_type=MESH)
    pl.semaphore_wait(barrier, len(devices))


class Remote:
    def __init__(self, sends, receives):
        self.sends, self.receives, self.slot = sends, receives, 0

    def reserve(self, number):
        self.slot += number
        return self.slot - number

    def copy(self, source, target, device, slot=None):
        slot = self.reserve(1) if slot is None else slot
        return pltpu.make_async_remote_copy(
            src_ref=source,
            dst_ref=target,
            send_sem=self.sends.at[slot],
            recv_sem=self.receives.at[slot],
            device_id=device,
            device_id_type=MESH,
        )


def sum_with_core(index, copies, grad_of, sent, came, put):
    slot = index % 2
    if index < 2:

        def keep(where, value):
            sent[(slot,) + where] = value.astype(BF16)

        grad_of(keep)
        copies[slot].start()
    else:
        copies[slot].wait_recv()

        def add(where, value):
            put(slot, where, (value + came[(slot,) + where].astype(F32)).astype(BF16))

        grad_of(add)
        copies[slot].wait_send()


def plane_copies(remote, near, sums, target, columns):
    size = sums.shape[1] // 2
    mine = pl.ds(pl.multiple_of(near.section * size, size), size)
    theirs = pl.ds(pl.multiple_of((1 - near.section) * size, size), size)
    return [
        remote.copy(sums.at[1, mine, columns], target.at[0, :, columns], near.beside),
        remote.copy(sums.at[0, theirs, columns], target.at[1, :, columns], near.across),
        remote.copy(sums.at[1, theirs, columns], target.at[2, :, columns], near.far),
    ]


def line_copies(remote, near, part, target, columns):
    size = part.shape[0] // near.count
    copies = []
    for i, device in enumerate(near.line):
        to = lax.rem(near.z_index + i + 1, near.count)
        rows = pl.ds(pl.multiple_of(to * size, size), size)
        copies.append(remote.copy(part.at[rows, columns], target.at[i, :, columns], device))
    return copies


def line_total(near, part, came, columns):
    size = came.shape[1]
    total = part[pl.ds(pl.multiple_of(near.z_index * size, size), size), columns].astype(F32)
    for i in range(near.count - 1):
        total = total + came[i, :, columns].astype(F32)
    return total


class FeedSum:
    def __init__(self, remote, near, scratch):
        self.near = near
        self.part, self.part_came, self.block, self.block_came = scratch
        size = self.part_came.shape[1]
        everything = slice(None)
        self.first = line_copies(remote, near, self.part, self.part_came, everything)
        self.second = [
            remote.copy(self.block.at[pl.ds(2 * size, size)], self.block_came.at[0], near.beside),
            remote.copy(self.block.at[pl.ds(size, size)], self.block_came.at[1], near.across),
            remote.copy(self.block.at[pl.ds(3 * size, size)], self.block_came.at[2], near.far),
        ]

    def start(self, first_terms, second_terms):
        for target, terms, copies in (
            (self.part, first_terms, self.first),
            (self.block, second_terms, self.second),
        ):
            total = terms[0].astype(F32)
            for term in terms[1:]:
                total = total + term.astype(F32)
            target[...] = total.astype(BF16)
            run_copies(copies)

    def finish(self):
        wait_copies(self.first + self.second)
        second = self.block[0 : self.block_came.shape[1], :].astype(F32)
        for i in range(3):
            second = second + self.block_came[i].astype(F32)
        return line_total(self.near, self.part, self.part_came, slice(None)), second


def first_columns(width):
    return 2 * width // 3


def feed_sum_scratch(width, line):
    first, size = first_columns(width), width // line
    return [
        pltpu.VMEM((width, first), BF16),
        pltpu.VMEM((line - 1, size, first), BF16),
        pltpu.VMEM((4 * size, width - first), BF16),
        pltpu.VMEM((3, size, width - first), BF16),
    ]


def feed_backward_kernel(grad_ref, middle_ref, norm_ref, *rest, columns, rider, line):
    pieces = 4
    rest = list(rest)
    actives = [rest.pop(0) for _ in range(pieces)]
    slopes = [rest.pop(0) for _ in range(pieces)]
    ups = [rest.pop(0) for _ in range(pieces)]
    downs = [rest.pop(0) for _ in range(pieces)]
    if rider:
        rider_ref = rest.pop(0)
        feed_terms = [rest.pop(0) for _ in range(5)]
    keep_ref, beside_ref, across_ref, far_ref, spread_ref = [rest.pop(0) for _ in range(5)]
    up_shift_grad_ref, middle_grad_ref, small_ref = [rest.pop(0) for _ in range(3)]
    if rider:
        feed_total_ref, mixer_part_ref = rest.pop(0), rest.pop(0)
    (
        normed_t,
        grad_t,
        normed_grad,
        up_weight,
        down_weight,
        active,
        slope,
        low_grad,
        sent,
        came,
        sems,
        sends,
        receives,
    ) = rest[:13]
    step = pl.program_id(0)
    rows_all, width = grad_ref.shape
    size = up_weight.shape[2]
    blocks = blocks_of(grad_ref)
    near = Neighbours(line)
    remote = Remote(sends, receives)
    core_copies = [remote.copy(sent.at[slot], came.at[slot], near.twin) for slot in range(2)]
    devices = [near.twin]
    everything = slice(None)
    if rider:
        rider_own, rider_came, rider_sems = rest[13:16]
        feed_sum = FeedSum(remote, near, rest[16:])
        devices += [near.beside, near.across, near.far] + near.line
        half = rider_own.shape[0]
        plane = plane_copies(remote, near, rider_ref, rider_came, everything)
        rider_keep = pltpu.make_async_copy(
            rider_ref.at[0, pl.ds(pl.multiple_of(near.section * half, half), half)],
            rider_own,
            rider_sems.at[len(feed_terms)],
        )
        cut = first_columns(width)
        spots = [sent.at[i // 2, i % 2, :, 0:cut] for i in range(4)]
        spots.append(active.at[1, 0 : feed_terms[4].shape[0], 0 : width - cut])
        term_copies = [
            pltpu.make_async_copy(term, spot, rider_sems.at[i])
            for i, (term, spot) in enumerate(zip(feed_terms, spots))
        ]
    copies = []
    for slot, i in enumerate(ORDER):
        own = pl.ds(columns[i] * size, size)
        at = slot % 2
        copies.append(
            [
                pltpu.make_async_copy(downs[i], down_weight.at[at], sems.at[0, at]),
                pltpu.make_async_copy(slopes[i].at[:, own], slope.at[at], sems.at[1, at]),
                pltpu.make_async_copy(ups[i], up_weight.at[at], sems.at[2, at]),
                pltpu.make_async_copy(actives[i].at[:, own], active.at[at], sems.at[3, at]),
            ]
        )

    @pl.when(step == 0)
    def _():
        run_copies(copies[0])
        if rider:
            run_copies(term_copies + [rider_keep])
        greet(devices)
        if rider:
            run_copies(plane)
            wait_copies(term_copies)
            terms = [spot[...] for spot in spots]
            feed_sum.start(terms[:4], terms[4:])

        def prepare(i, carry):
            rows = block_at(i)
            scaled, _ = normalise(middle_ref[rows, :])
            normed = (scaled * norm_ref[0:1, :] + norm_ref[1:2, :]).astype(BF16)
            normed_t[:, rows] = normed.T
            grad_t[:, rows] = grad_ref[rows, :].T
            return carry

        lax.fori_loop(0, blocks, prepare, 0)

    for index in range(pieces):

        @pl.when(step == index)
        def _():
            at = index % 2
            wait_copies(copies[index])
            if index + 1 < pieces:
                run_copies(copies[index + 1])
            shift_grad = jnp.zeros((1, size), F32)
            for rows in big_blocks(rows_all):
                hidden_grad = nt(grad_ref[rows, :], down_weight[at]) * slope[at, rows, :].astype(F32)
                low = hidden_grad.astype(BF16)
                low_grad[rows, :] = low
                shift_grad = shift_grad + jnp.sum(hidden_grad, axis=0, keepdims=True)
                term = nt(low, up_weight[at])
                normed_grad[rows, :] = term if index == 0 else normed_grad[rows, :] + term
            up_shift_grad_ref[near.slot_of(ORDER[index])] = shift_grad

            def grad_of(put):
                for rows in big_blocks(width):
                    put((0, rows, slice(None)), nn(normed_t[rows, :], low_grad[...]))
                    put((1, rows, slice(None)), nn(grad_t[rows, :], active[at]))

            def put(slot, where, value):
                inner, outer = ((keep_ref, across_ref), (beside_ref, far_ref))[slot]
                which, rows, _ = where
                cut = first_columns(width)
                value_low, value_high = value[:, :cut], value[:, cut:]

                @pl.when(near.section == which)
                def _():
                    inner[rows, :] = value_low

                @pl.when(near.section != which)
                def _():
                    outer[rows, :] = value_low

                part = width // line
                other_half = which + near.section * (1 - 2 * which)
                for first in range(rows.start, rows.stop, part):
                    at_row = pl.multiple_of((2 * slot + other_half) * part, part)
                    spread_ref[first // part, pl.ds(at_row, part), :] = value_high[first - rows.start : first - rows.start + part]

            sum_with_core(index, core_copies, grad_of, sent, came, put)

    @pl.when(step == pieces - 1)
    def _():
        def finish(i, sums):
            rows = block_at(i)
            scaled, inverse = normalise(middle_ref[rows, :])
            gradient = normed_grad[rows, :]
            upper = grad_ref[rows, :].astype(F32)
            middle_grad = upper + normalise_back(gradient, scaled, inverse, norm_ref[0:1, :])
            middle_grad_ref[rows, :] = middle_grad
            terms = (gradient * scaled, gradient, middle_grad, upper)
            return tuple(old + jnp.sum(term, axis=0, keepdims=True) for old, term in zip(sums, terms))

        zero = jnp.zeros((1, width), F32)
        sums = lax.fori_loop(0, blocks, finish, (zero, zero, zero, zero))
        for index, row in enumerate(sums):
            small_ref[index : index + 1, :] = row
        if rider:
            cut = first_columns(width)
            first_total, second_total = feed_sum.finish()
            feed_total_ref[:, :cut] = first_total.astype(BF16)
            feed_total_ref[:, cut:] = second_total.astype(BF16)
            rider_keep.wait()
            wait_copies(plane)
            total = rider_own[...].astype(F32)
            for i in range(3):
                total = total + rider_came[i].astype(F32)
            mixer_part_ref[...] = total.astype(BF16)


def feed_backward(grad, middle, norm, actives, slopes, columns, ups, downs, collective, rider=None):
    rows, width = middle.shape
    pieces = len(ups)
    size = ups[0].shape[1]
    operands = [*actives, *slopes, *ups, *downs] + list(rider or [])
    line = lax.axis_size("dp") // 2
    cut = first_columns(size)
    outs = [jax.ShapeDtypeStruct((width, cut), BF16)] * 4 + [
        jax.ShapeDtypeStruct((line, 4 * width // line, size - cut), BF16),
        jax.ShapeDtypeStruct((pieces, 1, size), F32),
        jax.ShapeDtypeStruct((rows, width), F32),
        jax.ShapeDtypeStruct((4, width), F32),
    ]
    scratch = [
        pltpu.VMEM((width, rows), BF16),
        pltpu.VMEM((width, rows), BF16),
        pltpu.VMEM((rows, width), F32),
        pltpu.VMEM((2, width, size), BF16),
        pltpu.VMEM((2, size, width), BF16),
        pltpu.VMEM((2, rows, size), BF16),
        pltpu.VMEM((2, rows, size), BF16),
        pltpu.VMEM((rows, size), BF16),
        pltpu.VMEM((2, 2, width, size), BF16),
        pltpu.VMEM((2, 2, width, size), BF16),
        pltpu.SemaphoreType.DMA((4, 2)),
        pltpu.SemaphoreType.DMA((32,)),
        pltpu.SemaphoreType.DMA((32,)),
    ]
    if rider is not None:
        half = width // 2
        outs += [
            jax.ShapeDtypeStruct((width // line, width), BF16),
            jax.ShapeDtypeStruct((half, width), BF16),
        ]
        scratch += [
            pltpu.VMEM((half, width), BF16),
            pltpu.VMEM((3, half, width), BF16),
            pltpu.SemaphoreType.DMA((6,)),
        ]
        scratch += feed_sum_scratch(width, line)
    return pl.pallas_call(
        functools.partial(
            feed_backward_kernel, columns=columns, rider=rider is not None, line=line
        ),
        grid=(pieces,),
        in_specs=[once((rows, width)), once((rows, width)), once((2, width))] + anywhere(len(operands)),
        out_specs=[once(out.shape) for out in outs],
        scratch_shapes=scratch,
        out_shape=outs,
        name="feed_backward",
        **settings(16_000_000_000, collective),
    )(grad, middle, norm, *operands)


def mixer_backward_kernel(
    place_ref, start_ref, tiles_ref, seg_ref, middle_grad_ref, qkv_ref_all, *rest, saved, heads
):
    pieces = len(saved)
    rest = [qkv_ref_all] + list(rest)
    qkvs = [rest.pop(0) for _ in range(pieces)]
    mixeds = [rest.pop(0) for _ in range(pieces)]
    log_totals = [rest.pop(0) for _ in range(pieces)]
    weights = [rest.pop(0) for _ in range(pieces)]
    projected_ref, qkv_shift_grad_ref = rest[:2]
    qkv, mixed, totals, out_weight, low_middle, mixed_grad, sums, sems = rest[2:]
    step = pl.program_id(0)
    cols = heads * HEAD_DIM
    copies = []
    for i in range(pieces):
        at = saved[i]
        copies.append(
            [
                pltpu.make_async_copy(weights[i].at[3 * cols : 4 * cols], out_weight.at[i], sems.at[0, i]),
                pltpu.make_async_copy(qkvs[i].at[at], qkv.at[i], sems.at[1, i]),
                pltpu.make_async_copy(mixeds[i].at[at], mixed.at[i], sems.at[2, i]),
                pltpu.make_async_copy(
                    log_totals[i].at[at * heads : (at + 1) * heads], totals.at[i], sems.at[3, i]
                ),
            ]
        )

    @pl.when(step == 0)
    def _():
        for group in copies:
            run_copies(group)
        low_middle[...] = middle_grad_ref[...].astype(BF16)

    for index in range(pieces):

        @pl.when(step == index)
        def _():
            wait_copies(copies[index])

    mixed_grad[...] = nt(out_weight[step], low_middle[...]).astype(BF16)
    sums[...] = jnp.zeros_like(sums)
    each_image(
        start_ref,
        tiles_ref,
        lambda index, at, span: attend_backward_image(
            index, at, span, heads, seg_ref, qkv.at[step], mixed.at[step], totals.at[step], mixed_grad, sums
        ),
    )
    gradient = sums[...]
    projected_ref[0] = gradient.astype(BF16)
    qkv_shift_grad_ref[0] = jnp.sum(gradient, axis=1, keepdims=True).T


def mixer_backward(images, middle_grad, qkvs, mixeds, log_totals, saved, weights):
    rows, width = middle_grad.shape
    count = len(weights)
    cols = width // 4
    heads = cols // HEAD_DIM
    place, start, tiles, segment = images
    operands = [*qkvs, *mixeds, *log_totals, *weights]
    return pl.pallas_call(
        functools.partial(mixer_backward_kernel, saved=saved, heads=heads),
        grid_spec=pltpu.PrefetchScalarGridSpec(
            num_scalar_prefetch=3,
            grid=(count,),
            in_specs=[once((1, rows)), once((rows, width))] + anywhere(len(operands)),
            out_specs=[
                pl.BlockSpec((1, 3 * cols, rows), lambda i, *_: (i, 0, 0)),
                pl.BlockSpec((1, 1, 3 * cols), lambda i, place, *_: (slot_of(place, i), 0, 0)),
            ],
            scratch_shapes=[
                pltpu.VMEM((count, 3 * cols, rows), BF16),
                pltpu.VMEM((count, cols, rows), BF16),
                pltpu.VMEM((count, heads, 1, rows), F32),
                pltpu.VMEM((count, cols, width), BF16),
                pltpu.VMEM((rows, width), BF16),
                pltpu.VMEM((cols, rows), BF16),
                pltpu.VMEM((3 * cols, rows), F32),
                pltpu.SemaphoreType.DMA((4, count)),
            ],
        ),
        out_shape=[
            jax.ShapeDtypeStruct((count, 3 * cols, rows), BF16),
            jax.ShapeDtypeStruct((count, 1, 3 * cols), F32),
        ],
        name="mixer_backward",
        **settings(16_000_000_000),
    )(place, start, tiles, segment, middle_grad, *operands)


class Line:
    def __init__(self, remote, near, ref, size, columns):
        self.near = near
        self.copies = []
        for hop in range(near.count - 1):
            pair = []
            for sign in (1, -1):
                origin = lax.rem(near.z_index - sign * hop + near.count, near.count)
                chunk = ref.at[near.core, :, pl.ds(pl.multiple_of(origin * size, size), size), columns]
                pair.append((sign, remote.copy(chunk, chunk, near.along(sign))))
            self.copies.append(pair)

    def each(self, hop, ahead, act):
        for sign, copy in self.copies[hop]:
            origin = self.near.z_index - sign * (hop + 1 - ahead)
            target = self.near.z_index + sign * ahead

            @pl.when((origin >= 0) & (origin < self.near.count) & (target >= 0) & (target < self.near.count))
            def _():
                act(copy)

    def start(self, hop):
        self.each(hop, 1, lambda copy: copy.start())

    def receive(self, hop):
        self.each(hop, 0, lambda copy: copy.wait_recv())

    def finish(self):
        for hop in range(self.near.count - 1):
            self.each(hop, 1, lambda copy: copy.wait_send())


def input_backward_kernel(hidden_ref, middle_grad_ref, norm_ref, projected, normed_in, *rest, saved, line, last):
    pieces = len(saved)
    rest = list(rest)
    mixeds = [rest.pop(0) for _ in range(pieces)]
    weights = [rest.pop(0) for _ in range(pieces)]
    if last:
        feed_terms = [rest.pop(0) for _ in range(5)]
        mixer_part1, feed_total1, other_grad = [rest.pop(0) for _ in range(3)]
        small_refs = [rest.pop(0) for _ in range(7)]
        feed_result, mixer_result, parts_result, vector_out = [rest.pop(0) for _ in range(4)]
    else:
        sums_ref, in_grad_ref, small_ref = [rest.pop(0) for _ in range(3)]
    projected_grad, mixed, normed, low_middle, weight, sent, came = [rest.pop(0) for _ in range(7)]
    sems, sends, receives = [rest.pop(0) for _ in range(3)]
    rows_all, width = hidden_ref.shape
    count = projected.shape[1]
    near = Neighbours(line)
    remote = Remote(sends, receives)
    everything = slice(None)
    devices = [near.twin]
    if last:
        devices += [near.beside, near.across, near.far] + near.line
        sums_ref, in_grad_ref = [rest.pop(0) for _ in range(2)]
        feed_sum = FeedSum(remote, near, [rest.pop(0) for _ in range(4)])
        part1_came = rest.pop(0)
    copies = []
    for i in range(pieces):
        copies.append(
            [
                pltpu.make_async_copy(
                    projected.at[i], projected_grad.at[i * count : (i + 1) * count], sems.at[0, i]
                ),
                pltpu.make_async_copy(mixeds[i].at[saved[i]], mixed.at[i], sems.at[1, i]),
                pltpu.make_async_copy(
                    weights[i].at[0:count], weight.at[i * count : (i + 1) * count], sems.at[2, i]
                ),
            ]
        )
    norm_copy = pltpu.make_async_copy(normed_in, normed, sems.at[3, 0])
    norm_copy.start()
    for i in ORDER:
        run_copies(copies[i])
    greet(devices)

    if last:
        terms = [term[...] for term in feed_terms]
        feed_sum.start(terms[:4], terms[4:])
        part1_line = line_copies(remote, near, mixer_part1, part1_came, everything)
        run_copies(part1_line)

    core_copies = [remote.copy(sent.at[slot], came.at[slot], near.twin) for slot in range(2)]
    low_middle[...] = middle_grad_ref[...].astype(BF16)
    norm_copy.wait()
    for index, piece in enumerate(ORDER):
        wait_copies(copies[piece])

        def grad_of(put, piece=piece):
            own = slice(piece * count, (piece + 1) * count)
            put((slice(0, count), everything), nn(projected_grad[own, :], normed[...]))
            put((slice(count, width), everything), nn(mixed[piece], low_middle[...]))

        def put(slot, where, value):
            sums_ref[(slot,) + where] = value

        sum_with_core(index, core_copies, grad_of, sent, came, put)

    if last:
        (
            mixer_came,
            mixer_part,
            line_came,
            feed_own,
            feed_other,
            mixer_own,
            mixer_other,
            feed_out,
            mixer_out,
            parts_out,
            vector,
            vector_came,
            locals_,
        ) = rest
        chunk_width = width // 2
        chunks = [slice(i * chunk_width, (i + 1) * chunk_width) for i in range(2)]
        plane = [plane_copies(remote, near, sums_ref, mixer_came, chunk) for chunk in chunks]

    def local(source, target, slot):
        return pltpu.make_async_copy(source, target, locals_.at[slot])

    def place_total(total0, total1, own_ref, other_ref, out_ref, chunk, slot):
        own_ref[:, chunk] = jnp.where(near.section == 0, total0, total1).astype(BF16)
        other_ref[:, chunk] = jnp.where(near.section == 0, total1, total0).astype(BF16)
        size = own_ref.shape[0]
        rows = pl.ds(pl.multiple_of(near.z_index * size, size), size)
        spot = out_ref.at[near.core, near.section, rows, chunk]
        keep = local(own_ref.at[:, chunk], spot, slot)
        keep.start()
        send = remote.copy(other_ref.at[:, chunk], spot, near.across)
        send.start()
        return [keep, send]

    if last:
        first = near.section == 0
        feed_pairs = []
        run_copies(plane[0])

    gain = jnp.zeros((1, width), F32)
    shift = jnp.zeros((1, width), F32)
    for index, rows in enumerate(big_blocks(rows_all)):
        scaled, inverse = normalise(hidden_ref[rows, :].astype(F32))
        gradient = tn(projected_grad[:, rows], weight[...])
        in_grad = middle_grad_ref[rows, :] + normalise_back(gradient, scaled, inverse, norm_ref[0:1, :])
        in_grad_ref[rows, :] = in_grad.astype(BF16)
        gain = gain + jnp.sum(gradient * scaled, axis=0, keepdims=True)
        shift = shift + jnp.sum(gradient, axis=0, keepdims=True)
        if last and index == 0:
            cut = first_columns(width)
            for chunk, total in zip((slice(0, cut), slice(cut, width)), feed_sum.finish()):
                feed_pairs.append(
                    place_total(
                        total, feed_total1[:, chunk].astype(F32), feed_own, feed_other, feed_out, chunk, len(feed_pairs)
                    )
                )
            run_copies(plane[1])

    if not last:
        small_ref[0:1, :] = gain
        small_ref[1:2, :] = shift
        return

    feed_size, mixer_size = feed_own.shape[0], mixer_own.shape[0]
    feed_chain = Line(remote, near, feed_out, feed_size, everything)
    mixer_chains = [Line(remote, near, mixer_out, mixer_size, chunk) for chunk in chunks]
    for pair in feed_pairs:
        wait_copies(pair)
    feed_chain.start(0)

    small0, ups0, shifts0, small1, ups1, shifts1, in_small1 = small_refs
    vector[...] = jnp.zeros_like(vector)
    ins = ((gain, shift), (in_small1[0:1, :], in_small1[1:2, :]))
    for layer, (small, ups, shifts) in enumerate(((small0, ups0, shifts0), (small1, ups1, shifts1))):
        rows = [ins[layer][0], small[0:1, :], ins[layer][1], small[1:2, :], small[2:3, :], small[3:4, :]]
        for i, row in enumerate(rows):
            vector[layer, i : i + 1, :] = row
        for i in range(pieces):
            vector[layer, 8 + i : 9 + i, :] = ups[i]
            vector[layer, 12 + i : 13 + i, 0:count] = shifts[i]

    def vector_round(devices, at):
        group = [remote.copy(vector, vector_came.at[at + i], device) for i, device in enumerate(devices)]
        run_copies(group)
        return group

    def vector_sum(group, at):
        wait_copies(group)
        total = vector[...]
        for i in range(len(group)):
            total = total + vector_came[at + i]
        vector[...] = total

    pending = vector_round([near.twin], 0)
    half = mixer_part.shape[0]
    mine = pl.ds(pl.multiple_of(near.section * half, half), half)
    spreads = []
    for group, chunk in zip(plane, chunks):
        wait_copies(group)
        part = sums_ref[0, mine, chunk].astype(F32)
        for i in range(3):
            part = part + mixer_came[i, :, chunk].astype(F32)
        mixer_part[:, chunk] = part.astype(BF16)
        spreads.append(line_copies(remote, near, mixer_part, line_came, chunk))
        run_copies(spreads[-1])
    vector_sum(pending, 0)
    pending = vector_round([near.beside, near.across, near.far], 1)
    rows = rows_all // 2
    inner = pl.ds(pl.multiple_of(near.lane * rows, rows), rows)
    outer = pl.ds(pl.multiple_of((1 - near.lane) * rows, rows), rows)
    spot = parts_out.at[2 * near.section + near.lane]
    at = remote.reserve(4)
    quarter = rows // 2
    inner_low = pl.ds(pl.multiple_of(near.lane * rows, quarter), quarter)
    inner_high = pl.ds(pl.multiple_of(near.lane * rows + quarter, quarter), quarter)

    def grad_copies(own, other):
        return [
            remote.copy(own.at[outer], spot, near.beside, at),
            remote.copy(other.at[inner_low], spot.at[0:quarter], near.across, at + 1),
            remote.copy(other.at[inner_high], spot.at[quarter:rows], near.across, at + 2),
            remote.copy(other.at[outer], spot, near.far, at + 3),
        ]

    def start_grads(which):
        @pl.when(first)
        def _():
            copies = grad_copies(in_grad_ref, other_grad)
            run_copies([copies[i] for i in which])

        @pl.when(near.section == 1)
        def _():
            copies = grad_copies(other_grad, in_grad_ref)
            run_copies([copies[i] for i in which])

    @pl.when(first)
    def _():
        local(in_grad_ref.at[inner], spot, 4).start()

    @pl.when(near.section == 1)
    def _():
        local(other_grad.at[inner], spot, 4).start()

    start_grads((0, 1))
    pairs = []
    for i, chunk in enumerate(chunks):
        wait_copies(spreads[i])
        total0 = line_total(near, mixer_part, line_came, chunk)
        if not pairs:
            wait_copies(part1_line)
        total1 = line_total(near, mixer_part1, part1_came, chunk)
        pairs.append(place_total(total0, total1, mixer_own, mixer_other, mixer_out, chunk, 2 + i))
    start_grads((2, 3))
    feed_chain.receive(0)
    feed_chain.start(1)
    vector_sum(pending, 1)
    pending = vector_round(near.line, 4)
    for pair, chain in zip(pairs, mixer_chains):
        wait_copies(pair)
        chain.start(0)
    for hop in range(1, line - 1):
        feed_chain.receive(hop)
        if hop + 1 < line - 1:
            feed_chain.start(hop + 1)
        for chain in mixer_chains:
            chain.receive(hop - 1)
            chain.start(hop)
    feed_twin = remote.copy(feed_out.at[near.core], feed_out.at[near.core], near.twin)
    feed_twin.start()
    vector_sum(pending, 4)
    vector_out[...] = jnp.where(first, vector[0], vector[1])
    for chain in mixer_chains:
        chain.receive(line - 2)
    mixer_twin = remote.copy(mixer_out.at[near.core], mixer_out.at[near.core], near.twin)
    mixer_twin.start()
    feed_twin.wait()
    feed_chain.finish()
    results = [local(feed_out, feed_result, 5), local(parts_out, parts_result, 6), local(mixer_out, mixer_result, 7)]
    results[0].start()
    for copy in grad_copies(in_grad_ref, other_grad):
        copy.wait()
    local(in_grad_ref.at[inner], spot, 4).wait()
    results[1].start()
    mixer_twin.wait()
    for chain in mixer_chains:
        chain.finish()
    results[2].start()
    wait_copies(results)


def input_backward(
    hidden, middle_grad, norm, projected, normed, mixeds, saved, weights, collective, finish=None
):
    rows, width = hidden.shape
    number, count, _ = projected.shape
    line = lax.axis_size("dp") // 2
    vmem = pl.BlockSpec(memory_space=pltpu.VMEM)
    far = pl.BlockSpec(memory_space=pl.ANY)
    operands = [hidden, middle_grad, norm, projected, normed, *mixeds, *weights]
    specs = [vmem] * 3 + [far] * (2 + 2 * number)
    feed_rows, half = width // line, width // 2
    mixer_rows = half // line
    scratch = [
        pltpu.VMEM((number * count, rows), BF16),
        pltpu.VMEM((number, width - count, rows), BF16),
        pltpu.VMEM((rows, width), BF16),
        pltpu.VMEM((rows, width), BF16),
        pltpu.VMEM((number * count, width), BF16),
        pltpu.VMEM((2, width, width), BF16),
        pltpu.VMEM((2, width, width), BF16),
        pltpu.SemaphoreType.DMA((4, number)),
        pltpu.SemaphoreType.DMA((64,)),
        pltpu.SemaphoreType.DMA((64,)),
    ]
    if finish is None:
        outs = [
            jax.ShapeDtypeStruct((2, width, width), BF16),
            jax.ShapeDtypeStruct((rows, width), BF16),
            jax.ShapeDtypeStruct((2, width), F32),
        ]
        out_specs = [vmem] * 3
    else:
        operands += list(finish)
        specs += [vmem] * 7 + [far] + [vmem] * (len(finish) - 8)
        outs = [
            jax.ShapeDtypeStruct((2, 2, width, width), BF16),
            jax.ShapeDtypeStruct((2, 2, half, width), BF16),
            jax.ShapeDtypeStruct((4, rows // 2, width), BF16),
            jax.ShapeDtypeStruct((16, width), F32),
        ]
        out_specs = [far] * 3 + [vmem]
        scratch += [
            pltpu.VMEM((2, width, width), BF16),
            pltpu.VMEM((rows, width), BF16),
            *feed_sum_scratch(width, line),
            pltpu.VMEM((line - 1, mixer_rows, width), BF16),
            pltpu.VMEM((3, half, width), BF16),
            pltpu.VMEM((half, width), BF16),
            pltpu.VMEM((line - 1, mixer_rows, width), BF16),
            pltpu.VMEM((feed_rows, width), BF16),
            pltpu.VMEM((feed_rows, width), BF16),
            pltpu.VMEM((mixer_rows, width), BF16),
            pltpu.VMEM((mixer_rows, width), BF16),
            pltpu.VMEM((2, 2, width, width), BF16),
            pltpu.VMEM((2, 2, half, width), BF16),
            pltpu.VMEM((4, rows // 2, width), BF16),
            pltpu.VMEM((2, 16, width), F32),
            pltpu.VMEM((3 + line, 2, 16, width), F32),
            pltpu.SemaphoreType.DMA((8,)),
        ]
    return pl.pallas_call(
        functools.partial(input_backward_kernel, saved=saved, line=line, last=finish is not None),
        in_specs=specs,
        out_specs=out_specs,
        scratch_shapes=scratch,
        out_shape=outs,
        name="input_backward",
        **settings(8_000_000_000, collective),
    )(*operands)


def place_states_kernel(place_ref, *rest):
    parts, out_ref, held, sems = rest[:4], rest[4], rest[5], rest[6]
    inward = [pltpu.make_async_copy(part, held.at[i], sems.at[0, i]) for i, part in enumerate(parts)]
    outward = [
        pltpu.make_async_copy(held.at[i], out_ref.at[place_ref[2] ^ i], sems.at[1, i]) for i in range(len(parts))
    ]
    run_copies(inward)
    for first, second in zip(inward, outward):
        first.wait()
        second.start()
    wait_copies(outward)


def place_states(place, parts):
    far = pl.BlockSpec(memory_space=pl.ANY)
    return pl.pallas_call(
        place_states_kernel,
        grid_spec=pltpu.PrefetchScalarGridSpec(
            num_scalar_prefetch=1,
            grid=(1,),
            in_specs=[far] * 4,
            out_specs=far,
            scratch_shapes=[
                pltpu.VMEM((4,) + parts[0].shape, BF16),
                pltpu.SemaphoreType.DMA((2, 4)),
            ],
        ),
        out_shape=jax.ShapeDtypeStruct((4,) + parts[0].shape, BF16),
        name="place_states",
        **settings(1_000_000),
    )(place, *parts)


def widen_kernel(low_ref, out_ref):
    out_ref[...] = low_ref[...].astype(F32)


def widen(parts):
    number, rows, width = parts.shape
    spec = pl.BlockSpec((1, rows, width), lambda i: (i, 0, 0))
    return pl.pallas_call(
        widen_kernel,
        grid=(number,),
        in_specs=[spec],
        out_specs=spec,
        out_shape=jax.ShapeDtypeStruct(parts.shape, F32),
        name="widen",
        **settings(1_000_000),
    )(parts)


def unpack_kernel(feed_ref, mixer_ref, qkv_ref, out_ref, up_ref, down_ref):
    width = feed_ref.shape[2]
    part = width // 4
    for core in range(2):
        up_ref[:, core * width : (core + 1) * width] = feed_ref[core, 0].astype(F32)
        down_ref[core * width : (core + 1) * width, :] = feed_ref[core, 1].astype(F32).T
        out_ref[core * part : (core + 1) * part, :] = mixer_ref[core, 3 * part :, :].astype(F32)
    for third in range(3):
        rows = slice(third * part, (third + 1) * part)
        both = jnp.concatenate([mixer_ref[0, rows, :], mixer_ref[1, rows, :]], axis=0)
        qkv_ref[third] = both.astype(F32).T


def unpack(feed, mixer):
    width = feed.shape[2]
    half = width // 2
    return pl.pallas_call(
        unpack_kernel,
        out_shape=[
            jax.ShapeDtypeStruct((3, width, half), F32),
            jax.ShapeDtypeStruct((half, width), F32),
            jax.ShapeDtypeStruct((width, 2 * width), F32),
            jax.ShapeDtypeStruct((2 * width, width), F32),
        ],
        name="unpack",
        compiler_params=pltpu.CompilerParams(vmem_limit_bytes=VMEM_LIMIT),
    )(feed, mixer)


def route(change):
    shape = [lax.axis_size(axis) for axis in AXES]
    pairs = []
    for s in range(shape[0]):
        for d in range(shape[1]):
            for t in range(shape[2]):
                to = change(s, d, t)
                if to is not None:
                    pairs.append(((s * shape[1] + d) * shape[2] + t, (to[0] * shape[1] + to[1]) * shape[2] + to[2]))
    return pairs


def moved(block, change):
    return lax.ppermute(block, AXES, route(change))


def over_tensor(s, d, t):
    return (s, d, 1 - t)


def over_section(s, d, t):
    return (1 - s, d, t)


def over_both(s, d, t):
    return (1 - s, d, 1 - t)


def over_core(s, d, t):
    return (s, d ^ 1, t)


def along_z(distance):
    count = lax.axis_size("dp") // 2
    return lambda s, d, t: (s, (d // 2 + distance) % count * 2 + d % 2, t)


def tie(*values):
    return lax.optimization_barrier(values)


def take_part(block, which, count, axis=0):
    size = block.shape[axis] // count
    return lax.dynamic_slice_in_dim(block, which * size, size, axis)


def added(*terms):
    total = terms[0].astype(F32)
    for term in terms[1:]:
        total = total + term.astype(F32)
    return total.astype(terms[0].dtype)


def reordered(pieces, lane, core):
    pieces = jnp.where(lane == 0, pieces, pieces[jnp.array([2, 3, 0, 1])])
    return jnp.where(core == 0, pieces, pieces[jnp.array([1, 0, 3, 2])])


def one_sequence_each(
    inputs,
    cotangent,
    segment_ids,
    norm_gains,
    norm_biases,
    qkv_weight,
    qv_bias,
    out_weight,
    up_weight,
    up_bias,
    down_weight,
    out_biases,
):
    section = lax.axis_index("section")
    group = lax.axis_index("dp")
    lane = lax.axis_index("tensor")
    core = group % 2
    z_index = group // 2
    z_count = lax.axis_size("dp") // 2
    width = inputs.shape[2]
    hidden = up_bias.shape[1]
    cols = qkv_weight.shape[3]
    part = cols // 2
    mine = 2 * section + lane

    def own_half(array, axis):
        return take_part(array, core, 2, axis)

    mixer_own = jnp.concatenate(
        [
            own_half(qkv_weight[0], 2).transpose(0, 2, 1).reshape(3 * part, width),
            own_half(out_weight[0], 0),
        ],
        axis=0,
    )
    up_own = own_half(up_weight[0], 1)
    down_own = own_half(down_weight[0], 0)
    small = jnp.concatenate(
        [item.reshape(-1) for item in (norm_gains, norm_biases, qv_bias, up_bias, out_biases)]
    )

    def sequence_halves(array):
        kept = lax.dynamic_index_in_dim(array, mine, 0, keepdims=False)
        sent = lax.dynamic_index_in_dim(array, 2 * section + 1 - lane, 0, keepdims=False)
        return kept, sent

    def joined(kept, came):
        return jnp.where(lane == 0, jnp.concatenate([kept, came], 0), jnp.concatenate([came, kept], 0))

    segment = lax.dynamic_index_in_dim(segment_ids, mine, 0, keepdims=True)
    ids = jnp.arange(IMAGE_IDS, dtype=jnp.int32)[:, None]
    begin = jnp.sum((segment < ids).astype(jnp.int32), axis=1)
    end = jnp.sum((segment <= ids).astype(jnp.int32), axis=1)
    start = begin // TILE
    place = jnp.stack([lane, core, mine]).astype(jnp.int32)
    images = (place, start, (end - 1) // TILE - start + 1, segment)

    def params(vector):
        gains = vector[: 2 * width].reshape(2, width)
        shifts = vector[2 * width : 4 * width].reshape(2, width)
        qv = vector[4 * width : 6 * width].reshape(2, 4, part)
        up_shift = vector[6 * width : 6 * width + hidden].reshape(4, 1, hidden // 4)
        outs = vector[6 * width + hidden :].reshape(2, 1, width)
        zero = jnp.zeros((4, part), F32)
        qkv_shift = jnp.concatenate([qv[0], zero, qv[1]], axis=1)
        norms = [jnp.stack([gains[i], shifts[i]]) for i in range(2)]
        return norms, qkv_shift[:, :, None], up_shift, outs

    def by_layer(own, came):
        return jnp.where(section == 0, own, came), jnp.where(section == 1, own, came)

    kept, sent = sequence_halves(inputs)
    came, mixer_came, small_came, up_own = tie(
        moved(sent, over_tensor), moved(mixer_own, over_section), moved(small, over_section), up_own
    )
    up_came = moved(up_own, over_section)
    state = joined(kept, came)
    mixers = by_layer(mixer_own, mixer_came)
    layer_params = [params(vector) for vector in by_layer(small, small_came)]
    mixer_pieces = [[mixers[0], moved(mixers[0], over_core)], None]
    norms, qkv_shift, up_shift, outs = layer_params[0]
    mixer_a, beside, up_came = tie(
        mixer_forward(images, state, norms[0], qkv_shift, mixer_pieces[0]),
        moved(mixers[0], over_tensor),
        up_came,
    )
    ups = by_layer(up_own, up_came)
    mixer_pieces[0] = mixer_pieces[0] + [beside, moved(beside, over_core)]
    mixer_b, up_beside, up_twin, down_came = tie(
        mixer_forward(
            images,
            state,
            norms[0],
            qkv_shift,
            mixer_pieces[0][2:],
            2,
            (mixer_a[3], mixer_a[1]),
            mixer_pieces[0],
            outs[0],
        ),
        moved(ups[0], over_tensor),
        moved(ups[0], over_core),
        moved(down_own, over_section),
    )
    downs = by_layer(down_own, down_came)
    down_twin = moved(downs[0], over_core)
    feed_a, down_beside, up_corner = tie(
        feed_forward(
            place, mixer_b[3], norms[1], up_shift, outs[1], [ups[0], up_twin], [downs[0], down_twin], 0, False
        ),
        moved(downs[0], over_tensor),
        moved(up_beside, over_core),
    )
    up_pieces = [[ups[0], up_twin, up_beside, up_corner], None]
    down_pieces = [[downs[0], down_twin, down_beside, moved(down_beside, over_core)], None]
    feed_b, beside, twin = tie(
        feed_forward(
            place, mixer_b[3], norms[1], up_shift, feed_a[0], up_pieces[0][2:], down_pieces[0][2:], 2, True
        ),
        moved(mixers[1], over_tensor),
        moved(mixers[1], over_core),
    )
    first_out = feed_b[0]
    saved = [
        dict(
            state=state,
            normed=mixer_a[3],
            qkv=[mixer_a[0], mixer_a[0], mixer_b[0], mixer_b[0]],
            mixed=[mixer_a[1], mixer_a[1], mixer_b[1], mixer_b[1]],
            totals=[mixer_a[2], mixer_a[2], mixer_b[2], mixer_b[2]],
            at=[0, 1, 0, 1],
            middle=mixer_b[3],
            active=[feed_a[1], feed_a[1], feed_b[1], feed_b[1]],
            slope=[feed_a[2], feed_a[2], feed_b[2], feed_b[2]],
        )
    ]
    norms, qkv_shift, up_shift, outs = layer_params[1]
    mixer_pieces[1] = [mixers[1], twin, beside, moved(beside, over_core)]
    mixer_a, up_beside, up_twin, down_beside, down_twin = tie(
        mixer_forward(images, first_out, norms[0], qkv_shift, mixer_pieces[1], 0, None, mixer_pieces[1], outs[0]),
        moved(ups[1], over_tensor),
        moved(ups[1], over_core),
        moved(downs[1], over_tensor),
        moved(downs[1], over_core),
    )
    up_pieces[1] = [ups[1], up_twin, up_beside, moved(up_beside, over_core)]
    down_pieces[1] = [downs[1], down_twin, down_beside, moved(down_beside, over_core)]
    grad_kept, grad_sent = sequence_halves(cotangent)
    feed_a, grad_came = tie(
        feed_forward(place, mixer_a[4], norms[1], up_shift, outs[1], up_pieces[1], down_pieces[1], 0, True),
        moved(grad_sent, over_tensor),
    )
    second_out = feed_a[0]
    saved.append(
        dict(
            state=first_out,
            normed=mixer_a[3],
            qkv=[mixer_a[0]] * 4,
            mixed=[mixer_a[1]] * 4,
            totals=[mixer_a[2]] * 4,
            at=[0, 1, 2, 3],
            middle=mixer_a[4],
            active=[feed_a[1]] * 4,
            slope=[feed_a[2]] * 4,
        )
    )
    grad = joined(grad_kept, grad_came)

    def exchange(own, other):
        return [
            take_part(own, lane, 2),
            moved(take_part(own, 1 - lane, 2), over_tensor),
            moved(take_part(other, lane, 2), over_section),
            moved(take_part(other, 1 - lane, 2), over_both),
        ]

    out_parts = exchange(
        jnp.where(section == 0, first_out, second_out), jnp.where(section == 0, second_out, first_out)
    )

    def feed_back(layer, grad, rider=None):
        kept = saved[layer]
        return feed_backward(
            grad,
            kept["middle"],
            layer_params[layer][0][1],
            kept["active"],
            kept["slope"],
            kept["at"],
            up_pieces[layer],
            down_pieces[layer],
            layer,
            rider,
        )

    def mixer_back(layer, middle_grad):
        kept = saved[layer]
        return mixer_backward(
            images, middle_grad, kept["qkv"], kept["mixed"], kept["totals"], kept["at"], mixer_pieces[layer]
        )

    def input_back(layer, middle_grad, projected, finish=None):
        kept = saved[layer]
        return input_backward(
            kept["state"],
            middle_grad,
            layer_params[layer][0][0],
            projected,
            kept["normed"],
            kept["mixed"],
            kept["at"],
            mixer_pieces[layer],
            2 + layer,
            finish,
        )

    def send_feed(feed):
        kept, beside, across, far, spread = feed[:5]
        plane = [
            moved(block, change)
            for block, change in ((beside, over_tensor), (across, over_section), (far, over_both))
        ]
        groups = [list(range(which, 2 * z_count, 2)) for which in range(2)]
        return [kept] + plane + [lax.psum_scatter(spread, "dp", axis_index_groups=groups)]

    feed1, out_parts = tie(feed_back(1, grad), out_parts)
    came = send_feed(feed1)
    feed1, mixer1, came[:4] = tie(feed1, mixer_back(1, feed1[6]), came[:4])
    (mixer_sums1, in_grad1, in_small1), came = tie(input_back(1, feed1[6], mixer1[0]), came)
    feed0 = feed_back(0, in_grad1, [mixer_sums1, *came])
    mixer0, came = tie(mixer_back(0, feed0[6]), send_feed(feed0))
    feed_sum, mixer_sum, in_parts, vector = input_back(
        0,
        feed0[6],
        mixer0[0],
        [
            *came,
            feed0[9],
            feed0[8],
            in_grad1,
            feed0[7],
            feed0[5],
            mixer0[1],
            feed1[7],
            feed1[5],
            mixer1[1],
            in_small1,
        ],
    )
    qkv_grad, out_grad, up_grad, down_grad = unpack(feed_sum, mixer_sum.reshape(2, 4 * part, width))
    states = place_states(place, out_parts)
    grads = widen(in_parts)
    qv_grad = vector[12:16, : 3 * part].reshape(4, 3, part)
    return (
        states[None],
        grads[None],
        vector[0:2][None],
        vector[2:4][None],
        qkv_grad[None],
        jnp.stack([qv_grad[:, 0].reshape(width), qv_grad[:, 2].reshape(width)])[None],
        out_grad[None],
        up_grad[None],
        vector[8:12].reshape(1, hidden),
        down_grad[None],
        vector[4:6][None],
    )


def passed_along(block, axis, distance):
    devices = range(lax.axis_size(axis))
    route = [(i - distance, i) for i in devices if i - distance in devices]
    return lax.ppermute(block, axis, route)


def norm_parts(token_rows, gain_row, shift_row):
    centre = token_rows - jnp.mean(token_rows, axis=-1, keepdims=True)
    inverse = lax.rsqrt(jnp.mean(centre * centre, axis=-1, keepdims=True) + EPSILON)
    scaled = centre * inverse
    return (scaled * gain_row + shift_row, scaled, inverse)


def norm_back(gradient, scaled, inverse, gain_row):
    upstream = gradient * gain_row
    return inverse * (
        upstream
        - jnp.mean(upstream, axis=-1, keepdims=True)
        - scaled * jnp.mean(upstream * scaled, axis=-1, keepdims=True)
    )


def gelu_exact(values):
    return jax.nn.gelu(values, approximate=False)


def head_view(matrix, heads_local):
    return matrix.reshape(matrix.shape[0], heads_local, HEAD_DIM)


def join_heads(stacked):
    return stacked.transpose(1, 0, 2).reshape(stacked.shape[1], stacked.shape[0] * stacked.shape[2])


def attend_forward(queries, key_rows, value_rows, segment):
    seq_len = queries.shape[0]
    half_rows = seq_len // 2
    heads_local = queries.shape[1] // HEAD_DIM
    scaling = HEAD_DIM ** (-0.5)
    query_heads = head_view(queries, heads_local)
    key_heads = head_view(key_rows, heads_local)
    value_heads = head_view(value_rows, heads_local)

    def one_item(item):
        head_index = item // 2
        row_start = item % 2 * half_rows
        head_keys = lax.dynamic_index_in_dim(key_heads, head_index, 1, keepdims=False)
        head_values = lax.dynamic_index_in_dim(value_heads, head_index, 1, keepdims=False)
        head_queries = lax.dynamic_index_in_dim(query_heads, head_index, 1, keepdims=False)
        block_queries = lax.dynamic_slice_in_dim(head_queries, row_start, half_rows, 0)
        block_segment = lax.dynamic_slice_in_dim(segment, row_start, half_rows, 0)
        scores = (
            jnp.einsum("qd,kd->qk", block_queries, head_keys, preferred_element_type=jnp.float32)
            * scaling
        )
        scores = jnp.where(block_segment[:, None] == segment[None, :], scores, NEGATIVE)
        row_peak = jnp.max(scores, axis=-1, keepdims=True)
        expanded = jnp.exp(scores - row_peak)
        denominator = jnp.sum(expanded, axis=-1, keepdims=True)
        weights = (expanded / denominator).astype(jnp.bfloat16)
        block_out = jnp.dot(weights, head_values, preferred_element_type=jnp.float32).astype(
            jnp.bfloat16
        )
        return (block_out, row_peak[:, 0] + jnp.log(denominator[:, 0]))

    outputs, log_totals = lax.map(one_item, jnp.arange(2 * heads_local, dtype=jnp.int32))
    mixed_rows = join_heads(outputs.reshape(heads_local, seq_len, HEAD_DIM))
    return (mixed_rows, log_totals.reshape(heads_local, seq_len))


def attend_backward(queries, key_rows, value_rows, mixed_grad, log_totals, segment):
    seq_len = queries.shape[0]
    half_rows = seq_len // 2
    heads_local = queries.shape[1] // HEAD_DIM
    scaling = HEAD_DIM ** (-0.5)
    query_heads = head_view(queries, heads_local)
    key_heads = head_view(key_rows, heads_local)
    value_heads = head_view(value_rows, heads_local)
    grad_heads = head_view(mixed_grad, heads_local)

    def one_head(head_index):
        head_queries = lax.dynamic_index_in_dim(query_heads, head_index, 1, keepdims=False)
        head_keys = lax.dynamic_index_in_dim(key_heads, head_index, 1, keepdims=False)
        head_values = lax.dynamic_index_in_dim(value_heads, head_index, 1, keepdims=False)
        head_grads = lax.dynamic_index_in_dim(grad_heads, head_index, 1, keepdims=False)
        head_totals = lax.dynamic_index_in_dim(log_totals, head_index, 0, keepdims=False)

        def one_block(carry, block_index):
            key_grad, value_grad = carry
            row_start = block_index * half_rows
            block_queries = lax.dynamic_slice_in_dim(head_queries, row_start, half_rows, 0)
            block_grads = lax.dynamic_slice_in_dim(head_grads, row_start, half_rows, 0)
            block_totals = lax.dynamic_slice_in_dim(head_totals, row_start, half_rows, 0)
            block_segment = lax.dynamic_slice_in_dim(segment, row_start, half_rows, 0)
            scores = (
                jnp.einsum(
                    "qd,kd->qk", block_queries, head_keys, preferred_element_type=jnp.float32
                )
                * scaling
            )
            scores = jnp.where(block_segment[:, None] == segment[None, :], scores, NEGATIVE)
            weights = jnp.exp(scores - block_totals[:, None])
            low_weights = weights.astype(jnp.bfloat16)
            block_out = jnp.dot(
                low_weights, head_values, preferred_element_type=jnp.float32
            ).astype(jnp.bfloat16)
            weight_grads = jnp.einsum(
                "qd,kd->qk", block_grads, head_values, preferred_element_type=jnp.float32
            )
            row_terms = jnp.sum(weights * weight_grads, axis=-1, keepdims=True)
            score_grads = (weights * (weight_grads - row_terms)).astype(jnp.bfloat16)
            query_grad = (
                jnp.dot(score_grads, head_keys, preferred_element_type=jnp.float32) * scaling
            )
            key_grad = (
                key_grad
                + jnp.einsum(
                    "qk,qd->kd", score_grads, block_queries, preferred_element_type=jnp.float32
                )
                * scaling
            )
            value_grad = value_grad + jnp.einsum(
                "qk,qd->kd", low_weights, block_grads, preferred_element_type=jnp.float32
            )
            return ((key_grad, value_grad), (block_out, query_grad))

        empty = jnp.zeros((seq_len, HEAD_DIM), jnp.float32)
        (key_grad, value_grad), (block_outs, query_grads) = lax.scan(
            one_block, (empty, empty), jnp.arange(2, dtype=jnp.int32)
        )
        return (
            block_outs.reshape(seq_len, HEAD_DIM),
            query_grads.reshape(seq_len, HEAD_DIM),
            key_grad,
            value_grad,
        )

    results = lax.map(one_head, jnp.arange(heads_local, dtype=jnp.int32))
    return tuple((join_heads(item) for item in results))


def store_at(array, value, which, running):
    return array.at[which].set(jnp.where(running, value, array[which]))


def pipelined(
    inputs,
    cotangent,
    segment_ids,
    norm_gains,
    norm_biases,
    qkv_weight,
    qv_bias,
    out_weight,
    up_weight,
    up_bias,
    down_weight,
    out_biases,
):
    section_index = lax.axis_index("section")
    section_count = lax.axis_size("section")
    lane_index = lax.axis_index("tensor")
    micro_count, own_rows, model_width = inputs.shape
    seq_len = segment_ids.shape[1]
    cols_local = qkv_weight.shape[3]
    hidden_local = up_weight.shape[2]
    heads_local = cols_local // HEAD_DIM
    gain_rows = norm_gains[0]
    shift_rows = norm_biases[0]
    joined = jnp.concatenate([qkv_weight[0, 0], qkv_weight[0, 1], qkv_weight[0, 2]], axis=1)
    query_shift = lax.dynamic_slice_in_dim(qv_bias[0, 0], lane_index * cols_local, cols_local)
    value_shift = lax.dynamic_slice_in_dim(qv_bias[0, 1], lane_index * cols_local, cols_local)
    up_shift = lax.dynamic_slice_in_dim(up_bias[0], lane_index * hidden_local, hidden_local)
    out_matrix = out_weight[0]
    up_matrix = up_weight[0]
    down_matrix = down_weight[0]
    mixer_shift = out_biases[0, 0]
    feed_shift = out_biases[0, 1]

    def spread_rows(normed_rows, weight):
        return (
            None,
            jnp.dot(
                lax.all_gather(normed_rows, "tensor", axis=0, tiled=True),
                weight,
                preferred_element_type=jnp.float32,
            ),
        )

    def regather(normed_rows):
        return lax.all_gather(normed_rows, "tensor", axis=0, tiled=True)

    def gather_grads(grad_rows):
        return lax.all_gather(grad_rows.astype(jnp.bfloat16), "tensor", axis=0, tiled=True)

    def branch_sum(left_rows, weight):
        return lax.psum_scatter(
            jnp.dot(left_rows, weight, preferred_element_type=jnp.float32).astype(jnp.bfloat16),
            "tensor",
            scatter_dimension=0,
            tiled=True,
        ).astype(jnp.float32)

    def input_sum(grad_rows, weight):
        return lax.psum_scatter(
            jnp.einsum("sc,dc->sd", grad_rows, weight, preferred_element_type=jnp.float32).astype(
                jnp.bfloat16
            ),
            "tensor",
            scatter_dimension=0,
            tiled=True,
        ).astype(jnp.float32)

    def split_projected(projected):
        queries = (projected[:, :cols_local] + query_shift).astype(jnp.bfloat16)
        key_rows = projected[:, cols_local : 2 * cols_local].astype(jnp.bfloat16)
        value_rows = (projected[:, 2 * cols_local :] + value_shift).astype(jnp.bfloat16)
        return (queries, key_rows, value_rows)

    def layer_backward(block_in, middle, log_totals, segment, out_grad):
        residual = block_in.astype(jnp.float32)
        full_grad = gather_grads(out_grad)
        normed_two, scaled_two, inverse_two = norm_parts(middle, gain_rows[1], shift_rows[1])
        normed_two = normed_two.astype(jnp.bfloat16)
        full_two = regather(normed_two)
        hidden = jnp.dot(full_two, up_matrix, preferred_element_type=jnp.float32) + up_shift
        active, gelu_pullback = jax.vjp(gelu_exact, hidden)
        active = active.astype(jnp.bfloat16)
        down_grad = jnp.einsum("sf,sd->fd", active, full_grad, preferred_element_type=jnp.float32)
        active_grad = jnp.einsum(
            "sd,fd->sf", full_grad, down_matrix, preferred_element_type=jnp.float32
        )
        hidden_grad = gelu_pullback(active_grad)[0]
        up_shift_grad = jnp.sum(hidden_grad, axis=0)
        hidden_low = hidden_grad.astype(jnp.bfloat16)
        up_grad = jnp.einsum("sd,sf->df", full_two, hidden_low, preferred_element_type=jnp.float32)
        normed_grad_two = input_sum(hidden_low, up_matrix)
        feed_shift_grad = jnp.sum(out_grad, axis=0)
        middle_grad = out_grad + norm_back(normed_grad_two, scaled_two, inverse_two, gain_rows[1])
        gain_two = jnp.sum(normed_grad_two * scaled_two, axis=0)
        shift_two = jnp.sum(normed_grad_two, axis=0)
        full_mid_grad = gather_grads(middle_grad)
        normed_one, scaled_one, inverse_one = norm_parts(residual, gain_rows[0], shift_rows[0])
        normed_one = normed_one.astype(jnp.bfloat16)
        full_one = regather(normed_one)
        projected = jnp.dot(full_one, joined, preferred_element_type=jnp.float32)
        queries, key_rows, value_rows = split_projected(projected)
        mixed_grad = jnp.einsum(
            "sd,cd->sc", full_mid_grad, out_matrix, preferred_element_type=jnp.float32
        ).astype(jnp.bfloat16)
        mixed_rows, query_grad, key_grad, value_grad = attend_backward(
            queries, key_rows, value_rows, mixed_grad, log_totals, segment
        )
        out_grad_matrix = jnp.einsum(
            "sc,sd->cd", mixed_rows, full_mid_grad, preferred_element_type=jnp.float32
        )
        mixer_shift_grad = jnp.sum(middle_grad, axis=0)
        qkv_low = jnp.concatenate([query_grad, key_grad, value_grad], axis=1).astype(jnp.bfloat16)
        joined_grad = jnp.einsum("sd,sc->dc", full_one, qkv_low, preferred_element_type=jnp.float32)
        normed_grad_one = input_sum(qkv_low, joined)
        in_grad = middle_grad + norm_back(normed_grad_one, scaled_one, inverse_one, gain_rows[0])
        gain_one = jnp.sum(normed_grad_one * scaled_one, axis=0)
        shift_one = jnp.sum(normed_grad_one, axis=0)
        qv_local = jnp.stack([jnp.sum(query_grad, axis=0), jnp.sum(value_grad, axis=0)])
        qv_full = lax.dynamic_update_slice_in_dim(
            jnp.zeros((2, model_width), jnp.float32), qv_local, lane_index * cols_local, 1
        )
        up_full = lax.dynamic_update_slice_in_dim(
            jnp.zeros((up_bias.shape[1],), jnp.float32), up_shift_grad, lane_index * hidden_local, 0
        )
        weight_terms = (joined_grad, out_grad_matrix, up_grad, down_grad)
        small_terms = (
            jnp.stack([gain_one, gain_two]),
            jnp.stack([shift_one, shift_two]),
            qv_full,
            up_full,
            jnp.stack([mixer_shift_grad, feed_shift_grad]),
        )
        return (in_grad, weight_terms, small_terms)

    ticks = micro_count + section_count - 1
    received = jnp.zeros((own_rows, model_width), jnp.bfloat16)
    saved_in = jnp.zeros_like(inputs)
    saved_mid = jnp.zeros((micro_count, own_rows, model_width), jnp.float32)
    saved_totals = jnp.zeros((micro_count, heads_local, seq_len), jnp.float32)
    states = jnp.zeros_like(inputs)
    for tick in range(ticks):
        micro = tick - section_index
        running = (micro >= 0) & (micro < micro_count)
        which = jnp.clip(micro, 0, micro_count - 1)
        own_in = lax.dynamic_index_in_dim(inputs, which, 0, keepdims=False)
        block_in = jnp.where(section_index == 0, own_in, received)
        segment = lax.dynamic_index_in_dim(segment_ids, which, 0, keepdims=False)
        layer_residual = block_in.astype(jnp.float32)
        layer_normed_one = norm_parts(layer_residual, gain_rows[0], shift_rows[0])[0].astype(
            jnp.bfloat16
        )
        layer_full_one, layer_projected = spread_rows(layer_normed_one, joined)
        layer_queries, layer_key_rows, layer_value_rows = split_projected(layer_projected)
        layer_mixed_rows, layer_log_totals = attend_forward(
            layer_queries, layer_key_rows, layer_value_rows, segment
        )
        layer_middle = layer_residual + branch_sum(layer_mixed_rows, out_matrix) + mixer_shift
        layer_normed_two = norm_parts(layer_middle, gain_rows[1], shift_rows[1])[0].astype(
            jnp.bfloat16
        )
        layer_full_two, layer_hidden = spread_rows(layer_normed_two, up_matrix)
        layer_active = gelu_exact(layer_hidden + up_shift).astype(jnp.bfloat16)
        block_out = layer_middle + branch_sum(layer_active, down_matrix) + feed_shift
        block_out, middle, log_totals, full_one, full_two = (
            block_out,
            layer_middle,
            layer_log_totals,
            layer_full_one,
            layer_full_two,
        )
        handed = block_out.astype(jnp.bfloat16)
        saved_in = store_at(saved_in, block_in, which, running)
        saved_mid = store_at(saved_mid, middle, which, running)
        saved_totals = store_at(saved_totals, log_totals, which, running)
        states = store_at(states, handed, which, running)
        if tick + 1 < ticks:
            received = passed_along(handed, "section", 1)
    back_received = jnp.zeros((own_rows, model_width), jnp.bfloat16)
    weight_totals = (
        jnp.zeros(joined.shape, jnp.float32),
        jnp.zeros(out_matrix.shape, jnp.float32),
        jnp.zeros(up_matrix.shape, jnp.float32),
        jnp.zeros(down_matrix.shape, jnp.float32),
    )
    small_totals = (
        jnp.zeros((2, model_width), jnp.float32),
        jnp.zeros((2, model_width), jnp.float32),
        jnp.zeros((2, model_width), jnp.float32),
        jnp.zeros((up_bias.shape[1],), jnp.float32),
        jnp.zeros((2, model_width), jnp.float32),
    )
    grads_store = jnp.zeros((micro_count, own_rows, model_width), jnp.float32)
    for tick in range(ticks):
        micro = tick - (section_count - 1) + section_index
        running = (micro >= 0) & (micro < micro_count)
        which = jnp.clip(micro, 0, micro_count - 1)
        own_grad = lax.dynamic_index_in_dim(cotangent, which, 0, keepdims=False)
        out_grad = jnp.where(section_index == section_count - 1, own_grad, back_received).astype(
            jnp.float32
        )
        in_grad, weight_terms, small_terms = layer_backward(
            lax.dynamic_index_in_dim(saved_in, which, 0, keepdims=False),
            lax.dynamic_index_in_dim(saved_mid, which, 0, keepdims=False),
            lax.dynamic_index_in_dim(saved_totals, which, 0, keepdims=False),
            lax.dynamic_index_in_dim(segment_ids, which, 0, keepdims=False),
            out_grad,
        )
        joined_term, out_term, up_term, down_term = tuple(
            (jnp.where(running, term, 0.0) for term in weight_terms)
        )
        weight_terms = (joined_term, out_term, up_term, down_term)
        weight_totals = tuple((total + term for total, term in zip(weight_totals, weight_terms)))
        small_totals = tuple(
            (
                total + jnp.where(running, term, 0.0)
                for total, term in zip(small_totals, small_terms)
            )
        )
        grads_store = store_at(grads_store, in_grad, which, running)
        if tick + 1 < ticks:
            back_received = passed_along(in_grad.astype(jnp.bfloat16), "section", -1)
    joined_total, out_total, up_total, down_total = weight_totals
    summed = (
        lax.psum(joined_total.astype(jnp.bfloat16), "dp").astype(jnp.float32),
        lax.psum(out_total.astype(jnp.bfloat16), "dp").astype(jnp.float32),
        lax.psum(up_total.astype(jnp.bfloat16), "dp").astype(jnp.float32),
        lax.psum(down_total.astype(jnp.bfloat16), "dp").astype(jnp.float32),
    )
    gain_total, shift_total, qv_total, up_shift_total, out_shift_total = small_totals
    small_summed = lax.psum(
        (gain_total, shift_total, qv_total, up_shift_total, out_shift_total), ("dp", "tensor")
    )
    qkv_grad = summed[0].reshape(model_width, 3, cols_local).transpose(1, 0, 2)
    return (
        states[None],
        grads_store[None],
        small_summed[0][None],
        small_summed[1][None],
        qkv_grad[None],
        small_summed[2][None],
        summed[1][None],
        summed[2][None],
        small_summed[3][None],
        summed[3][None],
        small_summed[4][None],
    )


def solution(mesh):
    placed = (
        P("dp", "tensor", None),
        P("dp", "tensor", None),
        P("dp", None),
        P("section", None, None),
        P("section", None, None),
        P("section", None, None, "tensor"),
        P("section", None, None),
        P("section", "tensor", None),
        P("section", None, "tensor"),
        P("section", None),
        P("section", "tensor", None),
        P("section", None, None),
    )
    sizes = dict(mesh.shape)

    def on_device(inputs, *rest):
        each = inputs.shape[0] == sizes["section"] * sizes["tensor"]
        paired = sizes["section"] == 2 and sizes["tensor"] == 2 and sizes["dp"] % 2 == 0
        if each and paired and sizes["dp"] == 8:
            return one_sequence_each(inputs, *rest)
        return pipelined(inputs, *rest)

    return jax.shard_map(
        on_device,
        mesh=mesh,
        in_specs=placed,
        out_specs=(
            P("section", "dp", "tensor", None),
            P("section", "dp", "tensor", None),
            P("section", None, None),
            P("section", None, None),
            P("section", None, None, "tensor"),
            P("section", None, None),
            P("section", "tensor", None),
            P("section", None, "tensor"),
            P("section", None),
            P("section", "tensor", None),
            P("section", None, None),
        ),
        check_vma=False,
    )
```

```python
import functools
import math

import jax
import jax.numpy as jnp
from jax import lax
from jax.experimental import pallas as pl
from jax.experimental.pallas import tpu as pltpu
from jax.sharding import PartitionSpec as P

HEAD_DIM = 48
IMAGE_IDS = 5
IMAGE_MOST = 512
EPSILON = 1e-05
NEGATIVE = -1e30
TILE = 128
BLOCK = 256
EXTRA = 16
LOG2E = math.log2(math.e)
SCALING = HEAD_DIM ** (-0.5)
AXES = ("section", "dp", "tensor")
VMEM_LIMIT = 60 * 1024 * 1024
MESH = pl.DeviceIdType.MESH
F32 = jnp.float32
BF16 = jnp.bfloat16


def nn(left, right):
    return lax.dot_general(left, right, (((1,), (0,)), ((), ())), preferred_element_type=F32)


def nt(left, right):
    return lax.dot_general(left, right, (((1,), (1,)), ((), ())), preferred_element_type=F32)


def tn(left, right):
    return lax.dot_general(left, right, (((0,), (0,)), ((), ())), preferred_element_type=F32)


def normalise(rows):
    centre = rows - jnp.mean(rows, axis=-1, keepdims=True)
    inverse = lax.rsqrt(jnp.mean(centre * centre, axis=-1, keepdims=True) + EPSILON)
    return centre * inverse, inverse


def normalise_back(gradient, scaled, inverse, gain):
    upstream = gradient * gain
    return inverse * (
        upstream
        - jnp.mean(upstream, axis=-1, keepdims=True)
        - scaled * jnp.mean(upstream * scaled, axis=-1, keepdims=True)
    )


def gelu_pair(values):
    share = 0.5 + 0.5 * lax.erf(values * math.sqrt(0.5))
    bell = jnp.exp2(values * values * (-0.5 * LOG2E))
    return values * share, share + values * bell * (1.0 / math.sqrt(2 * math.pi))


def extra_rows(rows, width):
    at = lax.broadcasted_iota(jnp.int32, (EXTRA, width), 0)
    out = jnp.zeros((EXTRA, width), F32)
    for index, row in enumerate(rows):
        out = jnp.where(at == index, row, out)
    return out.astype(BF16)


def three_parts(row):
    first = row.astype(BF16).astype(F32)
    second = (row - first).astype(BF16).astype(F32)
    return [first, second, row - first - second]


def each_image(start_ref, tiles_ref, body):
    most = IMAGE_MOST // TILE + 1

    def image(index, carry):
        first = start_ref[index]
        tiles = tiles_ref[index]
        for count in range(1, most + 1):

            @pl.when(tiles == count)
            def _():
                body(index, pl.multiple_of(first * TILE, TILE), count * TILE)

        return carry

    lax.fori_loop(0, IMAGE_IDS, image, 0)


def run_copies(copies):
    for copy in copies:
        copy.start()


def wait_copies(copies):
    for copy in copies:
        copy.wait()


def slot_of(place_ref, index):
    return 2 * (place_ref[0] ^ (index // 2)) + (place_ref[1] ^ (index % 2))


def once(shape):
    zeros = (0,) * len(shape)
    return pl.BlockSpec(shape, lambda *_: zeros, pipeline_mode=pl.Buffered(1))


def anywhere(count):
    return [pl.BlockSpec(memory_space=pl.ANY)] * count


def settings(flops, collective=None):
    remote = {} if collective is None else dict(collective_id=collective, has_side_effects=True)
    return dict(
        compiler_params=pltpu.CompilerParams(vmem_limit_bytes=VMEM_LIMIT, **remote),
        cost_estimate=pl.CostEstimate(flops=flops, bytes_accessed=1_000_000, transcendentals=0),
    )


def blocks_of(ref, axis=0):
    return ref.shape[axis] // BLOCK


def block_at(index):
    return pl.ds(pl.multiple_of(index * BLOCK, BLOCK), BLOCK)


def big_blocks(rows):
    size = rows // 2
    return [slice(i * size, (i + 1) * size) for i in range(2)]


def attend_forward_image(index, at, width, heads, seg_ref, qkv_ref, store):
    win = pl.ds(at, width)
    mine = seg_ref[:, win] == index
    mask = jnp.where(mine, 0.0, NEGATIVE)
    one = jnp.ones((1, width), F32)
    query_extra = extra_rows([mask, one], width)
    key_extra = extra_rows([one, mask], width)
    value_extra = extra_rows([one], width)
    cols = heads * HEAD_DIM

    def rows_of(third, head):
        low = third * cols + head * HEAD_DIM
        return qkv_ref[low : low + HEAD_DIM, win]

    def scores(head):
        queries = jnp.concatenate([rows_of(0, head), query_extra], axis=0)
        keys = jnp.concatenate([rows_of(1, head), key_extra], axis=0)
        return tn(keys, queries)

    following = scores(0)
    for head in range(heads):
        current = following
        if head + 1 < heads:
            following = scores(head + 1)
        peak = jnp.max(current, axis=0, keepdims=True)
        weights = jnp.exp2(current - peak).astype(BF16)
        mixed = nn(jnp.concatenate([rows_of(2, head), value_extra], axis=0), weights)
        total = mixed[HEAD_DIM : HEAD_DIM + 1]
        store(head, win, mine, mixed[:HEAD_DIM] * (1.0 / total), peak + jnp.log2(total))


def attend_backward_image(index, at, width, heads, seg_ref, qkv_ref, mixed_ref, total_ref, mixed_grad, sums):
    win = pl.ds(at, width)
    mine = seg_ref[:, win] == index
    mask = jnp.where(mine, 0.0, NEGATIVE)
    one = jnp.ones((1, width), F32)
    key_extra = extra_rows([one, mask, one, one, one], width)
    value_extra = extra_rows([one, one, one], width)
    cols = heads * HEAD_DIM

    def span(third, head):
        low = third * cols + head * HEAD_DIM
        return slice(low, low + HEAD_DIM)

    def products(head):
        own = span(0, head)
        grads = mixed_grad[own, win]
        inner = jnp.sum(grads.astype(F32) * mixed_ref[own, win].astype(F32), axis=0, keepdims=True)
        query_extra = extra_rows([mask, one] + three_parts(-total_ref[head, :, win]), width)
        grad_extra = extra_rows(three_parts(-inner), width)
        keys = jnp.concatenate([qkv_ref[span(1, head), win], key_extra], axis=0)
        queries = jnp.concatenate([qkv_ref[own, win], query_extra], axis=0)
        values = jnp.concatenate([qkv_ref[span(2, head), win], value_extra], axis=0)
        return tn(keys, queries), tn(values, jnp.concatenate([grads, grad_extra], axis=0))

    following = products(0)
    for head in range(heads):
        scores, terms = following
        if head + 1 < heads:
            following = products(head + 1)
        weights = jnp.exp2(scores)
        score_grads = (weights * terms).astype(BF16)
        sums[span(0, head), win] += nn(qkv_ref[span(1, head), win], score_grads) * SCALING
        sums[span(1, head), win] += nt(qkv_ref[span(0, head), win], score_grads) * (1.0 / LOG2E)
        sums[span(2, head), win] += nt(mixed_grad[span(0, head), win], weights.astype(BF16))


def mixer_forward_kernel(
    place_ref, start_ref, tiles_ref, seg_ref, hidden_ref, norm_ref, qkv_shift_ref, *rest, pieces, out_pieces, heads
):
    first = out_pieces in (0, pieces)
    last = out_pieces > 0
    rest = list(rest)
    weights = [rest.pop(0) for _ in range(pieces)]
    if not first:
        normed_in = rest.pop(0)
        mixed_before = rest.pop(0)
    if last:
        out_weights = [rest.pop(0) for _ in range(out_pieces)]
        out_shift_ref = rest.pop(0)
    qkv_ref, mixed_ref, total_ref = rest.pop(0), rest.pop(0), rest.pop(0)
    if first:
        normed_out = rest.pop(0)
    if last:
        middle_ref = rest.pop(0)
    weight, normed, sems = rest.pop(0), rest.pop(0), rest.pop(0)
    if last:
        out_weight, mixed_all, out_sems = rest
    step = pl.program_id(0)
    cols = heads * HEAD_DIM
    before = out_pieces - pieces if last else 0
    copies = [
        pltpu.make_async_copy(
            weights[i].at[0 : 3 * cols], weight.at[i], sems.at[i]
        )
        for i in range(pieces)
    ]
    if not first:
        norm_copy = pltpu.make_async_copy(normed_in, normed, sems.at[pieces])
    out_copies = []
    if last:
        for i in range(out_pieces):
            out_copies.append(
                pltpu.make_async_copy(
                    out_weights[i].at[3 * cols : 4 * cols],
                    out_weight.at[i * cols : (i + 1) * cols],
                    out_sems.at[i],
                )
            )
        for i in range(before):
            out_copies.append(
                pltpu.make_async_copy(
                    mixed_before.at[i], mixed_all.at[i * cols : (i + 1) * cols], out_sems.at[out_pieces + i]
                )
            )

    @pl.when(step == 0)
    def _():
        if not first:
            norm_copy.start()
        run_copies(copies + out_copies)
        if first:

            def norm_block(i, carry):
                rows = block_at(i)
                scaled, _ = normalise(hidden_ref[rows, :].astype(F32))
                result = (scaled * norm_ref[0:1, :] + norm_ref[1:2, :]).astype(BF16)
                normed[rows, :] = result
                normed_out[rows, :] = result
                return carry

            lax.fori_loop(0, blocks_of(hidden_ref), norm_block, 0)
        else:
            norm_copy.wait()

    for index in range(pieces):

        @pl.when(step == index)
        def _():
            copies[index].wait()

    projected = nt(weight[step], normed[...]) + qkv_shift_ref[0]
    qkv_ref[0, 0:cols, :] = (projected[0:cols] * (SCALING * LOG2E)).astype(BF16)
    qkv_ref[0, cols : 3 * cols, :] = projected[cols : 3 * cols].astype(BF16)

    def store(head, win, mine, mixed, total):
        rows = slice(head * HEAD_DIM, (head + 1) * HEAD_DIM)
        old = mixed_ref[0, rows, win].astype(F32)
        mixed_ref[0, rows, win] = jnp.where(mine, mixed, old).astype(BF16)
        total_ref[head, :, win] = jnp.where(mine, total, total_ref[head, :, win])

    each_image(
        start_ref,
        tiles_ref,
        lambda index, at, width: attend_forward_image(
            index, at, width, heads, seg_ref, qkv_ref.at[0], store
        ),
    )
    if last:
        mixed_all[pl.ds(pl.multiple_of((before + step) * cols, cols), cols), :] = mixed_ref[0]

        @pl.when(step == pieces - 1)
        def _():
            wait_copies(out_copies)

            for rows in big_blocks(hidden_ref.shape[0]):
                branch = tn(mixed_all[:, rows], out_weight[...])
                middle_ref[rows, :] = hidden_ref[rows, :].astype(F32) + branch + out_shift_ref[...]


def mixer_forward(images, hidden, norm, qkv_shift, pieces, offset=0, before=None, out_pieces=(), out_shift=None):
    rows, width = hidden.shape
    count = len(pieces)
    cols = width // 4
    heads = cols // HEAD_DIM
    place, start, tiles, segment = images
    operands = list(pieces)
    outs = [
        jax.ShapeDtypeStruct((count, 3 * cols, rows), BF16),
        jax.ShapeDtypeStruct((count, cols, rows), BF16),
        jax.ShapeDtypeStruct((count * heads, 1, rows), F32),
    ]
    scratch = [
        pltpu.VMEM((count, 3 * cols, width), BF16),
        pltpu.VMEM((rows, width), BF16),
        pltpu.SemaphoreType.DMA((count + 1,)),
    ]
    if before is None:
        outs.append(jax.ShapeDtypeStruct((rows, width), BF16))
    else:
        operands += list(before)
    specs = anywhere(len(operands) + len(out_pieces))
    operands += list(out_pieces)
    if out_pieces:
        operands.append(out_shift)
        specs.append(once((1, width)))
        outs.append(jax.ShapeDtypeStruct((rows, width), F32))
        scratch += [
            pltpu.VMEM((width, width), BF16),
            pltpu.VMEM((width, rows), BF16),
            pltpu.SemaphoreType.DMA((2 * len(out_pieces),)),
        ]
    return pl.pallas_call(
        functools.partial(
            mixer_forward_kernel,
            pieces=count,
            out_pieces=len(out_pieces),
            heads=heads,
        ),
        grid_spec=pltpu.PrefetchScalarGridSpec(
            num_scalar_prefetch=3,
            grid=(count,),
            in_specs=[
                once((1, rows)),
                once((rows, width)),
                once((2, width)),
                pl.BlockSpec((1, 3 * cols, 1), lambda i, place, *_: (slot_of(place, i + offset), 0, 0)),
            ]
            + specs,
            out_specs=[
                pl.BlockSpec((1, 3 * cols, rows), lambda i, *_: (i, 0, 0)),
                pl.BlockSpec((1, cols, rows), lambda i, *_: (i, 0, 0)),
                pl.BlockSpec((heads, 1, rows), lambda i, *_: (i, 0, 0)),
            ]
            + [once((rows, width))] * (len(outs) - 3),
            scratch_shapes=scratch,
        ),
        out_shape=outs,
        name="mixer_forward",
        **settings(4_000_000_000),
    )(place, start, tiles, segment, hidden, norm, qkv_shift, *operands)


def feed_forward_kernel(place_ref, middle_ref, norm_ref, up_shift_ref, start_ref, *rest, pieces, offset, last):
    ups, downs = rest[:pieces], rest[pieces : 2 * pieces]
    out_ref, active_ref, slope_ref, up_weight, down_weight, sems = rest[2 * pieces :]
    step = pl.program_id(0)
    size = up_weight.shape[2]
    copies = []
    for i in range(pieces):
        copies.append(
            pltpu.make_async_copy(ups[i], up_weight.at[i], sems.at[0, i])
        )
        copies.append(
            pltpu.make_async_copy(downs[i], down_weight.at[i], sems.at[1, i])
        )

    @pl.when(step == 0)
    def _():
        run_copies(copies)

    scaled, _ = normalise(middle_ref[...])
    normed = (scaled * norm_ref[0:1, :] + norm_ref[1:2, :]).astype(BF16)
    total = start_ref[...] if offset else middle_ref[...] + start_ref[...]

    @pl.when(step == 0)
    def _():
        wait_copies(copies)

    def raise_by(index):
        return nn(normed, up_weight[index]) + up_shift_ref[slot_of(place_ref, offset + index)]

    following = raise_by(0)
    for index in range(pieces):
        raised = following
        if index + 1 < pieces:
            following = raise_by(index + 1)
        part = pl.ds(index * size, size)
        active, slope = gelu_pair(raised)
        active = active.astype(BF16)
        active_ref[:, part] = active
        slope_ref[:, part] = slope.astype(BF16)
        total = total + nn(active, down_weight[index])
    out_ref[...] = total.astype(out_ref.dtype)


def feed_forward(place, middle, norm, up_shift, begin, ups, downs, offset, last):
    rows, width = middle.shape
    pieces = len(ups)
    size = up_shift.shape[2]
    hidden = size * pieces
    return pl.pallas_call(
        functools.partial(
            feed_forward_kernel,
            pieces=pieces,
            offset=offset,
            last=last,
        ),
        grid_spec=pltpu.PrefetchScalarGridSpec(
            num_scalar_prefetch=1,
            grid=(rows // BLOCK,),
            in_specs=[
                pl.BlockSpec((BLOCK, width), lambda i, *_: (i, 0)),
                once((2, width)),
                once(up_shift.shape),
                pl.BlockSpec((BLOCK, width), lambda i, *_: (i, 0)) if offset else once((1, width)),
            ]
            + anywhere(2 * pieces),
            out_specs=[
                pl.BlockSpec((BLOCK, width), lambda i, *_: (i, 0)),
                pl.BlockSpec((BLOCK, hidden), lambda i, *_: (i, 0)),
                pl.BlockSpec((BLOCK, hidden), lambda i, *_: (i, 0)),
            ],
            scratch_shapes=[
                pltpu.VMEM((pieces, width, size), BF16),
                pltpu.VMEM((pieces, size, width), BF16),
                pltpu.SemaphoreType.DMA((2, pieces)),
            ],
        ),
        out_shape=[
            jax.ShapeDtypeStruct((rows, width), BF16 if last else F32),
            jax.ShapeDtypeStruct((rows, hidden), BF16),
            jax.ShapeDtypeStruct((rows, hidden), BF16),
        ],
        name="feed_forward",
        **settings(4_000_000_000),
    )(place, middle, norm, up_shift, begin, *ups, *downs)


ORDER = (1, 3, 0, 2)


class Neighbours:
    def __init__(self, count):
        self.section, self.group, self.lane = [lax.axis_index(axis) for axis in AXES]
        self.core = lax.rem(self.group, 2)
        self.z_index = self.group // 2
        self.count = count
        self.twin = (self.section, self.group + 1 - 2 * self.core, self.lane)
        self.beside = (self.section, self.group, 1 - self.lane)
        self.across = (1 - self.section, self.group, self.lane)
        self.far = (1 - self.section, self.group, 1 - self.lane)
        self.line = [self.along(step) for step in range(1, count)]

    def along(self, step):
        return (self.section, lax.rem(self.z_index + step + self.count, self.count) * 2 + self.core, self.lane)

    def slot_of(self, index):
        return 2 * (self.lane + (index // 2) * (1 - 2 * self.lane)) + self.core + (index % 2) * (1 - 2 * self.core)


def greet(devices):
    barrier = pltpu.get_barrier_semaphore()
    for device in devices:
        pl.semaphore_signal(barrier, inc=1, device_id=device, device_id_type=MESH)
    pl.semaphore_wait(barrier, len(devices))


class Remote:
    def __init__(self, sends, receives):
        self.sends, self.receives, self.slot = sends, receives, 0

    def reserve(self, number):
        self.slot += number
        return self.slot - number

    def copy(self, source, target, device, slot=None):
        slot = self.reserve(1) if slot is None else slot
        return pltpu.make_async_remote_copy(
            src_ref=source,
            dst_ref=target,
            send_sem=self.sends.at[slot],
            recv_sem=self.receives.at[slot],
            device_id=device,
            device_id_type=MESH,
        )


def sum_with_core(index, copies, grad_of, sent, came, put):
    slot = index % 2
    if index < 2:

        def keep(where, value):
            sent[(slot,) + where] = value.astype(BF16)

        grad_of(keep)
        copies[slot].start()
    else:
        copies[slot].wait_recv()

        def add(where, value):
            put(slot, where, (value + came[(slot,) + where].astype(F32)).astype(BF16))

        grad_of(add)
        copies[slot].wait_send()


def plane_copies(remote, near, sums, target, columns):
    size = sums.shape[1] // 2
    mine = pl.ds(pl.multiple_of(near.section * size, size), size)
    theirs = pl.ds(pl.multiple_of((1 - near.section) * size, size), size)
    return [
        remote.copy(sums.at[1, mine, columns], target.at[0, :, columns], near.beside),
        remote.copy(sums.at[0, theirs, columns], target.at[1, :, columns], near.across),
        remote.copy(sums.at[1, theirs, columns], target.at[2, :, columns], near.far),
    ]


def line_copies(remote, near, part, target, columns):
    size = part.shape[0] // near.count
    copies = []
    for i, device in enumerate(near.line):
        to = lax.rem(near.z_index + i + 1, near.count)
        rows = pl.ds(pl.multiple_of(to * size, size), size)
        copies.append(remote.copy(part.at[rows, columns], target.at[i, :, columns], device))
    return copies


def line_total(near, part, came, columns):
    size = came.shape[1]
    total = part[pl.ds(pl.multiple_of(near.z_index * size, size), size), columns].astype(F32)
    for i in range(near.count - 1):
        total = total + came[i, :, columns].astype(F32)
    return total


class FeedSum:
    def __init__(self, remote, near, scratch):
        self.near = near
        self.part, self.part_came, self.block, self.block_came = scratch
        size = self.part_came.shape[1]
        everything = slice(None)
        self.first = line_copies(remote, near, self.part, self.part_came, everything)
        self.second = [
            remote.copy(self.block.at[pl.ds(2 * size, size)], self.block_came.at[0], near.beside),
            remote.copy(self.block.at[pl.ds(size, size)], self.block_came.at[1], near.across),
            remote.copy(self.block.at[pl.ds(3 * size, size)], self.block_came.at[2], near.far),
        ]

    def start(self, first_terms, second_terms):
        for target, terms, copies in (
            (self.part, first_terms, self.first),
            (self.block, second_terms, self.second),
        ):
            total = terms[0].astype(F32)
            for term in terms[1:]:
                total = total + term.astype(F32)
            target[...] = total.astype(BF16)
            run_copies(copies)

    def finish(self):
        wait_copies(self.first + self.second)
        second = self.block[0 : self.block_came.shape[1], :].astype(F32)
        for i in range(3):
            second = second + self.block_came[i].astype(F32)
        return line_total(self.near, self.part, self.part_came, slice(None)), second


def first_columns(width):
    return 2 * width // 3


def feed_sum_scratch(width, line):
    first, size = first_columns(width), width // line
    return [
        pltpu.VMEM((width, first), BF16),
        pltpu.VMEM((line - 1, size, first), BF16),
        pltpu.VMEM((4 * size, width - first), BF16),
        pltpu.VMEM((3, size, width - first), BF16),
    ]


def feed_backward_kernel(grad_ref, middle_ref, norm_ref, *rest, columns, rider, line):
    pieces = 4
    rest = list(rest)
    actives = [rest.pop(0) for _ in range(pieces)]
    slopes = [rest.pop(0) for _ in range(pieces)]
    ups = [rest.pop(0) for _ in range(pieces)]
    downs = [rest.pop(0) for _ in range(pieces)]
    if rider:
        rider_ref = rest.pop(0)
        feed_terms = [rest.pop(0) for _ in range(5)]
    keep_ref, beside_ref, across_ref, far_ref, spread_ref = [rest.pop(0) for _ in range(5)]
    up_shift_grad_ref, middle_grad_ref, small_ref = [rest.pop(0) for _ in range(3)]
    if rider:
        feed_total_ref, mixer_part_ref = rest.pop(0), rest.pop(0)
    (
        normed_t,
        grad_t,
        normed_grad,
        up_weight,
        down_weight,
        active,
        slope,
        low_grad,
        sent,
        came,
        sems,
        sends,
        receives,
    ) = rest[:13]
    step = pl.program_id(0)
    rows_all, width = grad_ref.shape
    size = up_weight.shape[2]
    blocks = blocks_of(grad_ref)
    near = Neighbours(line)
    remote = Remote(sends, receives)
    core_copies = [remote.copy(sent.at[slot], came.at[slot], near.twin) for slot in range(2)]
    devices = [near.twin]
    everything = slice(None)
    if rider:
        rider_own, rider_came, rider_sems = rest[13:16]
        feed_sum = FeedSum(remote, near, rest[16:])
        devices += [near.beside, near.across, near.far] + near.line
        half = rider_own.shape[0]
        plane = plane_copies(remote, near, rider_ref, rider_came, everything)
        rider_keep = pltpu.make_async_copy(
            rider_ref.at[0, pl.ds(pl.multiple_of(near.section * half, half), half)],
            rider_own,
            rider_sems.at[len(feed_terms)],
        )
        cut = first_columns(width)
        spots = [sent.at[i // 2, i % 2, :, 0:cut] for i in range(4)]
        spots.append(active.at[1, 0 : feed_terms[4].shape[0], 0 : width - cut])
        term_copies = [
            pltpu.make_async_copy(term, spot, rider_sems.at[i])
            for i, (term, spot) in enumerate(zip(feed_terms, spots))
        ]
    copies = []
    for slot, i in enumerate(ORDER):
        own = pl.ds(columns[i] * size, size)
        at = slot % 2
        copies.append(
            [
                pltpu.make_async_copy(downs[i], down_weight.at[at], sems.at[0, at]),
                pltpu.make_async_copy(slopes[i].at[:, own], slope.at[at], sems.at[1, at]),
                pltpu.make_async_copy(ups[i], up_weight.at[at], sems.at[2, at]),
                pltpu.make_async_copy(actives[i].at[:, own], active.at[at], sems.at[3, at]),
            ]
        )

    @pl.when(step == 0)
    def _():
        run_copies(copies[0])
        if rider:
            run_copies(term_copies + [rider_keep])
        greet(devices)
        if rider:
            run_copies(plane)
            wait_copies(term_copies)
            terms = [spot[...] for spot in spots]
            feed_sum.start(terms[:4], terms[4:])

        def prepare(i, carry):
            rows = block_at(i)
            scaled, _ = normalise(middle_ref[rows, :])
            normed = (scaled * norm_ref[0:1, :] + norm_ref[1:2, :]).astype(BF16)
            normed_t[:, rows] = normed.T
            grad_t[:, rows] = grad_ref[rows, :].T
            return carry

        lax.fori_loop(0, blocks, prepare, 0)

    for index in range(pieces):

        @pl.when(step == index)
        def _():
            at = index % 2
            wait_copies(copies[index])
            if index + 1 < pieces:
                run_copies(copies[index + 1])
            shift_grad = jnp.zeros((1, size), F32)
            for rows in big_blocks(rows_all):
                hidden_grad = nt(grad_ref[rows, :], down_weight[at]) * slope[at, rows, :].astype(F32)
                low = hidden_grad.astype(BF16)
                low_grad[rows, :] = low
                shift_grad = shift_grad + jnp.sum(hidden_grad, axis=0, keepdims=True)
                term = nt(low, up_weight[at])
                normed_grad[rows, :] = term if index == 0 else normed_grad[rows, :] + term
            up_shift_grad_ref[near.slot_of(ORDER[index])] = shift_grad

            def grad_of(put):
                for rows in big_blocks(width):
                    put((0, rows, slice(None)), nn(normed_t[rows, :], low_grad[...]))
                    put((1, rows, slice(None)), nn(grad_t[rows, :], active[at]))

            def put(slot, where, value):
                inner, outer = ((keep_ref, across_ref), (beside_ref, far_ref))[slot]
                which, rows, _ = where
                cut = first_columns(width)
                value_low, value_high = value[:, :cut], value[:, cut:]

                @pl.when(near.section == which)
                def _():
                    inner[rows, :] = value_low

                @pl.when(near.section != which)
                def _():
                    outer[rows, :] = value_low

                part = width // line
                other_half = which + near.section * (1 - 2 * which)
                for first in range(rows.start, rows.stop, part):
                    at_row = pl.multiple_of((2 * slot + other_half) * part, part)
                    spread_ref[first // part, pl.ds(at_row, part), :] = value_high[first - rows.start : first - rows.start + part]

            sum_with_core(index, core_copies, grad_of, sent, came, put)

    @pl.when(step == pieces - 1)
    def _():
        def finish(i, sums):
            rows = block_at(i)
            scaled, inverse = normalise(middle_ref[rows, :])
            gradient = normed_grad[rows, :]
            upper = grad_ref[rows, :].astype(F32)
            middle_grad = upper + normalise_back(gradient, scaled, inverse, norm_ref[0:1, :])
            middle_grad_ref[rows, :] = middle_grad
            terms = (gradient * scaled, gradient, middle_grad, upper)
            return tuple(old + jnp.sum(term, axis=0, keepdims=True) for old, term in zip(sums, terms))

        zero = jnp.zeros((1, width), F32)
        sums = lax.fori_loop(0, blocks, finish, (zero, zero, zero, zero))
        for index, row in enumerate(sums):
            small_ref[index : index + 1, :] = row
        if rider:
            cut = first_columns(width)
            first_total, second_total = feed_sum.finish()
            feed_total_ref[:, :cut] = first_total.astype(BF16)
            feed_total_ref[:, cut:] = second_total.astype(BF16)
            rider_keep.wait()
            wait_copies(plane)
            total = rider_own[...].astype(F32)
            for i in range(3):
                total = total + rider_came[i].astype(F32)
            mixer_part_ref[...] = total.astype(BF16)


def feed_backward(grad, middle, norm, actives, slopes, columns, ups, downs, collective, rider=None):
    rows, width = middle.shape
    pieces = len(ups)
    size = ups[0].shape[1]
    operands = [*actives, *slopes, *ups, *downs] + list(rider or [])
    line = lax.axis_size("dp") // 2
    cut = first_columns(size)
    outs = [jax.ShapeDtypeStruct((width, cut), BF16)] * 4 + [
        jax.ShapeDtypeStruct((line, 4 * width // line, size - cut), BF16),
        jax.ShapeDtypeStruct((pieces, 1, size), F32),
        jax.ShapeDtypeStruct((rows, width), F32),
        jax.ShapeDtypeStruct((4, width), F32),
    ]
    scratch = [
        pltpu.VMEM((width, rows), BF16),
        pltpu.VMEM((width, rows), BF16),
        pltpu.VMEM((rows, width), F32),
        pltpu.VMEM((2, width, size), BF16),
        pltpu.VMEM((2, size, width), BF16),
        pltpu.VMEM((2, rows, size), BF16),
        pltpu.VMEM((2, rows, size), BF16),
        pltpu.VMEM((rows, size), BF16),
        pltpu.VMEM((2, 2, width, size), BF16),
        pltpu.VMEM((2, 2, width, size), BF16),
        pltpu.SemaphoreType.DMA((4, 2)),
        pltpu.SemaphoreType.DMA((32,)),
        pltpu.SemaphoreType.DMA((32,)),
    ]
    if rider is not None:
        half = width // 2
        outs += [
            jax.ShapeDtypeStruct((width // line, width), BF16),
            jax.ShapeDtypeStruct((half, width), BF16),
        ]
        scratch += [
            pltpu.VMEM((half, width), BF16),
            pltpu.VMEM((3, half, width), BF16),
            pltpu.SemaphoreType.DMA((6,)),
        ]
        scratch += feed_sum_scratch(width, line)
    return pl.pallas_call(
        functools.partial(
            feed_backward_kernel, columns=columns, rider=rider is not None, line=line
        ),
        grid=(pieces,),
        in_specs=[once((rows, width)), once((rows, width)), once((2, width))] + anywhere(len(operands)),
        out_specs=[once(out.shape) for out in outs],
        scratch_shapes=scratch,
        out_shape=outs,
        name="feed_backward",
        **settings(16_000_000_000, collective),
    )(grad, middle, norm, *operands)


def mixer_backward_kernel(
    place_ref, start_ref, tiles_ref, seg_ref, middle_grad_ref, qkv_ref_all, *rest, saved, heads
):
    pieces = len(saved)
    rest = [qkv_ref_all] + list(rest)
    qkvs = [rest.pop(0) for _ in range(pieces)]
    mixeds = [rest.pop(0) for _ in range(pieces)]
    log_totals = [rest.pop(0) for _ in range(pieces)]
    weights = [rest.pop(0) for _ in range(pieces)]
    projected_ref, qkv_shift_grad_ref = rest[:2]
    qkv, mixed, totals, out_weight, low_middle, mixed_grad, sums, sems = rest[2:]
    step = pl.program_id(0)
    cols = heads * HEAD_DIM
    copies = []
    for i in range(pieces):
        at = saved[i]
        copies.append(
            [
                pltpu.make_async_copy(weights[i].at[3 * cols : 4 * cols], out_weight.at[i], sems.at[0, i]),
                pltpu.make_async_copy(qkvs[i].at[at], qkv.at[i], sems.at[1, i]),
                pltpu.make_async_copy(mixeds[i].at[at], mixed.at[i], sems.at[2, i]),
                pltpu.make_async_copy(
                    log_totals[i].at[at * heads : (at + 1) * heads], totals.at[i], sems.at[3, i]
                ),
            ]
        )

    @pl.when(step == 0)
    def _():
        for group in copies:
            run_copies(group)
        low_middle[...] = middle_grad_ref[...].astype(BF16)

    for index in range(pieces):

        @pl.when(step == index)
        def _():
            wait_copies(copies[index])

    mixed_grad[...] = nt(out_weight[step], low_middle[...]).astype(BF16)
    sums[...] = jnp.zeros_like(sums)
    each_image(
        start_ref,
        tiles_ref,
        lambda index, at, span: attend_backward_image(
            index, at, span, heads, seg_ref, qkv.at[step], mixed.at[step], totals.at[step], mixed_grad, sums
        ),
    )
    gradient = sums[...]
    projected_ref[0] = gradient.astype(BF16)
    qkv_shift_grad_ref[0] = jnp.sum(gradient, axis=1, keepdims=True).T


def mixer_backward(images, middle_grad, qkvs, mixeds, log_totals, saved, weights):
    rows, width = middle_grad.shape
    count = len(weights)
    cols = width // 4
    heads = cols // HEAD_DIM
    place, start, tiles, segment = images
    operands = [*qkvs, *mixeds, *log_totals, *weights]
    return pl.pallas_call(
        functools.partial(mixer_backward_kernel, saved=saved, heads=heads),
        grid_spec=pltpu.PrefetchScalarGridSpec(
            num_scalar_prefetch=3,
            grid=(count,),
            in_specs=[once((1, rows)), once((rows, width))] + anywhere(len(operands)),
            out_specs=[
                pl.BlockSpec((1, 3 * cols, rows), lambda i, *_: (i, 0, 0)),
                pl.BlockSpec((1, 1, 3 * cols), lambda i, place, *_: (slot_of(place, i), 0, 0)),
            ],
            scratch_shapes=[
                pltpu.VMEM((count, 3 * cols, rows), BF16),
                pltpu.VMEM((count, cols, rows), BF16),
                pltpu.VMEM((count, heads, 1, rows), F32),
                pltpu.VMEM((count, cols, width), BF16),
                pltpu.VMEM((rows, width), BF16),
                pltpu.VMEM((cols, rows), BF16),
                pltpu.VMEM((3 * cols, rows), F32),
                pltpu.SemaphoreType.DMA((4, count)),
            ],
        ),
        out_shape=[
            jax.ShapeDtypeStruct((count, 3 * cols, rows), BF16),
            jax.ShapeDtypeStruct((count, 1, 3 * cols), F32),
        ],
        name="mixer_backward",
        **settings(16_000_000_000),
    )(place, start, tiles, segment, middle_grad, *operands)


class Line:
    def __init__(self, remote, near, ref, size, columns):
        self.near = near
        self.copies = []
        for hop in range(near.count - 1):
            pair = []
            for sign in (1, -1):
                origin = lax.rem(near.z_index - sign * hop + near.count, near.count)
                chunk = ref.at[near.core, :, pl.ds(pl.multiple_of(origin * size, size), size), columns]
                pair.append((sign, remote.copy(chunk, chunk, near.along(sign))))
            self.copies.append(pair)

    def each(self, hop, ahead, act):
        for sign, copy in self.copies[hop]:
            origin = self.near.z_index - sign * (hop + 1 - ahead)
            target = self.near.z_index + sign * ahead

            @pl.when((origin >= 0) & (origin < self.near.count) & (target >= 0) & (target < self.near.count))
            def _():
                act(copy)

    def start(self, hop):
        self.each(hop, 1, lambda copy: copy.start())

    def receive(self, hop):
        self.each(hop, 0, lambda copy: copy.wait_recv())

    def finish(self):
        for hop in range(self.near.count - 1):
            self.each(hop, 1, lambda copy: copy.wait_send())


def input_backward_kernel(hidden_ref, middle_grad_ref, norm_ref, projected, normed_in, *rest, saved, line, last):
    pieces = len(saved)
    rest = list(rest)
    mixeds = [rest.pop(0) for _ in range(pieces)]
    weights = [rest.pop(0) for _ in range(pieces)]
    if last:
        feed_terms = [rest.pop(0) for _ in range(5)]
        mixer_part1, feed_total1, other_grad = [rest.pop(0) for _ in range(3)]
        small_refs = [rest.pop(0) for _ in range(7)]
        feed_result, mixer_result, parts_result, vector_out = [rest.pop(0) for _ in range(4)]
    else:
        sums_ref, in_grad_ref, small_ref = [rest.pop(0) for _ in range(3)]
    projected_grad, mixed, normed, low_middle, weight, sent, came = [rest.pop(0) for _ in range(7)]
    sems, sends, receives = [rest.pop(0) for _ in range(3)]
    rows_all, width = hidden_ref.shape
    count = projected.shape[1]
    near = Neighbours(line)
    remote = Remote(sends, receives)
    everything = slice(None)
    devices = [near.twin]
    if last:
        devices += [near.beside, near.across, near.far] + near.line
        sums_ref, in_grad_ref = [rest.pop(0) for _ in range(2)]
        feed_sum = FeedSum(remote, near, [rest.pop(0) for _ in range(4)])
        part1_came = rest.pop(0)
    copies = []
    for i in range(pieces):
        copies.append(
            [
                pltpu.make_async_copy(
                    projected.at[i], projected_grad.at[i * count : (i + 1) * count], sems.at[0, i]
                ),
                pltpu.make_async_copy(mixeds[i].at[saved[i]], mixed.at[i], sems.at[1, i]),
                pltpu.make_async_copy(
                    weights[i].at[0:count], weight.at[i * count : (i + 1) * count], sems.at[2, i]
                ),
            ]
        )
    norm_copy = pltpu.make_async_copy(normed_in, normed, sems.at[3, 0])
    norm_copy.start()
    for i in ORDER:
        run_copies(copies[i])
    greet(devices)

    if last:
        terms = [term[...] for term in feed_terms]
        feed_sum.start(terms[:4], terms[4:])
        part1_line = line_copies(remote, near, mixer_part1, part1_came, everything)
        run_copies(part1_line)

    core_copies = [remote.copy(sent.at[slot], came.at[slot], near.twin) for slot in range(2)]
    low_middle[...] = middle_grad_ref[...].astype(BF16)
    norm_copy.wait()
    for index, piece in enumerate(ORDER):
        wait_copies(copies[piece])

        def grad_of(put, piece=piece):
            own = slice(piece * count, (piece + 1) * count)
            put((slice(0, count), everything), nn(projected_grad[own, :], normed[...]))
            put((slice(count, width), everything), nn(mixed[piece], low_middle[...]))

        def put(slot, where, value):
            sums_ref[(slot,) + where] = value

        sum_with_core(index, core_copies, grad_of, sent, came, put)

    if last:
        (
            mixer_came,
            mixer_part,
            line_came,
            feed_own,
            feed_other,
            mixer_own,
            mixer_other,
            feed_out,
            mixer_out,
            parts_out,
            vector,
            vector_came,
            locals_,
        ) = rest
        chunk_width = width // 2
        chunks = [slice(i * chunk_width, (i + 1) * chunk_width) for i in range(2)]
        plane = [plane_copies(remote, near, sums_ref, mixer_came, chunk) for chunk in chunks]

    def local(source, target, slot):
        return pltpu.make_async_copy(source, target, locals_.at[slot])

    def place_total(total0, total1, own_ref, other_ref, out_ref, chunk, slot):
        own_ref[:, chunk] = jnp.where(near.section == 0, total0, total1).astype(BF16)
        other_ref[:, chunk] = jnp.where(near.section == 0, total1, total0).astype(BF16)
        size = own_ref.shape[0]
        rows = pl.ds(pl.multiple_of(near.z_index * size, size), size)
        spot = out_ref.at[near.core, near.section, rows, chunk]
        keep = local(own_ref.at[:, chunk], spot, slot)
        keep.start()
        send = remote.copy(other_ref.at[:, chunk], spot, near.across)
        send.start()
        return [keep, send]

    if last:
        first = near.section == 0
        feed_pairs = []
        run_copies(plane[0])

    gain = jnp.zeros((1, width), F32)
    shift = jnp.zeros((1, width), F32)
    for index, rows in enumerate(big_blocks(rows_all)):
        scaled, inverse = normalise(hidden_ref[rows, :].astype(F32))
        gradient = tn(projected_grad[:, rows], weight[...])
        in_grad = middle_grad_ref[rows, :] + normalise_back(gradient, scaled, inverse, norm_ref[0:1, :])
        in_grad_ref[rows, :] = in_grad.astype(BF16)
        gain = gain + jnp.sum(gradient * scaled, axis=0, keepdims=True)
        shift = shift + jnp.sum(gradient, axis=0, keepdims=True)
        if last and index == 0:
            cut = first_columns(width)
            for chunk, total in zip((slice(0, cut), slice(cut, width)), feed_sum.finish()):
                feed_pairs.append(
                    place_total(
                        total, feed_total1[:, chunk].astype(F32), feed_own, feed_other, feed_out, chunk, len(feed_pairs)
                    )
                )
            run_copies(plane[1])

    if not last:
        small_ref[0:1, :] = gain
        small_ref[1:2, :] = shift
        return

    feed_size, mixer_size = feed_own.shape[0], mixer_own.shape[0]
    feed_chain = Line(remote, near, feed_out, feed_size, everything)
    mixer_chains = [Line(remote, near, mixer_out, mixer_size, chunk) for chunk in chunks]
    for pair in feed_pairs:
        wait_copies(pair)
    feed_chain.start(0)

    small0, ups0, shifts0, small1, ups1, shifts1, in_small1 = small_refs
    vector[...] = jnp.zeros_like(vector)
    ins = ((gain, shift), (in_small1[0:1, :], in_small1[1:2, :]))
    for layer, (small, ups, shifts) in enumerate(((small0, ups0, shifts0), (small1, ups1, shifts1))):
        rows = [ins[layer][0], small[0:1, :], ins[layer][1], small[1:2, :], small[2:3, :], small[3:4, :]]
        for i, row in enumerate(rows):
            vector[layer, i : i + 1, :] = row
        for i in range(pieces):
            vector[layer, 8 + i : 9 + i, :] = ups[i]
            vector[layer, 12 + i : 13 + i, 0:count] = shifts[i]

    def vector_round(devices, at):
        group = [remote.copy(vector, vector_came.at[at + i], device) for i, device in enumerate(devices)]
        run_copies(group)
        return group

    def vector_sum(group, at):
        wait_copies(group)
        total = vector[...]
        for i in range(len(group)):
            total = total + vector_came[at + i]
        vector[...] = total

    pending = vector_round([near.twin], 0)
    half = mixer_part.shape[0]
    mine = pl.ds(pl.multiple_of(near.section * half, half), half)
    spreads = []
    for group, chunk in zip(plane, chunks):
        wait_copies(group)
        part = sums_ref[0, mine, chunk].astype(F32)
        for i in range(3):
            part = part + mixer_came[i, :, chunk].astype(F32)
        mixer_part[:, chunk] = part.astype(BF16)
        spreads.append(line_copies(remote, near, mixer_part, line_came, chunk))
        run_copies(spreads[-1])
    vector_sum(pending, 0)
    pending = vector_round([near.beside, near.across, near.far], 1)
    rows = rows_all // 2
    inner = pl.ds(pl.multiple_of(near.lane * rows, rows), rows)
    outer = pl.ds(pl.multiple_of((1 - near.lane) * rows, rows), rows)
    spot = parts_out.at[2 * near.section + near.lane]
    at = remote.reserve(4)
    quarter = rows // 2
    inner_low = pl.ds(pl.multiple_of(near.lane * rows, quarter), quarter)
    inner_high = pl.ds(pl.multiple_of(near.lane * rows + quarter, quarter), quarter)

    def grad_copies(own, other):
        return [
            remote.copy(own.at[outer], spot, near.beside, at),
            remote.copy(other.at[inner_low], spot.at[0:quarter], near.across, at + 1),
            remote.copy(other.at[inner_high], spot.at[quarter:rows], near.across, at + 2),
            remote.copy(other.at[outer], spot, near.far, at + 3),
        ]

    def start_grads(which):
        @pl.when(first)
        def _():
            copies = grad_copies(in_grad_ref, other_grad)
            run_copies([copies[i] for i in which])

        @pl.when(near.section == 1)
        def _():
            copies = grad_copies(other_grad, in_grad_ref)
            run_copies([copies[i] for i in which])

    @pl.when(first)
    def _():
        local(in_grad_ref.at[inner], spot, 4).start()

    @pl.when(near.section == 1)
    def _():
        local(other_grad.at[inner], spot, 4).start()

    start_grads((0, 1))
    pairs = []
    for i, chunk in enumerate(chunks):
        wait_copies(spreads[i])
        total0 = line_total(near, mixer_part, line_came, chunk)
        if not pairs:
            wait_copies(part1_line)
        total1 = line_total(near, mixer_part1, part1_came, chunk)
        pairs.append(place_total(total0, total1, mixer_own, mixer_other, mixer_out, chunk, 2 + i))
    start_grads((2, 3))
    feed_chain.receive(0)
    feed_chain.start(1)
    vector_sum(pending, 1)
    pending = vector_round(near.line, 4)
    for pair, chain in zip(pairs, mixer_chains):
        wait_copies(pair)
        chain.start(0)
    for hop in range(1, line - 1):
        feed_chain.receive(hop)
        if hop + 1 < line - 1:
            feed_chain.start(hop + 1)
        for chain in mixer_chains:
            chain.receive(hop - 1)
            chain.start(hop)
    feed_twin = remote.copy(feed_out.at[near.core], feed_out.at[near.core], near.twin)
    feed_twin.start()
    vector_sum(pending, 4)
    vector_out[...] = jnp.where(first, vector[0], vector[1])
    for chain in mixer_chains:
        chain.receive(line - 2)
    mixer_twin = remote.copy(mixer_out.at[near.core], mixer_out.at[near.core], near.twin)
    mixer_twin.start()
    feed_twin.wait()
    feed_chain.finish()
    results = [local(feed_out, feed_result, 5), local(parts_out, parts_result, 6), local(mixer_out, mixer_result, 7)]
    results[0].start()
    for copy in grad_copies(in_grad_ref, other_grad):
        copy.wait()
    local(in_grad_ref.at[inner], spot, 4).wait()
    results[1].start()
    mixer_twin.wait()
    for chain in mixer_chains:
        chain.finish()
    results[2].start()
    wait_copies(results)


def input_backward(
    hidden, middle_grad, norm, projected, normed, mixeds, saved, weights, collective, finish=None
):
    rows, width = hidden.shape
    number, count, _ = projected.shape
    line = lax.axis_size("dp") // 2
    vmem = pl.BlockSpec(memory_space=pltpu.VMEM)
    far = pl.BlockSpec(memory_space=pl.ANY)
    operands = [hidden, middle_grad, norm, projected, normed, *mixeds, *weights]
    specs = [vmem] * 3 + [far] * (2 + 2 * number)
    feed_rows, half = width // line, width // 2
    mixer_rows = half // line
    scratch = [
        pltpu.VMEM((number * count, rows), BF16),
        pltpu.VMEM((number, width - count, rows), BF16),
        pltpu.VMEM((rows, width), BF16),
        pltpu.VMEM((rows, width), BF16),
        pltpu.VMEM((number * count, width), BF16),
        pltpu.VMEM((2, width, width), BF16),
        pltpu.VMEM((2, width, width), BF16),
        pltpu.SemaphoreType.DMA((4, number)),
        pltpu.SemaphoreType.DMA((64,)),
        pltpu.SemaphoreType.DMA((64,)),
    ]
    if finish is None:
        outs = [
            jax.ShapeDtypeStruct((2, width, width), BF16),
            jax.ShapeDtypeStruct((rows, width), BF16),
            jax.ShapeDtypeStruct((2, width), F32),
        ]
        out_specs = [vmem] * 3
    else:
        operands += list(finish)
        specs += [vmem] * 7 + [far] + [vmem] * (len(finish) - 8)
        outs = [
            jax.ShapeDtypeStruct((2, 2, width, width), BF16),
            jax.ShapeDtypeStruct((2, 2, half, width), BF16),
            jax.ShapeDtypeStruct((4, rows // 2, width), BF16),
            jax.ShapeDtypeStruct((16, width), F32),
        ]
        out_specs = [far] * 3 + [vmem]
        scratch += [
            pltpu.VMEM((2, width, width), BF16),
            pltpu.VMEM((rows, width), BF16),
            *feed_sum_scratch(width, line),
            pltpu.VMEM((line - 1, mixer_rows, width), BF16),
            pltpu.VMEM((3, half, width), BF16),
            pltpu.VMEM((half, width), BF16),
            pltpu.VMEM((line - 1, mixer_rows, width), BF16),
            pltpu.VMEM((feed_rows, width), BF16),
            pltpu.VMEM((feed_rows, width), BF16),
            pltpu.VMEM((mixer_rows, width), BF16),
            pltpu.VMEM((mixer_rows, width), BF16),
            pltpu.VMEM((2, 2, width, width), BF16),
            pltpu.VMEM((2, 2, half, width), BF16),
            pltpu.VMEM((4, rows // 2, width), BF16),
            pltpu.VMEM((2, 16, width), F32),
            pltpu.VMEM((3 + line, 2, 16, width), F32),
            pltpu.SemaphoreType.DMA((8,)),
        ]
    return pl.pallas_call(
        functools.partial(input_backward_kernel, saved=saved, line=line, last=finish is not None),
        in_specs=specs,
        out_specs=out_specs,
        scratch_shapes=scratch,
        out_shape=outs,
        name="input_backward",
        **settings(8_000_000_000, collective),
    )(*operands)


def place_states_kernel(place_ref, *rest):
    parts, out_ref, held, sems = rest[:4], rest[4], rest[5], rest[6]
    inward = [pltpu.make_async_copy(part, held.at[i], sems.at[0, i]) for i, part in enumerate(parts)]
    outward = [
        pltpu.make_async_copy(held.at[i], out_ref.at[place_ref[2] ^ i], sems.at[1, i]) for i in range(len(parts))
    ]
    run_copies(inward)
    for first, second in zip(inward, outward):
        first.wait()
        second.start()
    wait_copies(outward)


def place_states(place, parts):
    far = pl.BlockSpec(memory_space=pl.ANY)
    return pl.pallas_call(
        place_states_kernel,
        grid_spec=pltpu.PrefetchScalarGridSpec(
            num_scalar_prefetch=1,
            grid=(1,),
            in_specs=[far] * 4,
            out_specs=far,
            scratch_shapes=[
                pltpu.VMEM((4,) + parts[0].shape, BF16),
                pltpu.SemaphoreType.DMA((2, 4)),
            ],
        ),
        out_shape=jax.ShapeDtypeStruct((4,) + parts[0].shape, BF16),
        name="place_states",
        **settings(1_000_000),
    )(place, *parts)


def unpack_kernel(parts_ref, ups_ref, downs_ref, mixer_ref, grads_ref, qkv_ref, out_ref, up_ref, down_ref):
    step = pl.program_id(0)
    width = ups_ref.shape[3]
    part = width // 4
    grads_ref[...] = parts_ref[...].astype(F32)
    for core in range(2):
        up_ref[:, core * width : (core + 1) * width] = ups_ref[core, 0].astype(F32)
    down_ref[...] = downs_ref[0, 0].astype(F32).T

    @pl.when(step < 3)
    def _():
        both = jnp.concatenate([mixer_ref[0], mixer_ref[1]], axis=0)
        qkv_ref[0] = both.astype(F32).T

    @pl.when(step == 3)
    def _():
        for core in range(2):
            out_ref[core * part : (core + 1) * part, :] = mixer_ref[core].astype(F32)


def unpack(parts, feed, mixer):
    number, rows, width = parts.shape
    half, part = width // 2, width // 4
    return pl.pallas_call(
        unpack_kernel,
        grid=(4,),
        in_specs=[
            pl.BlockSpec((1, rows, width), lambda i: (i, 0, 0)),
            pl.BlockSpec((2, 1, part, width), lambda i: (0, 0, i, 0)),
            pl.BlockSpec((1, 1, width, half), lambda i: (i // 2, 1, 0, i % 2)),
            pl.BlockSpec((2, part, width), lambda i: (0, i, 0)),
        ],
        out_specs=[
            pl.BlockSpec((1, rows, width), lambda i: (i, 0, 0)),
            pl.BlockSpec((1, width, half), lambda i: (lax.min(i, 2), 0, 0)),
            pl.BlockSpec((half, width), lambda i: (0, 0)),
            pl.BlockSpec((part, 2 * width), lambda i: (i, 0)),
            pl.BlockSpec((half, width), lambda i: (i, 0)),
        ],
        out_shape=[
            jax.ShapeDtypeStruct(parts.shape, F32),
            jax.ShapeDtypeStruct((3, width, half), F32),
            jax.ShapeDtypeStruct((half, width), F32),
            jax.ShapeDtypeStruct((width, 2 * width), F32),
            jax.ShapeDtypeStruct((2 * width, width), F32),
        ],
        name="unpack",
        **settings(1_000_000),
    )(parts, feed, feed, mixer)


def route(change):
    shape = [lax.axis_size(axis) for axis in AXES]
    pairs = []
    for s in range(shape[0]):
        for d in range(shape[1]):
            for t in range(shape[2]):
                to = change(s, d, t)
                if to is not None:
                    pairs.append(((s * shape[1] + d) * shape[2] + t, (to[0] * shape[1] + to[1]) * shape[2] + to[2]))
    return pairs


def moved(block, change):
    return lax.ppermute(block, AXES, route(change))


def over_tensor(s, d, t):
    return (s, d, 1 - t)


def over_section(s, d, t):
    return (1 - s, d, t)


def over_both(s, d, t):
    return (1 - s, d, 1 - t)


def over_core(s, d, t):
    return (s, d ^ 1, t)


def along_z(distance):
    count = lax.axis_size("dp") // 2
    return lambda s, d, t: (s, (d // 2 + distance) % count * 2 + d % 2, t)


def tie(*values):
    return lax.optimization_barrier(values)


def take_part(block, which, count, axis=0):
    size = block.shape[axis] // count
    return lax.dynamic_slice_in_dim(block, which * size, size, axis)


def added(*terms):
    total = terms[0].astype(F32)
    for term in terms[1:]:
        total = total + term.astype(F32)
    return total.astype(terms[0].dtype)


def reordered(pieces, lane, core):
    pieces = jnp.where(lane == 0, pieces, pieces[jnp.array([2, 3, 0, 1])])
    return jnp.where(core == 0, pieces, pieces[jnp.array([1, 0, 3, 2])])


def one_sequence_each(
    inputs,
    cotangent,
    segment_ids,
    norm_gains,
    norm_biases,
    qkv_weight,
    qv_bias,
    out_weight,
    up_weight,
    up_bias,
    down_weight,
    out_biases,
):
    section = lax.axis_index("section")
    group = lax.axis_index("dp")
    lane = lax.axis_index("tensor")
    core = group % 2
    z_index = group // 2
    z_count = lax.axis_size("dp") // 2
    width = inputs.shape[2]
    hidden = up_bias.shape[1]
    cols = qkv_weight.shape[3]
    part = cols // 2
    mine = 2 * section + lane

    def own_half(array, axis):
        return take_part(array, core, 2, axis)

    mixer_own = jnp.concatenate(
        [
            own_half(qkv_weight[0], 2).transpose(0, 2, 1).reshape(3 * part, width),
            own_half(out_weight[0], 0),
        ],
        axis=0,
    )
    up_own = own_half(up_weight[0], 1)
    down_own = own_half(down_weight[0], 0)
    small = jnp.concatenate(
        [item.reshape(-1) for item in (norm_gains, norm_biases, qv_bias, up_bias, out_biases)]
    )

    def sequence_halves(array):
        kept = lax.dynamic_index_in_dim(array, mine, 0, keepdims=False)
        sent = lax.dynamic_index_in_dim(array, 2 * section + 1 - lane, 0, keepdims=False)
        return kept, sent

    def joined(kept, came):
        return jnp.where(lane == 0, jnp.concatenate([kept, came], 0), jnp.concatenate([came, kept], 0))

    segment = lax.dynamic_index_in_dim(segment_ids, mine, 0, keepdims=True)
    ids = jnp.arange(IMAGE_IDS, dtype=jnp.int32)[:, None]
    begin = jnp.sum((segment < ids).astype(jnp.int32), axis=1)
    end = jnp.sum((segment <= ids).astype(jnp.int32), axis=1)
    start = begin // TILE
    place = jnp.stack([lane, core, mine]).astype(jnp.int32)
    images = (place, start, (end - 1) // TILE - start + 1, segment)

    def params(vector):
        gains = vector[: 2 * width].reshape(2, width)
        shifts = vector[2 * width : 4 * width].reshape(2, width)
        qv = vector[4 * width : 6 * width].reshape(2, 4, part)
        up_shift = vector[6 * width : 6 * width + hidden].reshape(4, 1, hidden // 4)
        outs = vector[6 * width + hidden :].reshape(2, 1, width)
        zero = jnp.zeros((4, part), F32)
        qkv_shift = jnp.concatenate([qv[0], zero, qv[1]], axis=1)
        norms = [jnp.stack([gains[i], shifts[i]]) for i in range(2)]
        return norms, qkv_shift[:, :, None], up_shift, outs

    def by_layer(own, came):
        return jnp.where(section == 0, own, came), jnp.where(section == 1, own, came)

    kept, sent = sequence_halves(inputs)
    grad_kept, grad_sent = sequence_halves(cotangent)
    came, mixer_came, small_came, up_own, down_own, grad_kept, grad_sent = tie(
        moved(sent, over_tensor),
        moved(mixer_own, over_section),
        moved(small, over_section),
        up_own,
        down_own,
        grad_kept,
        grad_sent,
    )
    up_came = moved(up_own, over_section)
    state = joined(kept, came)
    mixers = by_layer(mixer_own, mixer_came)
    layer_params = [params(vector) for vector in by_layer(small, small_came)]
    mixer_pieces = [[mixers[0], moved(mixers[0], over_core)], None]
    norms, qkv_shift, up_shift, outs = layer_params[0]
    mixer_a, beside, up_came = tie(
        mixer_forward(images, state, norms[0], qkv_shift, mixer_pieces[0]),
        moved(mixers[0], over_tensor),
        up_came,
    )
    ups = by_layer(up_own, up_came)
    mixer_pieces[0] = mixer_pieces[0] + [beside, moved(beside, over_core)]
    mixer_b, up_beside, up_twin, down_came = tie(
        mixer_forward(
            images,
            state,
            norms[0],
            qkv_shift,
            mixer_pieces[0][2:],
            2,
            (mixer_a[3], mixer_a[1]),
            mixer_pieces[0],
            outs[0],
        ),
        moved(ups[0], over_tensor),
        moved(ups[0], over_core),
        moved(down_own, over_section),
    )
    downs = by_layer(down_own, down_came)
    down_twin = moved(downs[0], over_core)
    feed_a, down_beside, up_corner = tie(
        feed_forward(
            place, mixer_b[3], norms[1], up_shift, outs[1], [ups[0], up_twin], [downs[0], down_twin], 0, False
        ),
        moved(downs[0], over_tensor),
        moved(up_beside, over_core),
    )
    up_pieces = [[ups[0], up_twin, up_beside, up_corner], None]
    down_pieces = [[downs[0], down_twin, down_beside, moved(down_beside, over_core)], None]
    feed_b, beside, twin = tie(
        feed_forward(
            place, mixer_b[3], norms[1], up_shift, feed_a[0], up_pieces[0][2:], down_pieces[0][2:], 2, True
        ),
        moved(mixers[1], over_tensor),
        moved(mixers[1], over_core),
    )
    first_out = feed_b[0]
    saved = [
        dict(
            state=state,
            normed=mixer_a[3],
            qkv=[mixer_a[0], mixer_a[0], mixer_b[0], mixer_b[0]],
            mixed=[mixer_a[1], mixer_a[1], mixer_b[1], mixer_b[1]],
            totals=[mixer_a[2], mixer_a[2], mixer_b[2], mixer_b[2]],
            at=[0, 1, 0, 1],
            middle=mixer_b[3],
            active=[feed_a[1], feed_a[1], feed_b[1], feed_b[1]],
            slope=[feed_a[2], feed_a[2], feed_b[2], feed_b[2]],
        )
    ]
    norms, qkv_shift, up_shift, outs = layer_params[1]
    mixer_pieces[1] = [mixers[1], twin, beside, moved(beside, over_core)]
    mixer_a, up_beside, up_twin, down_beside, down_twin = tie(
        mixer_forward(images, first_out, norms[0], qkv_shift, mixer_pieces[1], 0, None, mixer_pieces[1], outs[0]),
        moved(ups[1], over_tensor),
        moved(ups[1], over_core),
        moved(downs[1], over_tensor),
        moved(downs[1], over_core),
    )
    up_pieces[1] = [ups[1], up_twin, up_beside, moved(up_beside, over_core)]
    down_pieces[1] = [downs[1], down_twin, down_beside, moved(down_beside, over_core)]
    feed_a, grad_came = tie(
        feed_forward(place, mixer_a[4], norms[1], up_shift, outs[1], up_pieces[1], down_pieces[1], 0, True),
        moved(grad_sent, over_tensor),
    )
    second_out = feed_a[0]
    saved.append(
        dict(
            state=first_out,
            normed=mixer_a[3],
            qkv=[mixer_a[0]] * 4,
            mixed=[mixer_a[1]] * 4,
            totals=[mixer_a[2]] * 4,
            at=[0, 1, 2, 3],
            middle=mixer_a[4],
            active=[feed_a[1]] * 4,
            slope=[feed_a[2]] * 4,
        )
    )
    grad = joined(grad_kept, grad_came)

    def exchange(own, other):
        return [
            take_part(own, lane, 2),
            moved(take_part(own, 1 - lane, 2), over_tensor),
            moved(take_part(other, lane, 2), over_section),
            moved(take_part(other, 1 - lane, 2), over_both),
        ]

    out_parts = exchange(
        jnp.where(section == 0, first_out, second_out), jnp.where(section == 0, second_out, first_out)
    )

    def feed_back(layer, grad, rider=None):
        kept = saved[layer]
        return feed_backward(
            grad,
            kept["middle"],
            layer_params[layer][0][1],
            kept["active"],
            kept["slope"],
            kept["at"],
            up_pieces[layer],
            down_pieces[layer],
            layer,
            rider,
        )

    def mixer_back(layer, middle_grad):
        kept = saved[layer]
        return mixer_backward(
            images, middle_grad, kept["qkv"], kept["mixed"], kept["totals"], kept["at"], mixer_pieces[layer]
        )

    def input_back(layer, middle_grad, projected, finish=None):
        kept = saved[layer]
        return input_backward(
            kept["state"],
            middle_grad,
            layer_params[layer][0][0],
            projected,
            kept["normed"],
            kept["mixed"],
            kept["at"],
            mixer_pieces[layer],
            2 + layer,
            finish,
        )

    def send_feed(feed):
        kept, beside, across, far, spread = feed[:5]
        plane = [
            moved(block, change)
            for block, change in ((beside, over_tensor), (across, over_section), (far, over_both))
        ]
        groups = [list(range(which, 2 * z_count, 2)) for which in range(2)]
        return [kept] + plane + [lax.psum_scatter(spread, "dp", axis_index_groups=groups)]

    feed1, out_parts = tie(feed_back(1, grad), out_parts)
    came = send_feed(feed1)
    feed1, mixer1, came[:4] = tie(feed1, mixer_back(1, feed1[6]), came[:4])
    (mixer_sums1, in_grad1, in_small1), came = tie(input_back(1, feed1[6], mixer1[0]), came)
    feed0 = feed_back(0, in_grad1, [mixer_sums1, *came])
    mixer0, came = tie(mixer_back(0, feed0[6]), send_feed(feed0))
    feed_sum, mixer_sum, in_parts, vector = input_back(
        0,
        feed0[6],
        mixer0[0],
        [
            *came,
            feed0[9],
            feed0[8],
            in_grad1,
            feed0[7],
            feed0[5],
            mixer0[1],
            feed1[7],
            feed1[5],
            mixer1[1],
            in_small1,
        ],
    )
    grads, qkv_grad, out_grad, up_grad, down_grad = unpack(
        in_parts, feed_sum, mixer_sum.reshape(2, 4 * part, width)
    )
    states = place_states(place, out_parts)
    qv_grad = vector[12:16, : 3 * part].reshape(4, 3, part)
    return (
        states[None],
        grads[None],
        vector[0:2][None],
        vector[2:4][None],
        qkv_grad[None],
        jnp.stack([qv_grad[:, 0].reshape(width), qv_grad[:, 2].reshape(width)])[None],
        out_grad[None],
        up_grad[None],
        vector[8:12].reshape(1, hidden),
        down_grad[None],
        vector[4:6][None],
    )


def passed_along(block, axis, distance):
    devices = range(lax.axis_size(axis))
    route = [(i - distance, i) for i in devices if i - distance in devices]
    return lax.ppermute(block, axis, route)


def norm_parts(token_rows, gain_row, shift_row):
    centre = token_rows - jnp.mean(token_rows, axis=-1, keepdims=True)
    inverse = lax.rsqrt(jnp.mean(centre * centre, axis=-1, keepdims=True) + EPSILON)
    scaled = centre * inverse
    return (scaled * gain_row + shift_row, scaled, inverse)


def norm_back(gradient, scaled, inverse, gain_row):
    upstream = gradient * gain_row
    return inverse * (
        upstream
        - jnp.mean(upstream, axis=-1, keepdims=True)
        - scaled * jnp.mean(upstream * scaled, axis=-1, keepdims=True)
    )


def gelu_exact(values):
    return jax.nn.gelu(values, approximate=False)


def head_view(matrix, heads_local):
    return matrix.reshape(matrix.shape[0], heads_local, HEAD_DIM)


def join_heads(stacked):
    return stacked.transpose(1, 0, 2).reshape(stacked.shape[1], stacked.shape[0] * stacked.shape[2])


def attend_forward(queries, key_rows, value_rows, segment):
    seq_len = queries.shape[0]
    half_rows = seq_len // 2
    heads_local = queries.shape[1] // HEAD_DIM
    scaling = HEAD_DIM ** (-0.5)
    query_heads = head_view(queries, heads_local)
    key_heads = head_view(key_rows, heads_local)
    value_heads = head_view(value_rows, heads_local)

    def one_item(item):
        head_index = item // 2
        row_start = item % 2 * half_rows
        head_keys = lax.dynamic_index_in_dim(key_heads, head_index, 1, keepdims=False)
        head_values = lax.dynamic_index_in_dim(value_heads, head_index, 1, keepdims=False)
        head_queries = lax.dynamic_index_in_dim(query_heads, head_index, 1, keepdims=False)
        block_queries = lax.dynamic_slice_in_dim(head_queries, row_start, half_rows, 0)
        block_segment = lax.dynamic_slice_in_dim(segment, row_start, half_rows, 0)
        scores = (
            jnp.einsum("qd,kd->qk", block_queries, head_keys, preferred_element_type=jnp.float32)
            * scaling
        )
        scores = jnp.where(block_segment[:, None] == segment[None, :], scores, NEGATIVE)
        row_peak = jnp.max(scores, axis=-1, keepdims=True)
        expanded = jnp.exp(scores - row_peak)
        denominator = jnp.sum(expanded, axis=-1, keepdims=True)
        weights = (expanded / denominator).astype(jnp.bfloat16)
        block_out = jnp.dot(weights, head_values, preferred_element_type=jnp.float32).astype(
            jnp.bfloat16
        )
        return (block_out, row_peak[:, 0] + jnp.log(denominator[:, 0]))

    outputs, log_totals = lax.map(one_item, jnp.arange(2 * heads_local, dtype=jnp.int32))
    mixed_rows = join_heads(outputs.reshape(heads_local, seq_len, HEAD_DIM))
    return (mixed_rows, log_totals.reshape(heads_local, seq_len))


def attend_backward(queries, key_rows, value_rows, mixed_grad, log_totals, segment):
    seq_len = queries.shape[0]
    half_rows = seq_len // 2
    heads_local = queries.shape[1] // HEAD_DIM
    scaling = HEAD_DIM ** (-0.5)
    query_heads = head_view(queries, heads_local)
    key_heads = head_view(key_rows, heads_local)
    value_heads = head_view(value_rows, heads_local)
    grad_heads = head_view(mixed_grad, heads_local)

    def one_head(head_index):
        head_queries = lax.dynamic_index_in_dim(query_heads, head_index, 1, keepdims=False)
        head_keys = lax.dynamic_index_in_dim(key_heads, head_index, 1, keepdims=False)
        head_values = lax.dynamic_index_in_dim(value_heads, head_index, 1, keepdims=False)
        head_grads = lax.dynamic_index_in_dim(grad_heads, head_index, 1, keepdims=False)
        head_totals = lax.dynamic_index_in_dim(log_totals, head_index, 0, keepdims=False)

        def one_block(carry, block_index):
            key_grad, value_grad = carry
            row_start = block_index * half_rows
            block_queries = lax.dynamic_slice_in_dim(head_queries, row_start, half_rows, 0)
            block_grads = lax.dynamic_slice_in_dim(head_grads, row_start, half_rows, 0)
            block_totals = lax.dynamic_slice_in_dim(head_totals, row_start, half_rows, 0)
            block_segment = lax.dynamic_slice_in_dim(segment, row_start, half_rows, 0)
            scores = (
                jnp.einsum(
                    "qd,kd->qk", block_queries, head_keys, preferred_element_type=jnp.float32
                )
                * scaling
            )
            scores = jnp.where(block_segment[:, None] == segment[None, :], scores, NEGATIVE)
            weights = jnp.exp(scores - block_totals[:, None])
            low_weights = weights.astype(jnp.bfloat16)
            block_out = jnp.dot(
                low_weights, head_values, preferred_element_type=jnp.float32
            ).astype(jnp.bfloat16)
            weight_grads = jnp.einsum(
                "qd,kd->qk", block_grads, head_values, preferred_element_type=jnp.float32
            )
            row_terms = jnp.sum(weights * weight_grads, axis=-1, keepdims=True)
            score_grads = (weights * (weight_grads - row_terms)).astype(jnp.bfloat16)
            query_grad = (
                jnp.dot(score_grads, head_keys, preferred_element_type=jnp.float32) * scaling
            )
            key_grad = (
                key_grad
                + jnp.einsum(
                    "qk,qd->kd", score_grads, block_queries, preferred_element_type=jnp.float32
                )
                * scaling
            )
            value_grad = value_grad + jnp.einsum(
                "qk,qd->kd", low_weights, block_grads, preferred_element_type=jnp.float32
            )
            return ((key_grad, value_grad), (block_out, query_grad))

        empty = jnp.zeros((seq_len, HEAD_DIM), jnp.float32)
        (key_grad, value_grad), (block_outs, query_grads) = lax.scan(
            one_block, (empty, empty), jnp.arange(2, dtype=jnp.int32)
        )
        return (
            block_outs.reshape(seq_len, HEAD_DIM),
            query_grads.reshape(seq_len, HEAD_DIM),
            key_grad,
            value_grad,
        )

    results = lax.map(one_head, jnp.arange(heads_local, dtype=jnp.int32))
    return tuple((join_heads(item) for item in results))


def store_at(array, value, which, running):
    return array.at[which].set(jnp.where(running, value, array[which]))


def pipelined(
    inputs,
    cotangent,
    segment_ids,
    norm_gains,
    norm_biases,
    qkv_weight,
    qv_bias,
    out_weight,
    up_weight,
    up_bias,
    down_weight,
    out_biases,
):
    section_index = lax.axis_index("section")
    section_count = lax.axis_size("section")
    lane_index = lax.axis_index("tensor")
    micro_count, own_rows, model_width = inputs.shape
    seq_len = segment_ids.shape[1]
    cols_local = qkv_weight.shape[3]
    hidden_local = up_weight.shape[2]
    heads_local = cols_local // HEAD_DIM
    gain_rows = norm_gains[0]
    shift_rows = norm_biases[0]
    joined = jnp.concatenate([qkv_weight[0, 0], qkv_weight[0, 1], qkv_weight[0, 2]], axis=1)
    query_shift = lax.dynamic_slice_in_dim(qv_bias[0, 0], lane_index * cols_local, cols_local)
    value_shift = lax.dynamic_slice_in_dim(qv_bias[0, 1], lane_index * cols_local, cols_local)
    up_shift = lax.dynamic_slice_in_dim(up_bias[0], lane_index * hidden_local, hidden_local)
    out_matrix = out_weight[0]
    up_matrix = up_weight[0]
    down_matrix = down_weight[0]
    mixer_shift = out_biases[0, 0]
    feed_shift = out_biases[0, 1]

    def spread_rows(normed_rows, weight):
        return (
            None,
            jnp.dot(
                lax.all_gather(normed_rows, "tensor", axis=0, tiled=True),
                weight,
                preferred_element_type=jnp.float32,
            ),
        )

    def regather(normed_rows):
        return lax.all_gather(normed_rows, "tensor", axis=0, tiled=True)

    def gather_grads(grad_rows):
        return lax.all_gather(grad_rows.astype(jnp.bfloat16), "tensor", axis=0, tiled=True)

    def branch_sum(left_rows, weight):
        return lax.psum_scatter(
            jnp.dot(left_rows, weight, preferred_element_type=jnp.float32).astype(jnp.bfloat16),
            "tensor",
            scatter_dimension=0,
            tiled=True,
        ).astype(jnp.float32)

    def input_sum(grad_rows, weight):
        return lax.psum_scatter(
            jnp.einsum("sc,dc->sd", grad_rows, weight, preferred_element_type=jnp.float32).astype(
                jnp.bfloat16
            ),
            "tensor",
            scatter_dimension=0,
            tiled=True,
        ).astype(jnp.float32)

    def split_projected(projected):
        queries = (projected[:, :cols_local] + query_shift).astype(jnp.bfloat16)
        key_rows = projected[:, cols_local : 2 * cols_local].astype(jnp.bfloat16)
        value_rows = (projected[:, 2 * cols_local :] + value_shift).astype(jnp.bfloat16)
        return (queries, key_rows, value_rows)

    def layer_backward(block_in, middle, log_totals, segment, out_grad):
        residual = block_in.astype(jnp.float32)
        full_grad = gather_grads(out_grad)
        normed_two, scaled_two, inverse_two = norm_parts(middle, gain_rows[1], shift_rows[1])
        normed_two = normed_two.astype(jnp.bfloat16)
        full_two = regather(normed_two)
        hidden = jnp.dot(full_two, up_matrix, preferred_element_type=jnp.float32) + up_shift
        active, gelu_pullback = jax.vjp(gelu_exact, hidden)
        active = active.astype(jnp.bfloat16)
        down_grad = jnp.einsum("sf,sd->fd", active, full_grad, preferred_element_type=jnp.float32)
        active_grad = jnp.einsum(
            "sd,fd->sf", full_grad, down_matrix, preferred_element_type=jnp.float32
        )
        hidden_grad = gelu_pullback(active_grad)[0]
        up_shift_grad = jnp.sum(hidden_grad, axis=0)
        hidden_low = hidden_grad.astype(jnp.bfloat16)
        up_grad = jnp.einsum("sd,sf->df", full_two, hidden_low, preferred_element_type=jnp.float32)
        normed_grad_two = input_sum(hidden_low, up_matrix)
        feed_shift_grad = jnp.sum(out_grad, axis=0)
        middle_grad = out_grad + norm_back(normed_grad_two, scaled_two, inverse_two, gain_rows[1])
        gain_two = jnp.sum(normed_grad_two * scaled_two, axis=0)
        shift_two = jnp.sum(normed_grad_two, axis=0)
        full_mid_grad = gather_grads(middle_grad)
        normed_one, scaled_one, inverse_one = norm_parts(residual, gain_rows[0], shift_rows[0])
        normed_one = normed_one.astype(jnp.bfloat16)
        full_one = regather(normed_one)
        projected = jnp.dot(full_one, joined, preferred_element_type=jnp.float32)
        queries, key_rows, value_rows = split_projected(projected)
        mixed_grad = jnp.einsum(
            "sd,cd->sc", full_mid_grad, out_matrix, preferred_element_type=jnp.float32
        ).astype(jnp.bfloat16)
        mixed_rows, query_grad, key_grad, value_grad = attend_backward(
            queries, key_rows, value_rows, mixed_grad, log_totals, segment
        )
        out_grad_matrix = jnp.einsum(
            "sc,sd->cd", mixed_rows, full_mid_grad, preferred_element_type=jnp.float32
        )
        mixer_shift_grad = jnp.sum(middle_grad, axis=0)
        qkv_low = jnp.concatenate([query_grad, key_grad, value_grad], axis=1).astype(jnp.bfloat16)
        joined_grad = jnp.einsum("sd,sc->dc", full_one, qkv_low, preferred_element_type=jnp.float32)
        normed_grad_one = input_sum(qkv_low, joined)
        in_grad = middle_grad + norm_back(normed_grad_one, scaled_one, inverse_one, gain_rows[0])
        gain_one = jnp.sum(normed_grad_one * scaled_one, axis=0)
        shift_one = jnp.sum(normed_grad_one, axis=0)
        qv_local = jnp.stack([jnp.sum(query_grad, axis=0), jnp.sum(value_grad, axis=0)])
        qv_full = lax.dynamic_update_slice_in_dim(
            jnp.zeros((2, model_width), jnp.float32), qv_local, lane_index * cols_local, 1
        )
        up_full = lax.dynamic_update_slice_in_dim(
            jnp.zeros((up_bias.shape[1],), jnp.float32), up_shift_grad, lane_index * hidden_local, 0
        )
        weight_terms = (joined_grad, out_grad_matrix, up_grad, down_grad)
        small_terms = (
            jnp.stack([gain_one, gain_two]),
            jnp.stack([shift_one, shift_two]),
            qv_full,
            up_full,
            jnp.stack([mixer_shift_grad, feed_shift_grad]),
        )
        return (in_grad, weight_terms, small_terms)

    ticks = micro_count + section_count - 1
    received = jnp.zeros((own_rows, model_width), jnp.bfloat16)
    saved_in = jnp.zeros_like(inputs)
    saved_mid = jnp.zeros((micro_count, own_rows, model_width), jnp.float32)
    saved_totals = jnp.zeros((micro_count, heads_local, seq_len), jnp.float32)
    states = jnp.zeros_like(inputs)
    for tick in range(ticks):
        micro = tick - section_index
        running = (micro >= 0) & (micro < micro_count)
        which = jnp.clip(micro, 0, micro_count - 1)
        own_in = lax.dynamic_index_in_dim(inputs, which, 0, keepdims=False)
        block_in = jnp.where(section_index == 0, own_in, received)
        segment = lax.dynamic_index_in_dim(segment_ids, which, 0, keepdims=False)
        layer_residual = block_in.astype(jnp.float32)
        layer_normed_one = norm_parts(layer_residual, gain_rows[0], shift_rows[0])[0].astype(
            jnp.bfloat16
        )
        layer_full_one, layer_projected = spread_rows(layer_normed_one, joined)
        layer_queries, layer_key_rows, layer_value_rows = split_projected(layer_projected)
        layer_mixed_rows, layer_log_totals = attend_forward(
            layer_queries, layer_key_rows, layer_value_rows, segment
        )
        layer_middle = layer_residual + branch_sum(layer_mixed_rows, out_matrix) + mixer_shift
        layer_normed_two = norm_parts(layer_middle, gain_rows[1], shift_rows[1])[0].astype(
            jnp.bfloat16
        )
        layer_full_two, layer_hidden = spread_rows(layer_normed_two, up_matrix)
        layer_active = gelu_exact(layer_hidden + up_shift).astype(jnp.bfloat16)
        block_out = layer_middle + branch_sum(layer_active, down_matrix) + feed_shift
        block_out, middle, log_totals, full_one, full_two = (
            block_out,
            layer_middle,
            layer_log_totals,
            layer_full_one,
            layer_full_two,
        )
        handed = block_out.astype(jnp.bfloat16)
        saved_in = store_at(saved_in, block_in, which, running)
        saved_mid = store_at(saved_mid, middle, which, running)
        saved_totals = store_at(saved_totals, log_totals, which, running)
        states = store_at(states, handed, which, running)
        if tick + 1 < ticks:
            received = passed_along(handed, "section", 1)
    back_received = jnp.zeros((own_rows, model_width), jnp.bfloat16)
    weight_totals = (
        jnp.zeros(joined.shape, jnp.float32),
        jnp.zeros(out_matrix.shape, jnp.float32),
        jnp.zeros(up_matrix.shape, jnp.float32),
        jnp.zeros(down_matrix.shape, jnp.float32),
    )
    small_totals = (
        jnp.zeros((2, model_width), jnp.float32),
        jnp.zeros((2, model_width), jnp.float32),
        jnp.zeros((2, model_width), jnp.float32),
        jnp.zeros((up_bias.shape[1],), jnp.float32),
        jnp.zeros((2, model_width), jnp.float32),
    )
    grads_store = jnp.zeros((micro_count, own_rows, model_width), jnp.float32)
    for tick in range(ticks):
        micro = tick - (section_count - 1) + section_index
        running = (micro >= 0) & (micro < micro_count)
        which = jnp.clip(micro, 0, micro_count - 1)
        own_grad = lax.dynamic_index_in_dim(cotangent, which, 0, keepdims=False)
        out_grad = jnp.where(section_index == section_count - 1, own_grad, back_received).astype(
            jnp.float32
        )
        in_grad, weight_terms, small_terms = layer_backward(
            lax.dynamic_index_in_dim(saved_in, which, 0, keepdims=False),
            lax.dynamic_index_in_dim(saved_mid, which, 0, keepdims=False),
            lax.dynamic_index_in_dim(saved_totals, which, 0, keepdims=False),
            lax.dynamic_index_in_dim(segment_ids, which, 0, keepdims=False),
            out_grad,
        )
        joined_term, out_term, up_term, down_term = tuple(
            (jnp.where(running, term, 0.0) for term in weight_terms)
        )
        weight_terms = (joined_term, out_term, up_term, down_term)
        weight_totals = tuple((total + term for total, term in zip(weight_totals, weight_terms)))
        small_totals = tuple(
            (
                total + jnp.where(running, term, 0.0)
                for total, term in zip(small_totals, small_terms)
            )
        )
        grads_store = store_at(grads_store, in_grad, which, running)
        if tick + 1 < ticks:
            back_received = passed_along(in_grad.astype(jnp.bfloat16), "section", -1)
    joined_total, out_total, up_total, down_total = weight_totals
    summed = (
        lax.psum(joined_total.astype(jnp.bfloat16), "dp").astype(jnp.float32),
        lax.psum(out_total.astype(jnp.bfloat16), "dp").astype(jnp.float32),
        lax.psum(up_total.astype(jnp.bfloat16), "dp").astype(jnp.float32),
        lax.psum(down_total.astype(jnp.bfloat16), "dp").astype(jnp.float32),
    )
    gain_total, shift_total, qv_total, up_shift_total, out_shift_total = small_totals
    small_summed = lax.psum(
        (gain_total, shift_total, qv_total, up_shift_total, out_shift_total), ("dp", "tensor")
    )
    qkv_grad = summed[0].reshape(model_width, 3, cols_local).transpose(1, 0, 2)
    return (
        states[None],
        grads_store[None],
        small_summed[0][None],
        small_summed[1][None],
        qkv_grad[None],
        small_summed[2][None],
        summed[1][None],
        summed[2][None],
        small_summed[3][None],
        summed[3][None],
        small_summed[4][None],
    )


def solution(mesh):
    placed = (
        P("dp", "tensor", None),
        P("dp", "tensor", None),
        P("dp", None),
        P("section", None, None),
        P("section", None, None),
        P("section", None, None, "tensor"),
        P("section", None, None),
        P("section", "tensor", None),
        P("section", None, "tensor"),
        P("section", None),
        P("section", "tensor", None),
        P("section", None, None),
    )
    sizes = dict(mesh.shape)

    def on_device(inputs, *rest):
        each = inputs.shape[0] == sizes["section"] * sizes["tensor"]
        paired = sizes["section"] == 2 and sizes["tensor"] == 2 and sizes["dp"] % 2 == 0
        if each and paired and sizes["dp"] == 8:
            return one_sequence_each(inputs, *rest)
        return pipelined(inputs, *rest)

    return jax.shard_map(
        on_device,
        mesh=mesh,
        in_specs=placed,
        out_specs=(
            P("section", "dp", "tensor", None),
            P("section", "dp", "tensor", None),
            P("section", None, None),
            P("section", None, None),
            P("section", None, None, "tensor"),
            P("section", None, None),
            P("section", "tensor", None),
            P("section", None, "tensor"),
            P("section", None),
            P("section", "tensor", None),
            P("section", None, None),
        ),
        check_vma=False,
    )
```
